32 devices in a mesh: ctx: 8 (over z, y), head: 4 (over x, core).
Axes of the slice: x: 2, y: 2, z: 4, core: 2. Of those that a mesh axis runs over, the one named last changes fastest.
Arguments:
- queries: bfloat16 [8, 32, 128], P('ctx', 'head'), may hold values from -9 to 9
- k_new: bfloat16 [8, 16, 128], P('ctx', 'head'), may hold values from -9 to 9
- v_new: bfloat16 [8, 16, 128], P('ctx', 'head'), may hold values from -6 to 6
- k_suffix: bfloat16 [8, 256, 16, 128], P('ctx', None, 'head'), may hold values from -9 to 9
- v_suffix: bfloat16 [8, 256, 16, 128], P('ctx', None, 'head'), may hold values from -6 to 6
- lengths: int32 [8], P('ctx'), may hold values from 0 to 256, as said below
- k_prefix: bfloat16 [8192, 16, 128], P('ctx', 'head'), may hold values from -6 to 6
- v_prefix: bfloat16 [8192, 16, 128], P('ctx', 'head'), may hold values from -6 to 6
- w_out: bfloat16 [4096, 5376], P(None, ('ctx', 'head')), may hold values from -0.09375 to 0.09375
- residual: bfloat16 [8, 5376], P(None, ('ctx', 'head')), may hold values from -5 to 5
- norm_gain: float32 [5376], replicated, may hold values from 0.1 to 1.9
- w_gate: bfloat16 [5376, 21504], P(None, ('ctx', 'head')), may hold values from -0.078125 to 0.078125
- w_up: bfloat16 [5376, 21504], P(None, ('ctx', 'head')), may hold values from -0.078125 to 0.078125
- w_down: bfloat16 [21504, 5376], P(('ctx', 'head')), may hold values from -0.078125 to 0.078125
Outputs:
- attention: bfloat16 [8, 32, 128], P('ctx', 'head')
- next_hidden: bfloat16 [8, 5376], P(None, ('ctx', 'head'))
The draws below stay inside these ranges and needn't reach their ends.
Inputs may be any that keep to these rules, and one draw needn't show every extreme that they name: `lengths`: slots at or past a completion's length hold entries that no key uses.
All inputs are finite; a program needn't handle non-finite values.
Results may differ from the reference program's by a relative error of at most 0.008.
Values may be sent and summed in bfloat16 or wider, within the bound.
No kernel may reach another device: no remote copies, remote signals or barrier semaphores. Data moves between devices by JAX's collectives and lax.ppermute only.
A program may use at most 64 MiB of HBM per device.

```python
import jax
import jax.numpy as jnp
from jax import lax

D = 5376
FF = 21504
QH = 32
KVH = 16
HD = 128
SUF = 256
BLOCK = 512
BATCH = 8
PROMPT = 8192


def draw_queries(key, part):
    key = jax.random.fold_in(key, 3)
    noise_key = jax.random.fold_in(key, 0)
    values = 3.0 * jax.random.normal(noise_key, (BATCH, QH, HD), jnp.float32)
    values = jnp.clip(values, -9.0, 9.0)
    return values.astype(jnp.bfloat16)


def draw_k_prefix(key, part):
    key = jax.random.fold_in(key, 5)
    noise_key = jax.random.fold_in(key, 0)
    values = jax.random.normal(noise_key, (PROMPT, KVH, HD), jnp.float32)
    values = jnp.clip(values, -6.0, 6.0)
    return values.astype(jnp.bfloat16)


def draw_lengths(key, part):
    key = jax.random.fold_in(key, 7)
    base_key, long_key, offset_key = jax.random.split(key, 3)
    counts = jax.random.randint(base_key, (BATCH,), 0, SUF + 1)
    longest = jax.random.randint(long_key, (), 0, BATCH)
    shortest = (longest + 1 + jax.random.randint(offset_key, (), 0, BATCH - 1)) % BATCH
    places = jnp.arange(BATCH)
    counts = jnp.where(places == longest, SUF, counts)
    counts = jnp.where(places == shortest, 0, counts)
    return counts.astype(jnp.int32)


def spiked(values, key, source, target, shards_of, factor):
    owner, partner = [(jnp.arange(values.shape[axis_at]) // (values.shape[axis_at] // shards_of)).reshape([-1 if axis == axis_at else 1 for axis in range(values.ndim)]) for axis_at in (source, target)]
    chosen = jax.random.permutation(key, shards_of)[partner]
    strong = (owner == chosen) | (owner == (partner + shards_of // 2) % shards_of)
    return jnp.where(strong, factor * values, values)


def block_levels(stream_key, dims, shards, least, high):
    def one(dim, shards_of):
        steps = jax.random.uniform(jax.random.fold_in(jax.random.fold_in(stream_key, 6), dim), (shards_of,), jnp.float32, least / len(shards), high / len(shards))
        return jnp.repeat(jnp.exp(steps), dims[dim] // shards_of).reshape((-1,) + (1,) * (len(dims) - dim - 1))

    level = one(*shards[0])
    for cut in shards[1:]:
        level = level * one(*cut)
    return level


def gaussian(rng, extent, deviation, limit, shards=(), kind=jnp.bfloat16):
    drawn = deviation * jax.random.normal(rng, extent, jnp.float32)
    if shards:
        drawn = drawn * block_levels(rng, extent, shards, -0.22, 0.18)
    return jnp.clip(drawn, -limit, limit).astype(kind)


def gaussian_with(stream_key, dims, deviation, bound, cuts, heavy, kind=jnp.bfloat16):
    entries = deviation * jax.random.normal(stream_key, dims, jnp.float32)
    if cuts:
        entries = entries * block_levels(stream_key, dims, cuts, -0.22, 0.18)
    return jnp.clip(spiked(entries, jax.random.fold_in(stream_key, 3), *heavy), -bound, bound).astype(kind)


def setup_inputs(seed: int = 0) -> dict:
    streams_of = jax.random.split(jax.random.key(seed), 15)
    return {
        "queries": draw_queries(jax.random.fold_in(streams_of[14], 71), 0),
        "k_new": gaussian(streams_of[1], (BATCH, KVH, HD), 2.5, 9.0, ((0, 8), (1, 4))),
        "v_new": gaussian(streams_of[2], (BATCH, KVH, HD), 1.0, 6.0, ((0, 8), (1, 4))),
        "k_suffix": gaussian(streams_of[3], (BATCH, SUF, KVH, HD), 1.5, 9.0, ((0, 8), (2, 4))),
        "v_suffix": gaussian(streams_of[4], (BATCH, SUF, KVH, HD), 1.0, 6.0, ((0, 8), (2, 4))),
        "lengths": draw_lengths(jax.random.fold_in(streams_of[14], 71), 0),
        "k_prefix": draw_k_prefix(jax.random.fold_in(streams_of[14], 71), 0),
        "v_prefix": gaussian(streams_of[7], (PROMPT, KVH, HD), 1.0, 6.0, ((0, 8), (1, 4))),
        "w_out": gaussian(streams_of[8], (QH * HD, D), (QH * HD) ** -0.5, 0.09375, ((1, 32),)),
        "residual": gaussian(streams_of[9], (BATCH, D), 1.0, 5.0, ((1, 32),)),
        "norm_gain": jnp.clip(1.0 + 0.18 * jax.random.normal(streams_of[10], (D,), jnp.float32), 0.1, 1.9),
        "w_gate": gaussian(streams_of[11], (D, FF), D ** -0.5, 0.078125, ((1, 32),)),
        "w_up": gaussian(streams_of[12], (D, FF), D ** -0.5, 0.078125, ((1, 32),)),
        "w_down": gaussian_with(streams_of[13], (FF, D), FF ** -0.5, 0.078125, ((0, 32),), (0, 1, 32, 2.75)),
    }


score_scale = 168.0 ** (-0.5)
norm_epsilon = 1e-06

def join_parts(first, second):
    first_max, first_sum, first_total = first
    second_max, second_sum, second_total = second
    joint_max = jnp.maximum(first_max, second_max)
    first_factor = jnp.exp(first_max - joint_max)
    second_factor = jnp.exp(second_max - joint_max)
    joint_sum = first_sum * first_factor[..., None] + second_sum * second_factor[..., None]
    joint_total = first_total * first_factor + second_total * second_factor
    return (joint_max, joint_sum, joint_total)

def reference(queries, k_new, v_new, k_suffix, v_suffix, lengths, k_prefix, v_prefix, w_out, residual, norm_gain, w_gate, w_up, w_down):
    group_size = QH // KVH
    queries_all = queries.astype(jnp.float32).reshape(BATCH, KVH, group_size, HD)
    key_blocks = k_prefix.reshape(PROMPT // BLOCK, BLOCK, KVH, HD)
    value_blocks = v_prefix.reshape(PROMPT // BLOCK, BLOCK, KVH, HD)

    def block_step(running, block):
        key_block, value_block = block
        scores = jnp.einsum('bgrd,pgd->bgrp', queries_all, key_block.astype(jnp.float32)) * score_scale
        block_max = lax.optimization_barrier(jnp.max(scores, axis=-1))
        rounded = jnp.exp(scores - block_max[..., None]).astype(jnp.bfloat16)
        weights = lax.optimization_barrier(rounded).astype(jnp.float32)
        block_total = lax.optimization_barrier(jnp.sum(weights, axis=-1))
        block_sum = jnp.einsum('bgrp,pgd->bgrd', weights, value_block.astype(jnp.float32))
        return (join_parts(running, (block_max, block_sum, block_total)), None)
    start_max = jnp.full((BATCH, KVH, group_size), -jnp.inf, jnp.float32)
    start_sum = jnp.zeros((BATCH, KVH, group_size, HD), jnp.float32)
    start_total = jnp.zeros((BATCH, KVH, group_size), jnp.float32)
    prefix_part, unused = lax.scan(block_step, (start_max, start_sum, start_total), (key_blocks, value_blocks))

    def one_completion(items):
        query_rows, key_rows, value_rows, new_key, new_value, length = items
        scores = jnp.einsum('grd,sgd->grs', query_rows, key_rows.astype(jnp.float32)) * score_scale
        new_scores = jnp.einsum('grd,gd->gr', query_rows, new_key.astype(jnp.float32)) * score_scale
        in_use = (jnp.arange(SUF, dtype=jnp.int32) < length)[None, None, :]
        suffix_max = jnp.maximum(lax.optimization_barrier(jnp.max(jnp.where(in_use, scores, -jnp.inf), axis=-1)), new_scores)
        rounded = jnp.where(in_use, jnp.exp(scores - suffix_max[..., None]), 0.0).astype(jnp.bfloat16)
        weights = lax.optimization_barrier(rounded).astype(jnp.float32)
        new_rounded = jnp.exp(new_scores - suffix_max).astype(jnp.bfloat16)
        new_weight = lax.optimization_barrier(new_rounded).astype(jnp.float32)
        suffix_total = lax.optimization_barrier(jnp.sum(weights, axis=-1)) + new_weight
        suffix_sum = jnp.einsum('grs,sgd->grd', weights, value_rows.astype(jnp.float32))
        suffix_sum = suffix_sum + new_weight[..., None] * new_value.astype(jnp.float32)[:, None, :]
        return (suffix_max, suffix_sum, suffix_total)
    suffix_part = lax.map(one_completion, (queries_all, k_suffix, v_suffix, k_new, v_new, lengths))
    joined = join_parts(prefix_part, suffix_part)
    attention = (joined[1] / joined[2][..., None]).astype(jnp.bfloat16).reshape(BATCH, QH, HD)
    projected = jnp.dot(attention.reshape(BATCH, QH * HD), w_out, preferred_element_type=jnp.float32)
    hidden_state = (residual.astype(jnp.float32) + projected).astype(jnp.bfloat16)
    state_float = hidden_state.astype(jnp.float32)
    mean_square = lax.optimization_barrier(jnp.mean(state_float * state_float, axis=-1, keepdims=True))
    normed = (state_float * lax.rsqrt(mean_square + norm_epsilon) * norm_gain).astype(jnp.bfloat16)
    gate_values = jnp.dot(normed, w_gate, preferred_element_type=jnp.float32)
    up_values = jnp.dot(normed, w_up, preferred_element_type=jnp.float32)
    activated = (jax.nn.gelu(gate_values, approximate=True) * up_values).astype(jnp.bfloat16)
    next_hidden = (state_float + jnp.dot(activated, w_down, preferred_element_type=jnp.float32)).astype(jnp.bfloat16)
    return (attention, next_hidden)
```

```python
import functools

import jax
import jax.numpy as jnp
from jax import lax
from jax.experimental import pallas as pl
from jax.experimental.pallas import tpu as pltpu
from jax.sharding import PartitionSpec as P

SCORE_SCALE = 168.0 ** (-0.5)
NORM_EPSILON = 1e-06
MASKED = -1e30
BOTH = ("ctx", "head")


def pack_partial(row_max, row_total, row_sum):
    lane = lax.broadcasted_iota(jnp.int32, row_sum.shape, 1)
    return row_sum, jnp.where(lane == 0, row_max, row_total)


def masked_softmax(scores, keep):
    scores = jnp.where(keep, scores, MASKED)
    row_max = jnp.max(scores, axis=1, keepdims=True)
    weights = jnp.exp(scores - row_max).astype(jnp.bfloat16)
    row_total = jnp.sum(weights.astype(jnp.float32), axis=1, keepdims=True)
    return row_max, row_total, weights


def head_match(shape, heads, kv_heads):
    group = heads // kv_heads
    row = lax.broadcasted_iota(jnp.int32, shape, 0)
    column = lax.broadcasted_iota(jnp.int32, shape, 1)
    return lax.rem(row, heads) // group == lax.rem(column, kv_heads), column // kv_heads


def prefix_kernel(count, me_ref, *refs):
    arrived, (k_ref, v_ref, sum_ref, stat_ref, ordered_ref) = refs[:count], refs[count:]
    heads = arrived[0].shape[1]
    for step, ref in enumerate(arrived):
        owner = lax.rem(me_ref[0] + (count - step), count)
        ordered_ref[owner] = ref[0]
    positions, kv_heads, width = k_ref.shape
    keys = k_ref[...].reshape(positions * kv_heads, width)
    values = v_ref[...].reshape(positions * kv_heads, width)
    queries = ordered_ref[...].reshape(count * heads, width)
    scores = SCORE_SCALE * lax.dot_general(
        queries, keys, (((1,), (1,)), ((), ())), preferred_element_type=jnp.float32
    )
    match, unused = head_match(scores.shape, heads, kv_heads)
    row_max, row_total, weights = masked_softmax(scores, match)
    row_sum = jnp.dot(weights, values, preferred_element_type=jnp.float32)
    sum_ref[...], stat_ref[...] = pack_partial(row_max, row_total, row_sum)


def prefix_partials(me, arrived, k_prefix, v_prefix):
    count = len(arrived)
    unused, heads, width = arrived[0].shape
    shape = jax.ShapeDtypeStruct((count * heads, width), jnp.float32)
    whole = pl.BlockSpec(memory_space=pltpu.VMEM)
    return pl.pallas_call(
        functools.partial(prefix_kernel, count),
        out_shape=(shape, shape),
        in_specs=[pl.BlockSpec(memory_space=pltpu.SMEM)] + [whole] * (count + 2),
        scratch_shapes=[pltpu.VMEM((count, heads, width), jnp.bfloat16)],
        compiler_params=pltpu.CompilerParams(vmem_limit_bytes=24 * 1024 * 1024),
    )(me.astype(jnp.int32)[None], *arrived, k_prefix, v_prefix)


def suffix_kernel(length_ref, q_ref, k_ref, v_ref, k_new_ref, v_new_ref, sum_ref, stat_ref):
    unused, slots, kv_heads, width = k_ref.shape
    heads = q_ref.shape[1]
    keys = k_ref[0].reshape(slots * kv_heads, width)
    values = v_ref[0].reshape(slots * kv_heads, width)
    queries = q_ref[0]
    scores = SCORE_SCALE * lax.dot_general(
        queries, keys, (((1,), (1,)), ((), ())), preferred_element_type=jnp.float32
    )
    new_scores = SCORE_SCALE * lax.dot_general(
        queries, k_new_ref[0], (((1,), (1,)), ((), ())), preferred_element_type=jnp.float32
    )
    match, slot = head_match(scores.shape, heads, kv_heads)
    new_match, unused = head_match(new_scores.shape, heads, kv_heads)
    scores = jnp.where(match & (slot < length_ref[0]), scores, MASKED)
    new_scores = jnp.where(new_match, new_scores, MASKED)
    row_max = jnp.maximum(
        jnp.max(scores, axis=1, keepdims=True), jnp.max(new_scores, axis=1, keepdims=True)
    )
    weights = jnp.exp(scores - row_max).astype(jnp.bfloat16)
    new_weights = jnp.exp(new_scores - row_max).astype(jnp.bfloat16)
    row_total = jnp.sum(weights.astype(jnp.float32), axis=1, keepdims=True) + jnp.sum(
        new_weights.astype(jnp.float32), axis=1, keepdims=True
    )
    row_sum = jnp.dot(weights, values, preferred_element_type=jnp.float32) + jnp.dot(
        new_weights, v_new_ref[0], preferred_element_type=jnp.float32
    )
    sum_ref[...], stat_ref[...] = pack_partial(row_max, row_total, row_sum)


def suffix_partials(lengths, queries, k_suffix, v_suffix, k_new, v_new):
    shape = jax.ShapeDtypeStruct(queries.shape[1:], jnp.float32)
    whole = pl.BlockSpec(memory_space=pltpu.VMEM)
    return pl.pallas_call(
        suffix_kernel,
        out_shape=(shape, shape),
        in_specs=[pl.BlockSpec(memory_space=pltpu.SMEM)] + [whole] * 5,
        compiler_params=pltpu.CompilerParams(vmem_limit_bytes=8 * 1024 * 1024),
    )(lengths, queries, k_suffix, v_suffix, k_new, v_new)


def join_kernel(part_ref, sum_ref, stat_ref, out_ref):
    sources = part_ref.shape[1]
    suffix_max = stat_ref[:, 0:1]
    suffix_total = stat_ref[:, 1:2]
    joint_max = suffix_max
    for source in range(sources):
        joint_max = jnp.maximum(joint_max, part_ref[1, source, :, 0:1])
    factor = jnp.exp(suffix_max - joint_max)
    total = suffix_total * factor
    summed = sum_ref[...] * factor
    for source in range(sources):
        factor = jnp.exp(part_ref[1, source, :, 0:1] - joint_max)
        total = total + part_ref[1, source, :, 1:2] * factor
        summed = summed + part_ref[0, source] * factor
    out_ref[...] = (summed / total).astype(jnp.bfloat16)


def join_partials(parts, suffix_sum, suffix_stat):
    return pl.pallas_call(
        join_kernel,
        out_shape=jax.ShapeDtypeStruct(suffix_sum.shape, jnp.bfloat16),
        compiler_params=pltpu.CompilerParams(vmem_limit_bytes=8 * 1024 * 1024),
    )(parts, suffix_sum, suffix_stat)


def rotate(value, axis, count, steps):
    if steps == 0:
        return value
    return lax.ppermute(value, axis, [(i, (i + steps) % count) for i in range(count)])


def gather_every(value, devices):
    copies = jnp.broadcast_to(value[None], (devices, *value.shape))
    return lax.all_to_all(copies, BOTH, split_axis=0, concat_axis=0, tiled=True)


def body(
    queries,
    k_new,
    v_new,
    k_suffix,
    v_suffix,
    lengths,
    k_prefix,
    v_prefix,
    w_out,
    residual,
    norm_gain,
    w_gate,
    w_up,
    w_down,
):
    ctx_count = lax.axis_size("ctx")
    head_count = lax.axis_size("head")
    devices = ctx_count * head_count
    unused, heads, width = queries.shape
    columns = residual.shape[1]
    completions = residual.shape[0]

    arrived = [rotate(queries, "ctx", ctx_count, step) for step in range(ctx_count)]
    suffix_sum, suffix_stat = suffix_partials(lengths, queries, k_suffix, v_suffix, k_new, v_new)
    prefix_sum, prefix_stat = prefix_partials(lax.axis_index("ctx"), arrived, k_prefix, v_prefix)
    parts = jnp.stack([prefix_sum, prefix_stat], axis=0).reshape(2, ctx_count, heads, width)
    parts = lax.all_to_all(parts, "ctx", split_axis=1, concat_axis=1, tiled=True)
    attention = join_partials(parts, suffix_sum, suffix_stat)

    rows = gather_every(attention, devices).reshape(completions, devices * heads * width // completions)
    projected = jnp.dot(rows, w_out, preferred_element_type=jnp.float32)
    hidden_part = (residual.astype(jnp.float32) + projected).astype(jnp.bfloat16)

    hidden_state = gather_every(hidden_part, devices)
    hidden_state = jnp.swapaxes(hidden_state, 0, 1).reshape(completions, devices * columns)
    state_float = hidden_state.astype(jnp.float32)
    mean_square = jnp.mean(state_float * state_float, axis=-1, keepdims=True)
    normed = (state_float * lax.rsqrt(mean_square + NORM_EPSILON) * norm_gain).astype(jnp.bfloat16)
    gate_values = jnp.dot(normed, w_gate, preferred_element_type=jnp.float32)
    up_values = jnp.dot(normed, w_up, preferred_element_type=jnp.float32)
    activated = (jax.nn.gelu(gate_values, approximate=True) * up_values).astype(jnp.bfloat16)
    share = jnp.dot(activated, w_down, preferred_element_type=jnp.float32).astype(jnp.bfloat16)
    share = jnp.swapaxes(share.reshape(completions, devices, columns), 0, 1)
    shares = lax.all_to_all(share, BOTH, split_axis=0, concat_axis=0, tiled=True)
    summed = jnp.sum(shares.astype(jnp.float32), axis=0)
    next_hidden = (hidden_part.astype(jnp.float32) + summed).astype(jnp.bfloat16)
    return (attention[None], next_hidden)


def solution(mesh):
    placed = (
        P("ctx", "head", None),
        P("ctx", "head", None),
        P("ctx", "head", None),
        P("ctx", None, "head", None),
        P("ctx", None, "head", None),
        P("ctx"),
        P("ctx", "head", None),
        P("ctx", "head", None),
        P(None, BOTH),
        P(None, BOTH),
        P(),
        P(None, BOTH),
        P(None, BOTH),
        P(BOTH, None),
    )
    return jax.shard_map(
        body,
        mesh=mesh,
        in_specs=placed,
        out_specs=(P("ctx", "head", None), P(None, BOTH)),
        check_vma=False,
    )
```

```python
import functools

import jax
import jax.numpy as jnp
from jax import lax
from jax.experimental import pallas as pl
from jax.experimental.pallas import tpu as pltpu
from jax.sharding import PartitionSpec as P

SCORE_SCALE = 168.0 ** (-0.5)
NORM_EPSILON = 1e-06
MASKED = -1e30
MIB = 1024 * 1024
GRANT = 60 * MIB
LOADS = 4
FORWARD_LOADS = 6
BOTH = ("ctx", "head")


def head_match(shape, heads, kv_heads):
    group = heads // kv_heads
    row = lax.broadcasted_iota(jnp.int32, shape, 0)
    column = lax.broadcasted_iota(jnp.int32, shape, 1)
    return lax.rem(row, heads) // group == lax.rem(column, kv_heads), column // kv_heads


def dot_rows(left, right):
    return lax.dot_general(left, right, (((1,), (1,)), ((), ())), preferred_element_type=jnp.float32)


def stat_rows(row_max, row_total, shape):
    lane = lax.broadcasted_iota(jnp.int32, shape, 1)
    return jnp.where(lane == 0, row_max, row_total)


def row_chunks(rows, most):
    for count in range(most, 1, -1):
        if rows % (16 * count) == 0:
            return count
    return 1


def start_chunks(source, target, sems, first, most):
    count = row_chunks(source.shape[0], most)
    size = source.shape[0] // count
    copies = []
    for chunk in range(count):
        rows = pl.ds(chunk * size, size)
        copies.append(pltpu.make_async_copy(source.at[rows], target.at[rows], sems.at[first + chunk]))
    for copy in copies:
        copy.start()
    return copies


def suffix_kernel(
    length_ref, q_hbm, kn_hbm, vn_hbm, ks_hbm, vs_hbm, part_ref, q_ref, kn_ref, vn_ref, ks_ref, vs_ref, sems
):
    copies = [
        pltpu.make_async_copy(source, target, sems.at[place])
        for place, (source, target) in enumerate(
            ((q_hbm, q_ref), (kn_hbm, kn_ref), (ks_hbm, ks_ref), (vn_hbm, vn_ref), (vs_hbm, vs_ref))
        )
    ]
    for copy in copies:
        copy.start()
    unused, slots, kv_heads, width = ks_ref.shape
    heads = q_ref.shape[1]
    for copy in copies[:3]:
        copy.wait()
    queries = q_ref[0]
    scores = SCORE_SCALE * dot_rows(queries, ks_ref[0].reshape(slots * kv_heads, width))
    new_scores = SCORE_SCALE * dot_rows(queries, kn_ref[0])
    match, slot = head_match(scores.shape, heads, kv_heads)
    new_match, unused = head_match(new_scores.shape, heads, kv_heads)
    scores = jnp.where(match & (slot < length_ref[0]), scores, MASKED)
    new_scores = jnp.where(new_match, new_scores, MASKED)
    row_max = jnp.maximum(
        jnp.max(scores, axis=1, keepdims=True), jnp.max(new_scores, axis=1, keepdims=True)
    )
    weights = jnp.exp(scores - row_max).astype(jnp.bfloat16)
    new_weights = jnp.exp(new_scores - row_max).astype(jnp.bfloat16)
    row_total = jnp.sum(weights.astype(jnp.float32), axis=1, keepdims=True) + jnp.sum(
        new_weights.astype(jnp.float32), axis=1, keepdims=True
    )
    for copy in copies[3:]:
        copy.wait()
    row_sum = jnp.dot(
        weights, vs_ref[0].reshape(slots * kv_heads, width), preferred_element_type=jnp.float32
    ) + jnp.dot(new_weights, vn_ref[0], preferred_element_type=jnp.float32)
    part_ref[0] = row_sum
    part_ref[1] = stat_rows(row_max, row_total, row_sum.shape)


def suffix_partials(lengths, *operands):
    return pl.pallas_call(
        suffix_kernel,
        out_shape=jax.ShapeDtypeStruct((2, *operands[0].shape[1:]), jnp.float32),
        in_specs=[pl.BlockSpec(memory_space=pltpu.SMEM)] + [pl.BlockSpec(memory_space=pl.ANY)] * 5,
        scratch_shapes=[pltpu.VMEM(operand.shape, operand.dtype) for operand in operands]
        + [pltpu.SemaphoreType.DMA((5,))],
        compiler_params=pltpu.CompilerParams(vmem_limit_bytes=GRANT),
        cost_estimate=pl.CostEstimate(flops=10**7, bytes_accessed=2 * MIB, transcendentals=10**4),
    )(lengths, *operands)


def prefix_kernel(me_ref, *refs):
    arrived, (k_hbm, v_hbm, part_ref, ordered_ref, k_ref, v_ref, sems) = refs[:-7], refs[-7:]
    key_copies = start_chunks(k_hbm, k_ref, sems, 0, LOADS)
    value_copies = start_chunks(v_hbm, v_ref, sems, LOADS, LOADS)
    place = 0
    for ref in arrived:
        for source in range(ref.shape[0]):
            ordered_ref[lax.bitwise_xor(me_ref[0], place)] = ref[source]
            place += 1
    count, heads, width = ordered_ref.shape
    positions, kv_heads, unused = k_ref.shape
    size = positions // len(key_copies)
    queries = ordered_ref[...].reshape(count * heads, width)
    chunks = []
    for chunk, copy in enumerate(key_copies):
        copy.wait()
        keys = k_ref[chunk * size : (chunk + 1) * size].reshape(size * kv_heads, width)
        scores = SCORE_SCALE * dot_rows(queries, keys)
        match, unused = head_match(scores.shape, heads, kv_heads)
        chunks.append(jnp.where(match, scores, MASKED))
    row_max = functools.reduce(
        jnp.maximum, [jnp.max(scores, axis=1, keepdims=True) for scores in chunks]
    )
    row_total = jnp.zeros_like(row_max)
    row_sum = jnp.zeros((count * heads, width), jnp.float32)
    for chunk, copy in enumerate(value_copies):
        weights = jnp.exp(chunks[chunk] - row_max).astype(jnp.bfloat16)
        row_total += jnp.sum(weights.astype(jnp.float32), axis=1, keepdims=True)
        copy.wait()
        values = v_ref[chunk * size : (chunk + 1) * size].reshape(size * kv_heads, width)
        row_sum += jnp.dot(weights, values, preferred_element_type=jnp.float32)
    stats = stat_rows(row_max, row_total, row_sum.shape)
    part_ref[:, 0] = row_sum.reshape(count, heads, width)
    part_ref[:, 1] = stats.reshape(count, heads, width)


def prefix_partials(me, arrived, k_prefix, v_prefix):
    whole = pl.BlockSpec(memory_space=pltpu.VMEM)
    unused, heads, width = arrived[0].shape
    count = sum(piece.shape[0] for piece in arrived)
    return pl.pallas_call(
        prefix_kernel,
        out_shape=jax.ShapeDtypeStruct((count, 2, heads, width), jnp.float32),
        in_specs=[pl.BlockSpec(memory_space=pltpu.SMEM)]
        + [whole] * len(arrived)
        + [pl.BlockSpec(memory_space=pl.ANY)] * 2,
        scratch_shapes=[
            pltpu.VMEM((count, heads, width), jnp.bfloat16),
            pltpu.VMEM(k_prefix.shape, k_prefix.dtype),
            pltpu.VMEM(v_prefix.shape, v_prefix.dtype),
            pltpu.SemaphoreType.DMA((2 * LOADS,)),
        ],
        compiler_params=pltpu.CompilerParams(vmem_limit_bytes=GRANT),
    )(me.astype(jnp.int32)[None], *arrived, k_prefix, v_prefix)


def join_kernel(part_ref, suffix_ref, out_ref, copies_ref):
    sources = part_ref.shape[0]
    suffix_max = suffix_ref[1, :, 0:1]
    joint_max = suffix_max
    for source in range(sources):
        joint_max = jnp.maximum(joint_max, part_ref[source, 1, :, 0:1])
    factor = jnp.exp(suffix_max - joint_max)
    total = suffix_ref[1, :, 1:2] * factor
    summed = suffix_ref[0] * factor
    for source in range(sources):
        factor = jnp.exp(part_ref[source, 1, :, 0:1] - joint_max)
        total = total + part_ref[source, 1, :, 1:2] * factor
        summed = summed + part_ref[source, 0] * factor
    attention = (summed / total).astype(jnp.bfloat16)
    out_ref[...] = attention
    for place in range(copies_ref.shape[0]):
        copies_ref[place] = attention


def join_partials(parts, suffix_part, devices):
    shape = suffix_part.shape[1:]
    return pl.pallas_call(
        join_kernel,
        out_shape=(
            jax.ShapeDtypeStruct(shape, jnp.bfloat16),
            jax.ShapeDtypeStruct((devices, *shape), jnp.bfloat16),
        ),
        compiler_params=pltpu.CompilerParams(vmem_limit_bytes=8 * MIB),
    )(parts, suffix_part)


def project_kernel(rows_ref, w_ref, residual_ref, out_ref, copies_ref):
    projected = dot_rows(rows_ref[...], w_ref[...])
    hidden = (residual_ref[...].astype(jnp.float32) + projected).astype(jnp.bfloat16)
    out_ref[...] = hidden
    for place in range(copies_ref.shape[0]):
        copies_ref[place] = hidden


def project(rows, w_out, residual, devices):
    return pl.pallas_call(
        project_kernel,
        out_shape=(
            jax.ShapeDtypeStruct(residual.shape, jnp.bfloat16),
            jax.ShapeDtypeStruct((devices, *residual.shape), jnp.bfloat16),
        ),
        compiler_params=pltpu.CompilerParams(vmem_limit_bytes=12 * MIB),
    )(rows, w_out, residual)


def forward_kernel(
    state_ref, gain_ref, gate_hbm, up_hbm, down_hbm, out_ref, gate_ref, up_ref, down_ref, sems
):
    units = gate_ref.shape[0]
    count = row_chunks(units, FORWARD_LOADS)
    size = units // count
    copies = []
    for chunk in range(count):
        rows = pl.ds(chunk * size, size)
        for place, (source, target) in enumerate(
            ((gate_hbm, gate_ref), (up_hbm, up_ref), (down_hbm, down_ref))
        ):
            copies.append(
                pltpu.make_async_copy(source.at[rows], target.at[rows], sems.at[3 * chunk + place])
            )
            copies[-1].start()
    state = state_ref[...].astype(jnp.float32)
    mean_square = jnp.mean(state * state, axis=-1, keepdims=True)
    normed = (state * lax.rsqrt(mean_square + NORM_EPSILON) * gain_ref[...]).astype(jnp.bfloat16)
    total = jnp.zeros(out_ref.shape, jnp.float32)
    for chunk in range(count):
        rows = slice(chunk * size, (chunk + 1) * size)
        copies[3 * chunk].wait()
        gate_values = dot_rows(normed, gate_ref[rows])
        copies[3 * chunk + 1].wait()
        up_values = dot_rows(normed, up_ref[rows])
        activated = (jax.nn.gelu(gate_values, approximate=True) * up_values).astype(jnp.bfloat16)
        copies[3 * chunk + 2].wait()
        total += jnp.dot(activated, down_ref[rows], preferred_element_type=jnp.float32)
    out_ref[...] = total.astype(jnp.bfloat16)


def forward(state, gain, w_gate, w_up, w_down):
    whole = pl.BlockSpec(memory_space=pltpu.VMEM)
    return pl.pallas_call(
        forward_kernel,
        out_shape=jax.ShapeDtypeStruct(state.shape, jnp.bfloat16),
        in_specs=[whole, whole] + [pl.BlockSpec(memory_space=pl.ANY)] * 3,
        scratch_shapes=[pltpu.VMEM(w.shape, w.dtype) for w in (w_gate, w_up, w_down)]
        + [pltpu.SemaphoreType.DMA((3 * FORWARD_LOADS,))],
        compiler_params=pltpu.CompilerParams(vmem_limit_bytes=56 * MIB),
    )(state, gain, w_gate, w_up, w_down)


def gather_by_xor(value, axis):
    count = lax.axis_size(axis)
    pieces = [value]
    step = 1
    while step < count:
        partners = [(i, i ^ step) for i in range(count)]
        pieces.append(lax.ppermute(jnp.concatenate(pieces, axis=0), axis, partners))
        step *= 2
    return pieces


def exchange(copies):
    return lax.all_to_all(copies, BOTH, split_axis=0, concat_axis=0, tiled=True)


def body(
    queries,
    k_new,
    v_new,
    k_suffix,
    v_suffix,
    lengths,
    k_prefix,
    v_prefix,
    w_out,
    residual,
    norm_gain,
    w_gate,
    w_up,
    w_down,
):
    devices = lax.axis_size("ctx") * lax.axis_size("head")
    completions, columns = residual.shape

    arrived = gather_by_xor(queries, "ctx")
    suffix_part = suffix_partials(lengths, queries, k_new, v_new, k_suffix, v_suffix)
    parts = prefix_partials(lax.axis_index("ctx"), arrived, k_prefix, v_prefix)
    parts = lax.all_to_all(parts, "ctx", split_axis=0, concat_axis=0, tiled=True)
    attention, copies = join_partials(parts, suffix_part, devices)

    rows = exchange(copies).reshape(completions, w_out.shape[0])
    hidden_part, copies = project(rows, w_out.T, residual, devices)

    hidden_state = jnp.swapaxes(exchange(copies), 0, 1).reshape(completions, devices * columns)
    share = forward(hidden_state, norm_gain[None], w_gate.T, w_up.T, w_down)
    share = jnp.swapaxes(share.reshape(completions, devices, columns), 0, 1)
    summed = jnp.sum(exchange(share).astype(jnp.float32), axis=0)
    next_hidden = (hidden_part.astype(jnp.float32) + summed).astype(jnp.bfloat16)
    return (attention[None], next_hidden)


def solution(mesh):
    placed = (
        P("ctx", "head", None),
        P("ctx", "head", None),
        P("ctx", "head", None),
        P("ctx", None, "head", None),
        P("ctx", None, "head", None),
        P("ctx"),
        P("ctx", "head", None),
        P("ctx", "head", None),
        P(None, BOTH),
        P(None, BOTH),
        P(),
        P(None, BOTH),
        P(None, BOTH),
        P(BOTH, None),
    )
    return jax.shard_map(
        body,
        mesh=mesh,
        in_specs=placed,
        out_specs=(P("ctx", "head", None), P(None, BOTH)),
        check_vma=False,
    )
```

```python
import functools

import jax
import jax.numpy as jnp
from jax import lax
from jax.experimental import pallas as pl
from jax.experimental.pallas import tpu as pltpu
from jax.sharding import PartitionSpec as P

SCORE_SCALE = 168.0 ** (-0.5)
NORM_EPSILON = 1e-06
MASKED = -1e30
MIB = 1024 * 1024
LOADS = 6
COST = pl.CostEstimate(flops=10**9, bytes_accessed=32 * MIB, transcendentals=10**6)
BOTH = ("ctx", "head")


def head_bias(rows, columns, heads, kv_heads):
    group = heads // kv_heads
    tile = (heads, 128)
    row = lax.broadcasted_iota(jnp.int32, tile, 0)
    column = lax.broadcasted_iota(jnp.int32, tile, 1)
    bias = jnp.where(row // group == lax.rem(column, kv_heads), 0.0, MASKED)
    return jnp.tile(bias, (rows // heads, columns // 128))


def dot_rows(left, right):
    return lax.dot_general(left, right, (((1,), (1,)), ((), ())), preferred_element_type=jnp.float32)


def stat_rows(row_max, row_total, shape):
    lane = lax.broadcasted_iota(jnp.int32, shape, 1)
    return jnp.where(lane == 0, row_max, row_total)


def attention_kernel(
    length_ref, arrived_ref, q_hbm, kn_hbm, vn_hbm, ks_hbm, vs_hbm, kp_hbm, vp_hbm,
    part_ref,
    q_ref, kn_ref, vn_ref, ks_ref, vs_ref, kp_ref, vp_ref, sems,
):
    pairs = (
        (kp_hbm, kp_ref), (q_hbm, q_ref), (ks_hbm, ks_ref), (kn_hbm, kn_ref),
        (vs_hbm, vs_ref), (vn_hbm, vn_ref), (vp_hbm, vp_ref),
    )
    copies = [
        pltpu.make_async_copy(source, target, sems.at[place])
        for place, (source, target) in enumerate(pairs)
    ]
    for copy in copies:
        copy.start()
    count, heads, width = arrived_ref.shape
    kv_heads = kn_ref.shape[1]
    queries = arrived_ref[...].reshape(count * heads, width)
    copies[0].wait()
    scores = SCORE_SCALE * dot_rows(queries, kp_ref[...])
    scores = scores + head_bias(*scores.shape, heads, kv_heads)
    row_max = jnp.max(scores, axis=1, keepdims=True)
    weights = jnp.exp(scores - row_max).astype(jnp.bfloat16)
    row_total = jnp.sum(weights.astype(jnp.float32), axis=1, keepdims=True)
    for copy in copies[1:6]:
        copy.wait()
    own = q_ref[0]
    own_scores = SCORE_SCALE * dot_rows(own, ks_ref[...])
    new_scores = SCORE_SCALE * dot_rows(own, kn_ref[0])
    slot = lax.broadcasted_iota(jnp.int32, own_scores.shape, 1) // kv_heads
    own_scores = own_scores + head_bias(*own_scores.shape, heads, kv_heads)
    own_scores = jnp.where(slot < length_ref[0], own_scores, MASKED)
    new_scores = new_scores + head_bias(heads, 128, heads, kv_heads)[:, :kv_heads]
    suffix_max = jnp.maximum(
        jnp.max(own_scores, axis=1, keepdims=True), jnp.max(new_scores, axis=1, keepdims=True)
    )
    own_weights = jnp.exp(own_scores - suffix_max).astype(jnp.bfloat16)
    new_weights = jnp.exp(new_scores - suffix_max).astype(jnp.bfloat16)
    suffix_total = jnp.sum(own_weights.astype(jnp.float32), axis=1, keepdims=True) + jnp.sum(
        new_weights.astype(jnp.float32), axis=1, keepdims=True
    )
    suffix_sum = jnp.dot(own_weights, vs_ref[...], preferred_element_type=jnp.float32) + jnp.dot(
        new_weights, vn_ref[0], preferred_element_type=jnp.float32
    )
    copies[6].wait()
    row_sum = jnp.dot(weights, vp_ref[...], preferred_element_type=jnp.float32)
    part_ref[:, 0] = row_sum.reshape(count, heads, width)
    part_ref[:, 1] = stat_rows(row_max, row_total, row_sum.shape).reshape(count, heads, width)
    me = lax.axis_index("ctx")
    prefix_stat = part_ref[me, 1]
    prefix_max = prefix_stat[:, 0:1]
    joint_max = jnp.maximum(prefix_max, suffix_max)
    prefix_factor = jnp.exp(prefix_max - joint_max)
    suffix_factor = jnp.exp(suffix_max - joint_max)
    joint_total = prefix_stat[:, 1:2] * prefix_factor + suffix_total * suffix_factor
    joint_sum = part_ref[me, 0] * prefix_factor + suffix_sum * suffix_factor
    part_ref[me, 0] = joint_sum
    part_ref[me, 1] = stat_rows(joint_max, joint_total, joint_sum.shape)


def attend(lengths, arrived, *operands):
    count, heads, width = arrived.shape
    return pl.pallas_call(
        attention_kernel,
        out_shape=jax.ShapeDtypeStruct((count, 2, heads, width), jnp.float32),
        in_specs=[pl.BlockSpec(memory_space=pltpu.SMEM), pl.BlockSpec(memory_space=pltpu.VMEM)]
        + [pl.BlockSpec(memory_space=pl.ANY)] * len(operands),
        scratch_shapes=[pltpu.VMEM(operand.shape, operand.dtype) for operand in operands]
        + [pltpu.SemaphoreType.DMA((len(operands),))],
        compiler_params=pltpu.CompilerParams(vmem_limit_bytes=60 * MIB),
        cost_estimate=COST,
    )(lengths, arrived, *operands)


def join_kernel(part_ref, out_ref, copies_ref):
    sources = part_ref.shape[0]
    joint_max = functools.reduce(
        jnp.maximum, [part_ref[source, 1, :, 0:1] for source in range(sources)]
    )
    total = jnp.zeros_like(joint_max)
    summed = jnp.zeros(out_ref.shape, jnp.float32)
    for source in range(sources):
        factor = jnp.exp(part_ref[source, 1, :, 0:1] - joint_max)
        total = total + part_ref[source, 1, :, 1:2] * factor
        summed = summed + part_ref[source, 0] * factor
    attention = (summed / total).astype(jnp.bfloat16)
    out_ref[...] = attention
    for place in range(copies_ref.shape[0]):
        copies_ref[place] = attention


def join_partials(parts, devices):
    shape = parts.shape[2:]
    return pl.pallas_call(
        join_kernel,
        out_shape=(
            jax.ShapeDtypeStruct(shape, jnp.bfloat16),
            jax.ShapeDtypeStruct((devices, *shape), jnp.bfloat16),
        ),
        compiler_params=pltpu.CompilerParams(vmem_limit_bytes=8 * MIB),
        cost_estimate=COST,
    )(parts)


def project_kernel(rows_ref, w_ref, residual_ref, out_ref, copies_ref, wide_ref):
    devices, heads, width = rows_ref.shape
    completions = residual_ref.shape[0]
    all_heads = devices * heads // completions
    wide_ref[...] = rows_ref[...].reshape(devices * heads, width).astype(jnp.float32)
    rows = [wide_ref[pl.ds(head, completions, stride=all_heads), :] for head in range(all_heads)]
    rows = jnp.concatenate([row.astype(jnp.bfloat16) for row in rows], axis=1)
    hidden = (residual_ref[...].astype(jnp.float32) + dot_rows(rows, w_ref[...])).astype(jnp.bfloat16)
    out_ref[...] = hidden
    for place in range(copies_ref.shape[0]):
        copies_ref[place] = hidden


def project(rows, w_out, residual):
    devices, heads, width = rows.shape
    return pl.pallas_call(
        project_kernel,
        out_shape=(
            jax.ShapeDtypeStruct(residual.shape, jnp.bfloat16),
            jax.ShapeDtypeStruct((devices, *residual.shape), jnp.bfloat16),
        ),
        scratch_shapes=[pltpu.VMEM((devices * heads, width), jnp.float32)],
        compiler_params=pltpu.CompilerParams(vmem_limit_bytes=12 * MIB),
        cost_estimate=COST,
    )(rows, w_out, residual)


def row_chunks(rows, most):
    for count in range(most, 1, -1):
        if rows % (16 * count) == 0:
            return count
    return 1


def forward_kernel(
    pieces_ref, gain_ref, gate_hbm, up_hbm, down_hbm, out_ref, state_ref, gate_ref, up_ref, down_ref, sems
):
    units = gate_ref.shape[0]
    count = row_chunks(units, LOADS)
    size = units // count
    copies = []
    for chunk in range(count):
        rows = pl.ds(chunk * size, size)
        for place, (source, target) in enumerate(
            ((gate_hbm, gate_ref), (up_hbm, up_ref), (down_hbm, down_ref))
        ):
            copies.append(
                pltpu.make_async_copy(source.at[rows], target.at[rows], sems.at[3 * chunk + place])
            )
            copies[-1].start()
    devices, completions, columns = pieces_ref.shape
    for place in range(devices):
        state_ref[:, place * columns : (place + 1) * columns] = pieces_ref[place].astype(jnp.float32)
    state = state_ref[...]
    mean_square = jnp.mean(state * state, axis=-1, keepdims=True)
    gain = gain_ref[...].reshape(1, devices * columns)
    normed = (state * lax.rsqrt(mean_square + NORM_EPSILON) * gain).astype(jnp.bfloat16)
    share = jnp.zeros(state.shape, jnp.float32)
    for chunk in range(count):
        rows = slice(chunk * size, (chunk + 1) * size)
        copies[3 * chunk].wait()
        gate_values = dot_rows(gate_ref[rows], normed)
        copies[3 * chunk + 1].wait()
        up_values = dot_rows(up_ref[rows], normed)
        activated = jax.nn.gelu(gate_values, approximate=True) * up_values
        copies[3 * chunk + 2].wait()
        share += jnp.dot(
            activated.T.astype(jnp.bfloat16), down_ref[rows], preferred_element_type=jnp.float32
        )
    for place in range(devices):
        out_ref[place] = share[:, place * columns : (place + 1) * columns].astype(jnp.bfloat16)


def forward(pieces, gain, *weights):
    devices, completions, columns = pieces.shape
    whole = pl.BlockSpec(memory_space=pltpu.VMEM)
    return pl.pallas_call(
        forward_kernel,
        out_shape=jax.ShapeDtypeStruct(pieces.shape, jnp.bfloat16),
        in_specs=[whole, whole] + [pl.BlockSpec(memory_space=pl.ANY)] * 3,
        scratch_shapes=[pltpu.VMEM((completions, devices * columns), jnp.float32)]
        + [pltpu.VMEM(w.shape, w.dtype) for w in weights]
        + [pltpu.SemaphoreType.DMA((3 * LOADS,))],
        compiler_params=pltpu.CompilerParams(vmem_limit_bytes=56 * MIB),
        cost_estimate=COST,
    )(pieces, gain, *weights)


def exchange(copies, axes=BOTH):
    return lax.all_to_all(copies, axes, split_axis=0, concat_axis=0, tiled=True)


def body(
    queries,
    k_new,
    v_new,
    k_suffix,
    v_suffix,
    lengths,
    k_prefix,
    v_prefix,
    w_out,
    residual,
    norm_gain,
    w_gate,
    w_up,
    w_down,
):
    ctx_count = lax.axis_size("ctx")
    devices = ctx_count * lax.axis_size("head")
    arrived = exchange(jnp.broadcast_to(queries, (ctx_count, *queries.shape[1:])), "ctx")
    rows_of = lambda values: values.reshape(-1, values.shape[-1])
    parts = attend(
        lengths, arrived, queries, k_new, v_new, *map(rows_of, (k_suffix, v_suffix, k_prefix, v_prefix))
    )
    attention, copies = join_partials(exchange(parts, "ctx"), devices)
    hidden_part, copies = project(exchange(copies), w_out.T, residual)
    shares = forward(exchange(copies), norm_gain, w_gate.T, w_up.T, w_down)
    summed = jnp.sum(exchange(shares).astype(jnp.float32), axis=0)
    next_hidden = (hidden_part.astype(jnp.float32) + summed).astype(jnp.bfloat16)
    return (attention[None], next_hidden)


def solution(mesh):
    placed = (
        P("ctx", "head", None),
        P("ctx", "head", None),
        P("ctx", "head", None),
        P("ctx", None, "head", None),
        P("ctx", None, "head", None),
        P("ctx"),
        P("ctx", "head", None),
        P("ctx", "head", None),
        P(None, BOTH),
        P(None, BOTH),
        P(),
        P(None, BOTH),
        P(None, BOTH),
        P(BOTH, None),
    )
    return jax.shard_map(
        body,
        mesh=mesh,
        in_specs=placed,
        out_specs=(P("ctx", "head", None), P(None, BOTH)),
        check_vma=False,
    )
```

```python
import functools

import jax
import jax.numpy as jnp
from jax import lax
from jax.experimental import pallas as pl
from jax.experimental.pallas import tpu as pltpu
from jax.sharding import PartitionSpec as P

SCORE_SCALE = 168.0 ** (-0.5)
NORM_EPSILON = 1e-06
MASKED = -1e30
MIB = 1024 * 1024
LOADS = 3
COST = pl.CostEstimate(flops=10**9, bytes_accessed=32 * MIB, transcendentals=10**6)
BOTH = ("ctx", "head")


def head_bias(rows, columns, heads, kv_heads):
    group = heads // kv_heads
    tile = (heads, 128)
    row = lax.broadcasted_iota(jnp.int32, tile, 0)
    column = lax.broadcasted_iota(jnp.int32, tile, 1)
    bias = jnp.where(row // group == lax.rem(column, kv_heads), 0.0, MASKED)
    return jnp.tile(bias, (rows // heads, columns // 128))


def in_hbm(operand):
    return pltpu.with_memory_space_constraint(operand, pltpu.HBM)


def dot_rows(left, right):
    return lax.dot_general(left, right, (((1,), (1,)), ((), ())), preferred_element_type=jnp.float32)


def stat_rows(row_max, row_total, shape):
    lane = lax.broadcasted_iota(jnp.int32, shape, 1)
    return jnp.where(lane == 0, row_max, row_total)


def spread_kernel(source_ref, copies_ref, sems):
    copies = [
        pltpu.make_async_copy(source_ref, copies_ref.at[pl.ds(place, 1)], sems.at[place])
        for place in range(copies_ref.shape[0])
    ]
    for copy in copies:
        copy.start()
    for copy in copies:
        copy.wait()


def spread(value, count):
    return pl.pallas_call(
        spread_kernel,
        out_shape=jax.ShapeDtypeStruct((count, *value.shape[1:]), value.dtype),
        in_specs=[pl.BlockSpec(memory_space=pl.ANY)],
        scratch_shapes=[pltpu.SemaphoreType.DMA((count,))],
        compiler_params=pltpu.CompilerParams(vmem_limit_bytes=4 * MIB),
    )(in_hbm(value))


def attention_kernel(
    length_ref, arrived_ref, q_hbm, kn_hbm, vn_hbm, ks_hbm, vs_hbm, kp_hbm, vp_hbm,
    part_ref,
    q_ref, kn_ref, vn_ref, ks_ref, vs_ref, kp_ref, vp_ref, sems,
):
    pairs = (
        (kp_hbm, kp_ref), (q_hbm, q_ref), (ks_hbm, ks_ref), (kn_hbm, kn_ref),
        (vs_hbm, vs_ref), (vn_hbm, vn_ref), (vp_hbm, vp_ref),
    )
    copies = [
        pltpu.make_async_copy(source, target, sems.at[place])
        for place, (source, target) in enumerate(pairs)
    ]
    copies[0].start()
    count, heads, width = arrived_ref.shape
    kv_heads = kn_ref.shape[1]
    queries = arrived_ref[...].reshape(count * heads, width)
    copies[0].wait()
    for copy in copies[1:]:
        copy.start()
    scores = SCORE_SCALE * dot_rows(queries, kp_ref[...])
    scores = scores + head_bias(*scores.shape, heads, kv_heads)
    row_max = jnp.max(scores, axis=1, keepdims=True)
    weights = jnp.exp(scores - row_max).astype(jnp.bfloat16)
    row_total = jnp.sum(weights.astype(jnp.float32), axis=1, keepdims=True)
    for copy in copies[1:6]:
        copy.wait()
    own = q_ref[0]
    own_scores = SCORE_SCALE * dot_rows(own, ks_ref[...])
    new_scores = SCORE_SCALE * dot_rows(own, kn_ref[0])
    slot = lax.broadcasted_iota(jnp.int32, own_scores.shape, 1) // kv_heads
    own_scores = own_scores + head_bias(*own_scores.shape, heads, kv_heads)
    own_scores = jnp.where(slot < length_ref[0], own_scores, MASKED)
    new_scores = new_scores + head_bias(heads, 128, heads, kv_heads)[:, :kv_heads]
    suffix_max = jnp.maximum(
        jnp.max(own_scores, axis=1, keepdims=True), jnp.max(new_scores, axis=1, keepdims=True)
    )
    own_weights = jnp.exp(own_scores - suffix_max).astype(jnp.bfloat16)
    new_weights = jnp.exp(new_scores - suffix_max).astype(jnp.bfloat16)
    suffix_total = jnp.sum(own_weights.astype(jnp.float32), axis=1, keepdims=True) + jnp.sum(
        new_weights.astype(jnp.float32), axis=1, keepdims=True
    )
    suffix_sum = jnp.dot(own_weights, vs_ref[...], preferred_element_type=jnp.float32) + jnp.dot(
        new_weights, vn_ref[0], preferred_element_type=jnp.float32
    )
    copies[6].wait()
    row_sum = jnp.dot(weights, vp_ref[...], preferred_element_type=jnp.float32)
    part_ref[:, 0] = row_sum.reshape(count, heads, width)
    part_ref[:, 1] = stat_rows(row_max, row_total, row_sum.shape).reshape(count, heads, width)
    me = lax.axis_index("ctx")
    prefix_stat = part_ref[me, 1]
    prefix_max = prefix_stat[:, 0:1]
    joint_max = jnp.maximum(prefix_max, suffix_max)
    prefix_factor = jnp.exp(prefix_max - joint_max)
    suffix_factor = jnp.exp(suffix_max - joint_max)
    joint_total = prefix_stat[:, 1:2] * prefix_factor + suffix_total * suffix_factor
    joint_sum = part_ref[me, 0] * prefix_factor + suffix_sum * suffix_factor
    part_ref[me, 0] = joint_sum
    part_ref[me, 1] = stat_rows(joint_max, joint_total, joint_sum.shape)


def attend(lengths, arrived, *operands):
    count, heads, width = arrived.shape
    return pl.pallas_call(
        attention_kernel,
        out_shape=jax.ShapeDtypeStruct((count, 2, heads, width), jnp.float32),
        in_specs=[pl.BlockSpec(memory_space=pltpu.SMEM), pl.BlockSpec(memory_space=pltpu.VMEM)]
        + [pl.BlockSpec(memory_space=pl.ANY)] * len(operands),
        scratch_shapes=[pltpu.VMEM(operand.shape, operand.dtype) for operand in operands]
        + [pltpu.SemaphoreType.DMA((len(operands),))],
        compiler_params=pltpu.CompilerParams(vmem_limit_bytes=24 * MIB),
        cost_estimate=COST,
    )(lengths, arrived, *map(in_hbm, operands))


def join_kernel(part_ref, out_ref, copies_ref):
    sources = part_ref.shape[0]
    joint_max = functools.reduce(
        jnp.maximum, [part_ref[source, 1, :, 0:1] for source in range(sources)]
    )
    total = jnp.zeros_like(joint_max)
    summed = jnp.zeros(out_ref.shape, jnp.float32)
    for source in range(sources):
        factor = jnp.exp(part_ref[source, 1, :, 0:1] - joint_max)
        total = total + part_ref[source, 1, :, 1:2] * factor
        summed = summed + part_ref[source, 0] * factor
    attention = (summed / total).astype(jnp.bfloat16)
    out_ref[...] = attention
    for place in range(copies_ref.shape[0]):
        copies_ref[place] = attention


def join_partials(parts, devices):
    shape = parts.shape[2:]
    return pl.pallas_call(
        join_kernel,
        out_shape=(
            jax.ShapeDtypeStruct(shape, jnp.bfloat16),
            jax.ShapeDtypeStruct((devices, *shape), jnp.bfloat16),
        ),
        compiler_params=pltpu.CompilerParams(vmem_limit_bytes=8 * MIB),
        cost_estimate=COST,
    )(parts)


def project_kernel(rows_ref, w_ref, residual_ref, out_ref, copies_ref, wide_ref):
    devices, heads, width = rows_ref.shape
    completions = residual_ref.shape[0]
    all_heads = devices * heads // completions
    wide_ref[...] = rows_ref[...].reshape(devices * heads, width).astype(jnp.float32)
    rows = [wide_ref[pl.ds(head, completions, stride=all_heads), :] for head in range(all_heads)]
    rows = jnp.concatenate([row.astype(jnp.bfloat16) for row in rows], axis=1)
    hidden = (residual_ref[...].astype(jnp.float32) + dot_rows(rows, w_ref[...])).astype(jnp.bfloat16)
    out_ref[...] = hidden
    for place in range(copies_ref.shape[0]):
        copies_ref[place] = hidden


def project(rows, w_out, residual):
    devices, heads, width = rows.shape
    return pl.pallas_call(
        project_kernel,
        out_shape=(
            jax.ShapeDtypeStruct(residual.shape, jnp.bfloat16),
            jax.ShapeDtypeStruct((devices, *residual.shape), jnp.bfloat16),
        ),
        scratch_shapes=[pltpu.VMEM((devices * heads, width), jnp.float32)],
        compiler_params=pltpu.CompilerParams(vmem_limit_bytes=12 * MIB),
        cost_estimate=COST,
    )(rows, w_out, residual)


def row_chunks(rows, most):
    for count in range(most, 1, -1):
        if rows % (16 * count) == 0:
            return count
    return 1


def forward_kernel(
    pieces_ref, gain_ref, gate_hbm, up_hbm, down_hbm, out_ref, state_ref, gate_ref, up_ref, down_ref, sems
):
    units = gate_ref.shape[0]
    count = row_chunks(units, LOADS)
    size = units // count
    copies = []
    for chunk in range(count):
        rows = pl.ds(chunk * size, size)
        for place, (source, target) in enumerate(
            ((gate_hbm, gate_ref), (up_hbm, up_ref), (down_hbm, down_ref))
        ):
            copies.append(
                pltpu.make_async_copy(source.at[rows], target.at[rows], sems.at[3 * chunk + place])
            )
            copies[-1].start()
    devices, completions, columns = pieces_ref.shape
    for place in range(devices):
        state_ref[:, place * columns : (place + 1) * columns] = pieces_ref[place].astype(jnp.float32)
    state = state_ref[...]
    mean_square = jnp.mean(state * state, axis=-1, keepdims=True)
    gain = gain_ref[...].reshape(1, devices * columns)
    normed = (state * lax.rsqrt(mean_square + NORM_EPSILON) * gain).astype(jnp.bfloat16)
    share = jnp.zeros(state.shape, jnp.float32)
    for chunk in range(count):
        rows = slice(chunk * size, (chunk + 1) * size)
        copies[3 * chunk].wait()
        gate_values = dot_rows(normed, gate_ref[rows])
        copies[3 * chunk + 1].wait()
        up_values = dot_rows(normed, up_ref[rows])
        activated = (jax.nn.gelu(gate_values, approximate=True) * up_values).astype(jnp.bfloat16)
        copies[3 * chunk + 2].wait()
        share += jnp.dot(activated, down_ref[rows], preferred_element_type=jnp.float32)
    for place in range(devices):
        out_ref[place] = share[:, place * columns : (place + 1) * columns].astype(jnp.bfloat16)


def forward(pieces, gain, *weights):
    devices, completions, columns = pieces.shape
    whole = pl.BlockSpec(memory_space=pltpu.VMEM)
    return pl.pallas_call(
        forward_kernel,
        out_shape=jax.ShapeDtypeStruct(pieces.shape, jnp.bfloat16),
        in_specs=[whole, whole] + [pl.BlockSpec(memory_space=pl.ANY)] * 3,
        scratch_shapes=[pltpu.VMEM((completions, devices * columns), jnp.float32)]
        + [pltpu.VMEM(w.shape, w.dtype) for w in weights]
        + [pltpu.SemaphoreType.DMA((3 * LOADS,))],
        compiler_params=pltpu.CompilerParams(vmem_limit_bytes=30 * MIB),
        cost_estimate=COST,
    )(pieces, gain, *map(in_hbm, weights))


def exchange(copies, axes=BOTH):
    return lax.all_to_all(copies, axes, split_axis=0, concat_axis=0, tiled=True)


def body(
    queries,
    k_new,
    v_new,
    k_suffix,
    v_suffix,
    lengths,
    k_prefix,
    v_prefix,
    w_out,
    residual,
    norm_gain,
    w_gate,
    w_up,
    w_down,
):
    ctx_count = lax.axis_size("ctx")
    devices = ctx_count * lax.axis_size("head")
    arrived = exchange(spread(queries, ctx_count), "ctx")
    rows_of = lambda values: values.reshape(-1, values.shape[-1])
    parts = attend(
        lengths, arrived, queries, k_new, v_new, *map(rows_of, (k_suffix, v_suffix, k_prefix, v_prefix))
    )
    attention, copies = join_partials(exchange(parts, "ctx"), devices)
    hidden_part, copies = project(exchange(copies), w_out.T, residual)
    shares = forward(exchange(copies), norm_gain, w_gate.T, w_up.T, w_down)
    summed = jnp.sum(exchange(shares).astype(jnp.float32), axis=0)
    next_hidden = (hidden_part.astype(jnp.float32) + summed).astype(jnp.bfloat16)
    return (attention[None], next_hidden)


def solution(mesh):
    placed = (
        P("ctx", "head", None),
        P("ctx", "head", None),
        P("ctx", "head", None),
        P("ctx", None, "head", None),
        P("ctx", None, "head", None),
        P("ctx"),
        P("ctx", "head", None),
        P("ctx", "head", None),
        P(None, BOTH),
        P(None, BOTH),
        P(),
        P(None, BOTH),
        P(None, BOTH),
        P(BOTH, None),
    )
    return jax.shard_map(
        body,
        mesh=mesh,
        in_specs=placed,
        out_specs=(P("ctx", "head", None), P(None, BOTH)),
        check_vma=False,
    )
```

```python
import functools

import jax
import jax.numpy as jnp
from jax import lax
from jax.experimental import pallas as pl
from jax.experimental.pallas import tpu as pltpu
from jax.sharding import PartitionSpec as P

SCORE_SCALE = 168.0 ** (-0.5)
NORM_EPSILON = 1e-06
MASKED = -1e30
MIB = 1024 * 1024
CHUNKS = 3
SPLIT = 2
AHEAD = 5
COST = pl.CostEstimate(flops=10**9, bytes_accessed=32 * MIB, transcendentals=10**6)
BOTH = ("ctx", "head")


def head_bias(rows, columns, heads, kv_heads):
    group = heads // kv_heads
    tile = (heads, 128)
    row = lax.broadcasted_iota(jnp.int32, tile, 0)
    column = lax.broadcasted_iota(jnp.int32, tile, 1)
    bias = jnp.where(row // group == lax.rem(column, kv_heads), 0.0, MASKED)
    return jnp.tile(bias, (rows // heads, columns // 128))


def in_hbm(operand):
    return pltpu.with_memory_space_constraint(operand, pltpu.HBM)


def dot_rows(left, right):
    return lax.dot_general(left, right, (((1,), (1,)), ((), ())), preferred_element_type=jnp.float32)


def stat_rows(row_max, row_total, shape):
    lane = lax.broadcasted_iota(jnp.int32, shape, 1)
    return jnp.where(lane == 0, row_max, row_total)


def spread_kernel(source_ref, copies_ref, sems):
    copies = [
        pltpu.make_async_copy(source_ref, copies_ref.at[pl.ds(place, 1)], sems.at[place])
        for place in range(copies_ref.shape[0])
    ]
    for copy in copies:
        copy.start()
    for copy in copies:
        copy.wait()


def spread(value, count):
    return pl.pallas_call(
        spread_kernel,
        out_shape=jax.ShapeDtypeStruct((count, *value.shape[1:]), value.dtype),
        in_specs=[pl.BlockSpec(memory_space=pl.ANY)],
        out_specs=pl.BlockSpec(memory_space=pl.ANY),
        scratch_shapes=[pltpu.SemaphoreType.DMA((count,))],
        compiler_params=pltpu.CompilerParams(vmem_limit_bytes=4 * MIB),
    )(in_hbm(value))


def attention_kernel(
    length_ref, arrived_ref, q_hbm, kn_hbm, vn_hbm, ks_hbm, vs_hbm, kp_hbm, vp_hbm,
    part_ref,
    q_ref, kn_ref, vn_ref, ks_ref, vs_ref, kp_ref, vp_ref, sems,
):
    pairs = (
        (kp_hbm, kp_ref), (q_hbm, q_ref), (ks_hbm, ks_ref), (kn_hbm, kn_ref),
        (vs_hbm, vs_ref), (vn_hbm, vn_ref), (vp_hbm, vp_ref),
    )
    copies = [
        pltpu.make_async_copy(source, target, sems.at[place])
        for place, (source, target) in enumerate(pairs)
    ]
    copies[0].start()
    count, heads, width = arrived_ref.shape
    kv_heads = kn_ref.shape[1]
    queries = arrived_ref[...].reshape(count * heads, width)
    copies[0].wait()
    for copy in copies[1:]:
        copy.start()
    scores = SCORE_SCALE * dot_rows(queries, kp_ref[...])
    scores = scores + head_bias(*scores.shape, heads, kv_heads)
    row_max = jnp.max(scores, axis=1, keepdims=True)
    weights = jnp.exp(scores - row_max).astype(jnp.bfloat16)
    row_total = jnp.sum(weights.astype(jnp.float32), axis=1, keepdims=True)
    for copy in copies[1:6]:
        copy.wait()
    own = q_ref[0]
    own_scores = SCORE_SCALE * dot_rows(own, ks_ref[...])
    new_scores = SCORE_SCALE * dot_rows(own, kn_ref[0])
    slot = lax.broadcasted_iota(jnp.int32, own_scores.shape, 1) // kv_heads
    own_scores = own_scores + head_bias(*own_scores.shape, heads, kv_heads)
    own_scores = jnp.where(slot < length_ref[0], own_scores, MASKED)
    new_scores = new_scores + head_bias(heads, 128, heads, kv_heads)[:, :kv_heads]
    suffix_max = jnp.maximum(
        jnp.max(own_scores, axis=1, keepdims=True), jnp.max(new_scores, axis=1, keepdims=True)
    )
    own_weights = jnp.exp(own_scores - suffix_max).astype(jnp.bfloat16)
    new_weights = jnp.exp(new_scores - suffix_max).astype(jnp.bfloat16)
    suffix_total = jnp.sum(own_weights.astype(jnp.float32), axis=1, keepdims=True) + jnp.sum(
        new_weights.astype(jnp.float32), axis=1, keepdims=True
    )
    suffix_sum = jnp.dot(own_weights, vs_ref[...], preferred_element_type=jnp.float32) + jnp.dot(
        new_weights, vn_ref[0], preferred_element_type=jnp.float32
    )
    copies[6].wait()
    row_sum = jnp.dot(weights, vp_ref[...], preferred_element_type=jnp.float32)
    part_ref[:, 0] = row_sum.reshape(count, heads, width)
    part_ref[:, 1] = stat_rows(row_max, row_total, row_sum.shape).reshape(count, heads, width)
    me = lax.axis_index("ctx")
    prefix_stat = part_ref[me, 1]
    prefix_max = prefix_stat[:, 0:1]
    joint_max = jnp.maximum(prefix_max, suffix_max)
    prefix_factor = jnp.exp(prefix_max - joint_max)
    suffix_factor = jnp.exp(suffix_max - joint_max)
    joint_total = prefix_stat[:, 1:2] * prefix_factor + suffix_total * suffix_factor
    joint_sum = part_ref[me, 0] * prefix_factor + suffix_sum * suffix_factor
    part_ref[me, 0] = joint_sum
    part_ref[me, 1] = stat_rows(joint_max, joint_total, joint_sum.shape)


def attend(lengths, arrived, *operands):
    count, heads, width = arrived.shape
    return pl.pallas_call(
        attention_kernel,
        out_shape=jax.ShapeDtypeStruct((count, 2, heads, width), jnp.float32),
        in_specs=[pl.BlockSpec(memory_space=pltpu.SMEM), pl.BlockSpec(memory_space=pltpu.VMEM)]
        + [pl.BlockSpec(memory_space=pl.ANY)] * len(operands),
        scratch_shapes=[pltpu.VMEM(operand.shape, operand.dtype) for operand in operands]
        + [pltpu.SemaphoreType.DMA((len(operands),))],
        compiler_params=pltpu.CompilerParams(vmem_limit_bytes=24 * MIB),
        cost_estimate=COST,
    )(lengths, arrived, *map(in_hbm, operands))


def join_kernel(part_ref, copies_ref):
    sources = part_ref.shape[0]
    joint_max = functools.reduce(
        jnp.maximum, [part_ref[source, 1, :, 0:1] for source in range(sources)]
    )
    total = jnp.zeros_like(joint_max)
    summed = jnp.zeros(part_ref.shape[2:], jnp.float32)
    for source in range(sources):
        factor = jnp.exp(part_ref[source, 1, :, 0:1] - joint_max)
        total = total + part_ref[source, 1, :, 1:2] * factor
        summed = summed + part_ref[source, 0] * factor
    attention = (summed / total).astype(jnp.bfloat16)
    for place in range(copies_ref.shape[0]):
        copies_ref[place] = attention


def join_partials(parts, devices):
    shape = parts.shape[2:]
    return pl.pallas_call(
        join_kernel,
        out_shape=jax.ShapeDtypeStruct((devices, *shape), jnp.bfloat16),
        compiler_params=pltpu.CompilerParams(vmem_limit_bytes=8 * MIB),
        cost_estimate=COST,
    )(parts)


def project_kernel(rows_ref, w_ref, residual_ref, out_ref, copies_ref, wide_ref):
    devices, heads, width = rows_ref.shape
    completions = residual_ref.shape[0]
    all_heads = devices * heads // completions
    wide_ref[...] = rows_ref[...].reshape(devices * heads, width).astype(jnp.float32)
    rows = [wide_ref[pl.ds(head, completions, stride=all_heads), :] for head in range(all_heads)]
    rows = jnp.concatenate([row.astype(jnp.bfloat16) for row in rows], axis=1)
    hidden = (residual_ref[...].astype(jnp.float32) + dot_rows(rows, w_ref[...])).astype(jnp.bfloat16)
    out_ref[...] = hidden
    for place in range(copies_ref.shape[0]):
        copies_ref[place] = hidden


def project(rows, w_out, residual):
    devices, heads, width = rows.shape
    return pl.pallas_call(
        project_kernel,
        out_shape=(
            jax.ShapeDtypeStruct(residual.shape, jnp.bfloat16),
            jax.ShapeDtypeStruct((devices, *residual.shape), jnp.bfloat16),
        ),
        scratch_shapes=[pltpu.VMEM((devices * heads, width), jnp.float32)],
        compiler_params=pltpu.CompilerParams(vmem_limit_bytes=12 * MIB),
        cost_estimate=COST,
    )(rows, w_out, residual)


def row_chunks(rows, most):
    for count in range(most, 1, -1):
        if rows % (16 * count) == 0:
            return count
    return 1


def forward_kernel(
    pieces_ref, gain_ref, copies_ref, gate_hbm, up_hbm, down_hbm, out_ref, attention_hbm,
    state_ref, gate_ref, up_ref, down_ref, sems,
):
    units = gate_ref.shape[0]
    count = row_chunks(units, CHUNKS)
    size = units // count
    split = row_chunks(size, SPLIT)
    matrices = ((gate_hbm, gate_ref), (up_hbm, up_ref), (down_hbm, down_ref))
    loads = []
    for chunk in range(count):
        for source, target in matrices:
            for piece in range(split):
                rows = pl.ds(chunk * size + piece * (size // split), size // split)
                loads.append(
                    pltpu.make_async_copy(source.at[rows], target.at[rows], sems.at[len(loads)])
                )
    for load in loads[:AHEAD]:
        load.start()
    keep = pltpu.make_async_copy(copies_ref.at[0], attention_hbm, sems.at[len(loads)])
    keep.start()

    def arrived(place, chunk):
        first = (3 * chunk + place) * split
        for load in range(first, first + split):
            loads[load].wait()
            if load + AHEAD < len(loads):
                loads[load + AHEAD].start()
        return matrices[place][1][chunk * size : (chunk + 1) * size]

    devices, completions, columns = pieces_ref.shape
    for place in range(devices):
        state_ref[:, place * columns : (place + 1) * columns] = pieces_ref[place].astype(jnp.float32)
    state = state_ref[...]
    mean_square = jnp.mean(state * state, axis=-1, keepdims=True)
    gain = gain_ref[...].reshape(1, devices * columns)
    normed = (state * lax.rsqrt(mean_square + NORM_EPSILON) * gain).astype(jnp.bfloat16)
    share = jnp.zeros(state.shape, jnp.float32)
    for chunk in range(count):
        gate_values = dot_rows(normed, arrived(0, chunk))
        up_values = dot_rows(normed, arrived(1, chunk))
        activated = (jax.nn.gelu(gate_values, approximate=True) * up_values).astype(jnp.bfloat16)
        share += jnp.dot(activated, arrived(2, chunk), preferred_element_type=jnp.float32)
    for place in range(devices):
        out_ref[place] = share[:, place * columns : (place + 1) * columns].astype(jnp.bfloat16)
    keep.wait()


def forward(pieces, gain, copies, *weights):
    devices, completions, columns = pieces.shape
    whole = pl.BlockSpec(memory_space=pltpu.VMEM)
    far = pl.BlockSpec(memory_space=pl.ANY)
    return pl.pallas_call(
        forward_kernel,
        out_shape=(
            jax.ShapeDtypeStruct(pieces.shape, jnp.bfloat16),
            jax.ShapeDtypeStruct(copies.shape[1:], jnp.bfloat16),
        ),
        in_specs=[whole, whole, whole, far, far, far],
        out_specs=(whole, far),
        scratch_shapes=[pltpu.VMEM((completions, devices * columns), jnp.float32)]
        + [pltpu.VMEM(w.shape, w.dtype) for w in weights]
        + [pltpu.SemaphoreType.DMA((3 * CHUNKS * SPLIT + 1,))],
        compiler_params=pltpu.CompilerParams(vmem_limit_bytes=30 * MIB),
        cost_estimate=COST,
    )(pieces, gain, copies, *map(in_hbm, weights))


def exchange(copies, axes=BOTH):
    return lax.all_to_all(copies, axes, split_axis=0, concat_axis=0, tiled=True)


def body(
    queries,
    k_new,
    v_new,
    k_suffix,
    v_suffix,
    lengths,
    k_prefix,
    v_prefix,
    w_out,
    residual,
    norm_gain,
    w_gate,
    w_up,
    w_down,
):
    ctx_count = lax.axis_size("ctx")
    devices = ctx_count * lax.axis_size("head")
    arrived = exchange(spread(queries, ctx_count), "ctx")
    rows_of = lambda values: values.reshape(-1, values.shape[-1])
    parts = attend(
        lengths, arrived, queries, k_new, v_new, *map(rows_of, (k_suffix, v_suffix, k_prefix, v_prefix))
    )
    copies = join_partials(exchange(parts, "ctx"), devices)
    hidden_part, hidden_copies = project(exchange(copies), w_out.T, residual)
    shares, attention = forward(
        exchange(hidden_copies), norm_gain, copies, w_gate.T, w_up.T, w_down
    )
    summed = jnp.sum(exchange(shares).astype(jnp.float32), axis=0)
    next_hidden = (hidden_part.astype(jnp.float32) + summed).astype(jnp.bfloat16)
    return (attention[None], next_hidden)


def solution(mesh):
    placed = (
        P("ctx", "head", None),
        P("ctx", "head", None),
        P("ctx", "head", None),
        P("ctx", None, "head", None),
        P("ctx", None, "head", None),
        P("ctx"),
        P("ctx", "head", None),
        P("ctx", "head", None),
        P(None, BOTH),
        P(None, BOTH),
        P(),
        P(None, BOTH),
        P(None, BOTH),
        P(BOTH, None),
    )
    return jax.shard_map(
        body,
        mesh=mesh,
        in_specs=placed,
        out_specs=(P("ctx", "head", None), P(None, BOTH)),
        check_vma=False,
    )
```

```python
import functools

import jax
import jax.numpy as jnp
from jax import lax
from jax.experimental import pallas as pl
from jax.experimental.pallas import tpu as pltpu
from jax.sharding import PartitionSpec as P

SCORE_SCALE = 168.0 ** (-0.5)
NORM_EPSILON = 1e-06
MASKED = -1e30
MIB = 1024 * 1024
COST = pl.CostEstimate(flops=10**10, bytes_accessed=MIB, transcendentals=10**6)
BOTH = ("ctx", "head")


def head_bias(rows, columns, heads, kv_heads):
    group = heads // kv_heads
    tile = (heads, 128)
    row = lax.broadcasted_iota(jnp.int32, tile, 0)
    column = lax.broadcasted_iota(jnp.int32, tile, 1)
    bias = jnp.where(row // group == lax.rem(column, kv_heads), 0.0, MASKED)
    return jnp.tile(bias, (rows // heads, columns // 128))


def in_hbm(operand):
    return pltpu.with_memory_space_constraint(operand, pltpu.HBM)


def dot_rows(left, right):
    return lax.dot_general(left, right, (((1,), (1,)), ((), ())), preferred_element_type=jnp.float32)


def stat_rows(row_max, row_total, shape):
    lane = lax.broadcasted_iota(jnp.int32, shape, 1)
    return jnp.where(lane == 0, row_max, row_total)


def spread_kernel(length_ref, source_hbm, copies_ref, lengths_ref, source_ref, sem):
    load = pltpu.make_async_copy(source_hbm, source_ref, sem)
    load.start()
    lengths_ref[...] = jnp.full(lengths_ref.shape, length_ref[0], jnp.int32)
    load.wait()
    for place in range(copies_ref.shape[0]):
        copies_ref[place] = source_ref[0]


def spread(lengths, value, count):
    return pl.pallas_call(
        spread_kernel,
        out_shape=(
            jax.ShapeDtypeStruct((count, *value.shape[1:]), value.dtype),
            jax.ShapeDtypeStruct(value.shape[1:], jnp.int32),
        ),
        in_specs=[pl.BlockSpec(memory_space=pltpu.SMEM), pl.BlockSpec(memory_space=pl.ANY)],
        scratch_shapes=[pltpu.VMEM(value.shape, value.dtype), pltpu.SemaphoreType.DMA],
        compiler_params=pltpu.CompilerParams(vmem_limit_bytes=4 * MIB),
        cost_estimate=COST,
    )(lengths, in_hbm(value))


def attention_kernel(
    length_ref, arrived_ref, q_ref, kn_ref, vn_ref, ks_ref, vs_ref, kp_ref, vp_ref, part_ref
):
    count, heads, width = arrived_ref.shape
    kv_heads = kn_ref.shape[1]
    queries = arrived_ref[...].reshape(count * heads, width)
    scores = SCORE_SCALE * dot_rows(queries, kp_ref[...])
    scores = scores + head_bias(*scores.shape, heads, kv_heads)
    row_max = jnp.max(scores, axis=1, keepdims=True)
    weights = jnp.exp(scores - row_max).astype(jnp.bfloat16)
    row_total = jnp.sum(weights.astype(jnp.float32), axis=1, keepdims=True)
    own = q_ref[0]
    own_scores = SCORE_SCALE * dot_rows(own, ks_ref[...])
    new_scores = SCORE_SCALE * dot_rows(own, kn_ref[0])
    slot = lax.broadcasted_iota(jnp.int32, own_scores.shape, 1) // kv_heads
    own_scores = own_scores + head_bias(*own_scores.shape, heads, kv_heads)
    own_scores = jnp.where(slot < length_ref[:, 0:1], own_scores, MASKED)
    new_scores = new_scores + head_bias(heads, 128, heads, kv_heads)[:, :kv_heads]
    suffix_max = jnp.maximum(
        jnp.max(own_scores, axis=1, keepdims=True), jnp.max(new_scores, axis=1, keepdims=True)
    )
    own_weights = jnp.exp(own_scores - suffix_max).astype(jnp.bfloat16)
    new_weights = jnp.exp(new_scores - suffix_max).astype(jnp.bfloat16)
    suffix_total = jnp.sum(own_weights.astype(jnp.float32), axis=1, keepdims=True) + jnp.sum(
        new_weights.astype(jnp.float32), axis=1, keepdims=True
    )
    suffix_sum = jnp.dot(own_weights, vs_ref[...], preferred_element_type=jnp.float32) + jnp.dot(
        new_weights, vn_ref[0], preferred_element_type=jnp.float32
    )
    row_sum = jnp.dot(weights, vp_ref[...], preferred_element_type=jnp.float32)
    part_ref[:, 0] = row_sum.reshape(count, heads, width)
    part_ref[:, 1] = stat_rows(row_max, row_total, row_sum.shape).reshape(count, heads, width)
    me = lax.axis_index("ctx")
    prefix_stat = part_ref[me, 1]
    prefix_max = prefix_stat[:, 0:1]
    joint_max = jnp.maximum(prefix_max, suffix_max)
    prefix_factor = jnp.exp(prefix_max - joint_max)
    suffix_factor = jnp.exp(suffix_max - joint_max)
    joint_total = prefix_stat[:, 1:2] * prefix_factor + suffix_total * suffix_factor
    joint_sum = part_ref[me, 0] * prefix_factor + suffix_sum * suffix_factor
    part_ref[me, 0] = joint_sum
    part_ref[me, 1] = stat_rows(joint_max, joint_total, joint_sum.shape)


def attend(lengths, arrived, *operands):
    return pl.pallas_call(
        attention_kernel,
        out_shape=jax.ShapeDtypeStruct((arrived.shape[0], 2, *arrived.shape[1:]), jnp.float32),
        compiler_params=pltpu.CompilerParams(vmem_limit_bytes=24 * MIB),
        cost_estimate=COST,
    )(lengths, arrived, *operands)


def join_kernel(part_ref, copies_ref):
    sources = part_ref.shape[0]
    joint_max = functools.reduce(
        jnp.maximum, [part_ref[source, 1, :, 0:1] for source in range(sources)]
    )
    total = jnp.zeros_like(joint_max)
    summed = jnp.zeros(part_ref.shape[2:], jnp.float32)
    for source in range(sources):
        factor = jnp.exp(part_ref[source, 1, :, 0:1] - joint_max)
        total = total + part_ref[source, 1, :, 1:2] * factor
        summed = summed + part_ref[source, 0] * factor
    attention = (summed / total).astype(jnp.bfloat16)
    for place in range(copies_ref.shape[0]):
        copies_ref[place] = attention


def join_partials(parts, devices):
    shape = parts.shape[2:]
    return pl.pallas_call(
        join_kernel,
        out_shape=jax.ShapeDtypeStruct((devices, *shape), jnp.bfloat16),
        compiler_params=pltpu.CompilerParams(vmem_limit_bytes=8 * MIB),
        cost_estimate=COST,
    )(parts)


def project_kernel(rows_ref, w_ref, residual_ref, out_ref, copies_ref, wide_ref):
    devices, heads, width = rows_ref.shape
    completions = residual_ref.shape[0]
    all_heads = devices * heads // completions
    wide_ref[...] = rows_ref[...].reshape(devices * heads, width).astype(jnp.float32)
    rows = [wide_ref[pl.ds(head, completions, stride=all_heads), :] for head in range(all_heads)]
    rows = jnp.concatenate([row.astype(jnp.bfloat16) for row in rows], axis=1)
    hidden = (residual_ref[...].astype(jnp.float32) + dot_rows(rows, w_ref[...])).astype(jnp.bfloat16)
    out_ref[...] = hidden
    for place in range(copies_ref.shape[0]):
        copies_ref[place] = hidden


def project(rows, w_out, residual):
    devices, heads, width = rows.shape
    return pl.pallas_call(
        project_kernel,
        out_shape=(
            jax.ShapeDtypeStruct(residual.shape, jnp.bfloat16),
            jax.ShapeDtypeStruct((devices, *residual.shape), jnp.bfloat16),
        ),
        scratch_shapes=[pltpu.VMEM((devices * heads, width), jnp.float32)],
        compiler_params=pltpu.CompilerParams(vmem_limit_bytes=12 * MIB),
        cost_estimate=COST,
    )(rows, w_out, residual)


def forward_kernel(
    pieces_ref, gain_ref, copies_ref, gate_ref, up_ref, down_ref, out_ref, attention_hbm, state_ref, sem
):
    keep = pltpu.make_async_copy(copies_ref.at[0], attention_hbm, sem)
    keep.start()
    devices, completions, columns = pieces_ref.shape
    for place in range(devices):
        state_ref[:, place * columns : (place + 1) * columns] = pieces_ref[place].astype(jnp.float32)
    state = state_ref[...]
    mean_square = jnp.mean(state * state, axis=-1, keepdims=True)
    gain = gain_ref[...].reshape(1, devices * columns)
    normed = (state * lax.rsqrt(mean_square + NORM_EPSILON) * gain).astype(jnp.bfloat16)
    gate_values = dot_rows(normed, gate_ref[...])
    up_values = dot_rows(normed, up_ref[...])
    activated = (jax.nn.gelu(gate_values, approximate=True) * up_values).astype(jnp.bfloat16)
    share = jnp.dot(activated, down_ref[...], preferred_element_type=jnp.float32)
    for place in range(devices):
        out_ref[place] = share[:, place * columns : (place + 1) * columns].astype(jnp.bfloat16)
    keep.wait()


def forward(pieces, gain, copies, *weights):
    devices, completions, columns = pieces.shape
    return pl.pallas_call(
        forward_kernel,
        out_shape=(
            jax.ShapeDtypeStruct(pieces.shape, jnp.bfloat16),
            jax.ShapeDtypeStruct(copies.shape[1:], jnp.bfloat16),
        ),
        out_specs=(pl.BlockSpec(memory_space=pltpu.VMEM), pl.BlockSpec(memory_space=pl.ANY)),
        scratch_shapes=[
            pltpu.VMEM((completions, devices * columns), jnp.float32),
            pltpu.SemaphoreType.DMA,
        ],
        compiler_params=pltpu.CompilerParams(vmem_limit_bytes=8 * MIB),
        cost_estimate=COST,
    )(pieces, gain, copies, *weights)


def exchange(copies, axes=BOTH):
    return lax.all_to_all(copies, axes, split_axis=0, concat_axis=0, tiled=True)


def body(
    queries,
    k_new,
    v_new,
    k_suffix,
    v_suffix,
    lengths,
    k_prefix,
    v_prefix,
    w_out,
    residual,
    norm_gain,
    w_gate,
    w_up,
    w_down,
):
    ctx_count = lax.axis_size("ctx")
    devices = ctx_count * lax.axis_size("head")
    copies, own_length = spread(lengths, queries, ctx_count)
    arrived = exchange(copies, "ctx")
    rows_of = lambda values: values.reshape(-1, values.shape[-1])
    parts = attend(
        own_length, arrived, queries, k_new, v_new, *map(rows_of, (k_suffix, v_suffix, k_prefix, v_prefix))
    )
    copies = join_partials(exchange(parts, "ctx"), devices)
    hidden_part, hidden_copies = project(exchange(copies), w_out.T, residual)
    shares, attention = forward(
        exchange(hidden_copies), norm_gain, copies, w_gate.T, w_up.T, w_down
    )
    summed = jnp.sum(exchange(shares).astype(jnp.float32), axis=0)
    next_hidden = (hidden_part.astype(jnp.float32) + summed).astype(jnp.bfloat16)
    return (attention[None], next_hidden)


def solution(mesh):
    placed = (
        P("ctx", "head", None),
        P("ctx", "head", None),
        P("ctx", "head", None),
        P("ctx", None, "head", None),
        P("ctx", None, "head", None),
        P("ctx"),
        P("ctx", "head", None),
        P("ctx", "head", None),
        P(None, BOTH),
        P(None, BOTH),
        P(),
        P(None, BOTH),
        P(None, BOTH),
        P(BOTH, None),
    )
    return jax.shard_map(
        body,
        mesh=mesh,
        in_specs=placed,
        out_specs=(P("ctx", "head", None), P(None, BOTH)),
        check_vma=False,
    )
```

```python
import functools

import jax
import jax.numpy as jnp
from jax import lax
from jax.experimental import pallas as pl
from jax.experimental.pallas import tpu as pltpu
from jax.sharding import PartitionSpec as P

SCORE_SCALE = 168.0 ** (-0.5)
NORM_EPSILON = 1e-06
MASKED = -1e30
MIB = 1024 * 1024
COST = pl.CostEstimate(flops=10**10, bytes_accessed=MIB, transcendentals=10**6)
BOTH = ("ctx", "head")


def head_bias(rows, columns, heads, kv_heads):
    group = heads // kv_heads
    tile = (heads, 128)
    row = lax.broadcasted_iota(jnp.int32, tile, 0)
    column = lax.broadcasted_iota(jnp.int32, tile, 1)
    bias = jnp.where(row // group == lax.rem(column, kv_heads), 0.0, MASKED)
    return jnp.tile(bias, (rows // heads, columns // 128))


def in_hbm(operand):
    return pltpu.with_memory_space_constraint(operand, pltpu.HBM)


def dot_rows(left, right):
    return lax.dot_general(left, right, (((1,), (1,)), ((), ())), preferred_element_type=jnp.float32)


def stat_rows(row_max, row_total, shape):
    lane = lax.broadcasted_iota(jnp.int32, shape, 1)
    return jnp.where(lane == 0, row_max, row_total)


def spread_kernel(length_ref, source_hbm, copies_ref, lengths_ref, source_ref, sem):
    load = pltpu.make_async_copy(source_hbm, source_ref, sem)
    load.start()
    lengths_ref[...] = jnp.full(lengths_ref.shape, length_ref[0], jnp.int32)
    load.wait()
    for place in range(copies_ref.shape[0]):
        copies_ref[place] = source_ref[0]


def spread(lengths, value, count):
    return pl.pallas_call(
        spread_kernel,
        out_shape=(
            jax.ShapeDtypeStruct((count, *value.shape[1:]), value.dtype),
            jax.ShapeDtypeStruct(value.shape[1:], jnp.int32),
        ),
        in_specs=[pl.BlockSpec(memory_space=pltpu.SMEM), pl.BlockSpec(memory_space=pl.ANY)],
        scratch_shapes=[pltpu.VMEM(value.shape, value.dtype), pltpu.SemaphoreType.DMA],
        compiler_params=pltpu.CompilerParams(vmem_limit_bytes=4 * MIB),
        cost_estimate=COST,
    )(lengths, in_hbm(value))


def attention_kernel(
    groups, length_ref, arrived_ref, q_ref, kn_ref, vn_ref, ks_ref, vs_ref, kp_ref, vp_ref,
    part_ref, sum_ref, stat_ref,
):
    count, heads, width = sum_ref.shape
    me, group = lax.axis_index("ctx"), lax.axis_index("head")
    kv_heads = kn_ref.shape[1]
    queries = jnp.concatenate([arrived_ref[place * groups + group] for place in range(count)], axis=0)
    scores = SCORE_SCALE * dot_rows(queries, kp_ref[...])
    scores = scores + head_bias(*scores.shape, heads, kv_heads)
    row_max = jnp.max(scores, axis=1, keepdims=True)
    weights = jnp.exp(scores - row_max).astype(jnp.bfloat16)
    row_total = jnp.sum(weights.astype(jnp.float32), axis=1, keepdims=True)
    own = q_ref[0]
    own_scores = SCORE_SCALE * dot_rows(own, ks_ref[...])
    new_scores = SCORE_SCALE * dot_rows(own, kn_ref[0])
    slot = lax.broadcasted_iota(jnp.int32, own_scores.shape, 1) // kv_heads
    own_scores = own_scores + head_bias(*own_scores.shape, heads, kv_heads)
    own_scores = jnp.where(slot < length_ref[:, 0:1], own_scores, MASKED)
    new_scores = new_scores + head_bias(heads, 128, heads, kv_heads)[:, :kv_heads]
    suffix_max = jnp.maximum(
        jnp.max(own_scores, axis=1, keepdims=True), jnp.max(new_scores, axis=1, keepdims=True)
    )
    own_weights = jnp.exp(own_scores - suffix_max).astype(jnp.bfloat16)
    new_weights = jnp.exp(new_scores - suffix_max).astype(jnp.bfloat16)
    suffix_total = jnp.sum(own_weights.astype(jnp.float32), axis=1, keepdims=True) + jnp.sum(
        new_weights.astype(jnp.float32), axis=1, keepdims=True
    )
    suffix_sum = jnp.dot(own_weights, vs_ref[...], preferred_element_type=jnp.float32) + jnp.dot(
        new_weights, vn_ref[0], preferred_element_type=jnp.float32
    )
    row_sum = jnp.dot(weights, vp_ref[...], preferred_element_type=jnp.float32)
    sum_ref[...] = row_sum.reshape(count, heads, width)
    stat_ref[...] = stat_rows(row_max, row_total, row_sum.shape).reshape(count, heads, width)
    prefix_stat = stat_ref[me]
    prefix_max = prefix_stat[:, 0:1]
    joint_max = jnp.maximum(prefix_max, suffix_max)
    prefix_factor = jnp.exp(prefix_max - joint_max)
    suffix_factor = jnp.exp(suffix_max - joint_max)
    joint_total = prefix_stat[:, 1:2] * prefix_factor + suffix_total * suffix_factor
    joint_sum = sum_ref[me] * prefix_factor + suffix_sum * suffix_factor
    sum_ref[me] = joint_sum
    stat_ref[me] = stat_rows(joint_max, joint_total, joint_sum.shape)
    share = heads // groups
    for place in range(count):
        for taker in range(groups):
            rows = slice(taker * share, (taker + 1) * share)
            part_ref[place * groups + taker, :share] = sum_ref[place, rows]
            part_ref[place * groups + taker, share:] = stat_ref[place, rows]


def attend(groups, lengths, arrived, *operands):
    devices, heads, width = arrived.shape
    count = devices // groups
    return pl.pallas_call(
        functools.partial(attention_kernel, groups),
        out_shape=jax.ShapeDtypeStruct((devices, 2 * (heads // groups), width), jnp.float32),
        scratch_shapes=[pltpu.VMEM((count, heads, width), jnp.float32)] * 2,
        compiler_params=pltpu.CompilerParams(vmem_limit_bytes=24 * MIB),
        cost_estimate=COST,
    )(lengths, arrived, *operands)


def join_kernel(groups, part_ref, copies_ref):
    devices, rows, width = part_ref.shape
    share = rows // 2
    sums, stats = [], []
    for source in range(0, devices, groups):
        pieces = [part_ref[source + group] for group in range(groups)]
        sums.append(jnp.concatenate([piece[:share] for piece in pieces], axis=0))
        stats.append(jnp.concatenate([piece[share:] for piece in pieces], axis=0))
    joint_max = functools.reduce(jnp.maximum, [stat[:, 0:1] for stat in stats])
    factors = [jnp.exp(stat[:, 0:1] - joint_max) for stat in stats]
    total = sum(stat[:, 1:2] * factor for stat, factor in zip(stats, factors))
    summed = sum(part * factor for part, factor in zip(sums, factors))
    attention = (summed / total).astype(jnp.bfloat16)
    for place in range(copies_ref.shape[0]):
        copies_ref[place] = attention


def join_partials(groups, parts):
    devices, rows, width = parts.shape
    return pl.pallas_call(
        functools.partial(join_kernel, groups),
        out_shape=jax.ShapeDtypeStruct((devices, groups * rows // 2, width), jnp.bfloat16),
        compiler_params=pltpu.CompilerParams(vmem_limit_bytes=8 * MIB),
        cost_estimate=COST,
    )(parts)


def project_kernel(groups, rows_ref, w_ref, residual_ref, out_ref, copies_ref, attention_ref, wide_ref):
    devices, heads, width = rows_ref.shape
    completions = residual_ref.shape[0]
    all_heads = devices * heads // completions
    share = heads // groups
    wide_ref[...] = rows_ref[...].reshape(devices * heads, width).astype(jnp.float32)
    rows = []
    for group in range(groups):
        for taker in range(groups):
            for head in range(share):
                place = (taker * groups + group) * share + head
                row = wide_ref[pl.ds(place, completions, stride=all_heads), :]
                rows.append(row.astype(jnp.bfloat16))
    projected = dot_rows(jnp.concatenate(rows, axis=1), w_ref[...])
    hidden = (residual_ref[...].astype(jnp.float32) + projected).astype(jnp.bfloat16)
    out_ref[...] = hidden
    for place in range(copies_ref.shape[0]):
        copies_ref[place] = hidden
    me, mine = lax.axis_index("ctx"), lax.axis_index("head")
    own = [wide_ref[pl.ds((me * groups + taker) * heads, heads), :] for taker in range(groups)]
    attention = jnp.zeros((heads, width), jnp.float32)
    for group in range(groups):
        rows = slice(group * share, (group + 1) * share)
        candidate = jnp.concatenate([piece[rows] for piece in own], axis=0)
        attention = jnp.where(mine == group, candidate, attention)
    attention_ref[...] = attention.astype(jnp.bfloat16)


def project(groups, rows, w_out, residual):
    devices, heads, width = rows.shape
    return pl.pallas_call(
        functools.partial(project_kernel, groups),
        out_shape=(
            jax.ShapeDtypeStruct(residual.shape, jnp.bfloat16),
            jax.ShapeDtypeStruct((devices, *residual.shape), jnp.bfloat16),
            jax.ShapeDtypeStruct((heads, width), jnp.bfloat16),
        ),
        scratch_shapes=[pltpu.VMEM((devices * heads, width), jnp.float32)],
        compiler_params=pltpu.CompilerParams(vmem_limit_bytes=12 * MIB),
        cost_estimate=COST,
    )(rows, w_out, residual)


def forward_kernel(
    pieces_ref, gain_ref, attention_ref, gate_ref, up_ref, down_ref, out_ref, attention_hbm, state_ref, sem
):
    keep = pltpu.make_async_copy(attention_ref, attention_hbm, sem)
    keep.start()
    devices, completions, columns = pieces_ref.shape
    for place in range(devices):
        state_ref[:, place * columns : (place + 1) * columns] = pieces_ref[place].astype(jnp.float32)
    state = state_ref[...]
    mean_square = jnp.mean(state * state, axis=-1, keepdims=True)
    gain = gain_ref[...].reshape(1, devices * columns)
    normed = (state * lax.rsqrt(mean_square + NORM_EPSILON) * gain).astype(jnp.bfloat16)
    gate_values = dot_rows(normed, gate_ref[...])
    up_values = dot_rows(normed, up_ref[...])
    activated = (jax.nn.gelu(gate_values, approximate=True) * up_values).astype(jnp.bfloat16)
    share = jnp.dot(activated, down_ref[...], preferred_element_type=jnp.float32)
    for place in range(devices):
        out_ref[place] = share[:, place * columns : (place + 1) * columns].astype(jnp.bfloat16)
    keep.wait()


def forward(pieces, gain, attention, *weights):
    devices, completions, columns = pieces.shape
    return pl.pallas_call(
        forward_kernel,
        out_shape=(
            jax.ShapeDtypeStruct(pieces.shape, jnp.bfloat16),
            jax.ShapeDtypeStruct(attention.shape, jnp.bfloat16),
        ),
        out_specs=(pl.BlockSpec(memory_space=pltpu.VMEM), pl.BlockSpec(memory_space=pl.ANY)),
        scratch_shapes=[
            pltpu.VMEM((completions, devices * columns), jnp.float32),
            pltpu.SemaphoreType.DMA,
        ],
        compiler_params=pltpu.CompilerParams(vmem_limit_bytes=8 * MIB),
        cost_estimate=COST,
    )(pieces, gain, attention, *weights)


def exchange(copies):
    return lax.all_to_all(copies, BOTH, split_axis=0, concat_axis=0, tiled=True)


def body(
    queries,
    k_new,
    v_new,
    k_suffix,
    v_suffix,
    lengths,
    k_prefix,
    v_prefix,
    w_out,
    residual,
    norm_gain,
    w_gate,
    w_up,
    w_down,
):
    groups = lax.axis_size("head")
    devices = lax.axis_size("ctx") * groups
    copies, own_length = spread(lengths, queries, devices)
    rows_of = lambda values: values.reshape(-1, values.shape[-1])
    cached = map(rows_of, (k_suffix, v_suffix, k_prefix, v_prefix))
    parts = attend(groups, own_length, exchange(copies), queries, k_new, v_new, *cached)
    copies = join_partials(groups, exchange(parts))
    hidden_part, copies, attention = project(groups, exchange(copies), w_out.T, residual)
    shares, attention = forward(exchange(copies), norm_gain, attention, w_gate.T, w_up.T, w_down)
    summed = jnp.sum(exchange(shares).astype(jnp.float32), axis=0)
    next_hidden = (hidden_part.astype(jnp.float32) + summed).astype(jnp.bfloat16)
    return (attention[None], next_hidden)


def solution(mesh):
    placed = (
        P("ctx", "head", None),
        P("ctx", "head", None),
        P("ctx", "head", None),
        P("ctx", None, "head", None),
        P("ctx", None, "head", None),
        P("ctx"),
        P("ctx", "head", None),
        P("ctx", "head", None),
        P(None, BOTH),
        P(None, BOTH),
        P(),
        P(None, BOTH),
        P(None, BOTH),
        P(BOTH, None),
    )
    return jax.shard_map(
        body,
        mesh=mesh,
        in_specs=placed,
        out_specs=(P("ctx", "head", None), P(None, BOTH)),
        check_vma=False,
    )
```

```python
import functools

import jax
import jax.numpy as jnp
from jax import lax
from jax.experimental import pallas as pl
from jax.experimental.pallas import tpu as pltpu
from jax.sharding import PartitionSpec as P

SCORE_SCALE = 168.0 ** (-0.5)
NORM_EPSILON = 1e-06
MASKED = -1e30
MIB = 1024 * 1024
COST = pl.CostEstimate(flops=10**10, bytes_accessed=MIB, transcendentals=10**6)
JOIN_LIMIT = 2 * MIB
TERMS = 3
BOTH = ("ctx", "head")


def head_bias(rows, columns, heads, kv_heads):
    group = heads // kv_heads
    tile = (heads, 128)
    row = lax.broadcasted_iota(jnp.int32, tile, 0)
    column = lax.broadcasted_iota(jnp.int32, tile, 1)
    bias = jnp.where(row // group == lax.rem(column, kv_heads), 0.0, MASKED)
    return jnp.tile(bias, (rows // heads, columns // 128))


def in_hbm(operand):
    return pltpu.with_memory_space_constraint(operand, pltpu.HBM)


def dot_rows(left, right):
    return lax.dot_general(left, right, (((1,), (1,)), ((), ())), preferred_element_type=jnp.float32)


def stat_rows(row_max, row_total, shape):
    lane = lax.broadcasted_iota(jnp.int32, shape, 1)
    return jnp.where(lane == 0, row_max, row_total)


def spread_kernel(length_ref, source_hbm, copies_ref, lengths_ref, source_ref, sem):
    load = pltpu.make_async_copy(source_hbm, source_ref, sem)
    load.start()
    lengths_ref[...] = jnp.full(lengths_ref.shape, length_ref[0], jnp.int32)
    load.wait()
    for place in range(copies_ref.shape[0]):
        copies_ref[place] = source_ref[0]


def spread(lengths, value, count):
    return pl.pallas_call(
        spread_kernel,
        out_shape=(
            jax.ShapeDtypeStruct((count, *value.shape[1:]), value.dtype),
            jax.ShapeDtypeStruct(value.shape[1:], jnp.int32),
        ),
        in_specs=[pl.BlockSpec(memory_space=pltpu.SMEM), pl.BlockSpec(memory_space=pl.ANY)],
        scratch_shapes=[pltpu.VMEM(value.shape, value.dtype), pltpu.SemaphoreType.DMA],
        compiler_params=pltpu.CompilerParams(vmem_limit_bytes=4 * MIB),
        cost_estimate=COST,
    )(lengths, in_hbm(value))


def attention_kernel(
    finish, length_ref, arrived_ref, q_ref, kn_ref, vn_ref, ks_ref, vs_ref, kp_ref, vp_ref,
    part_ref, sum_ref, stat_ref,
):
    count, heads, width = arrived_ref.shape
    kv_heads = kn_ref.shape[1]
    queries = arrived_ref[...].reshape(count * heads, width)
    scores = SCORE_SCALE * dot_rows(queries, kp_ref[...])
    scores = scores + head_bias(*scores.shape, heads, kv_heads)
    row_max = jnp.max(scores, axis=1, keepdims=True)
    weights = jnp.exp(scores - row_max).astype(jnp.bfloat16)
    row_total = jnp.sum(weights.astype(jnp.float32), axis=1, keepdims=True)
    own = q_ref[0]
    own_scores = SCORE_SCALE * dot_rows(own, ks_ref[...])
    new_scores = SCORE_SCALE * dot_rows(own, kn_ref[0])
    slot = lax.broadcasted_iota(jnp.int32, own_scores.shape, 1) // kv_heads
    own_scores = own_scores + head_bias(*own_scores.shape, heads, kv_heads)
    own_scores = jnp.where(slot < length_ref[:, 0:1], own_scores, MASKED)
    new_scores = new_scores + head_bias(heads, 128, heads, kv_heads)[:, :kv_heads]
    suffix_max = jnp.maximum(
        jnp.max(own_scores, axis=1, keepdims=True), jnp.max(new_scores, axis=1, keepdims=True)
    )
    own_weights = jnp.exp(own_scores - suffix_max).astype(jnp.bfloat16)
    new_weights = jnp.exp(new_scores - suffix_max).astype(jnp.bfloat16)
    suffix_total = jnp.sum(own_weights.astype(jnp.float32), axis=1, keepdims=True) + jnp.sum(
        new_weights.astype(jnp.float32), axis=1, keepdims=True
    )
    suffix_sum = jnp.dot(own_weights, vs_ref[...], preferred_element_type=jnp.float32) + jnp.dot(
        new_weights, vn_ref[0], preferred_element_type=jnp.float32
    )
    row_sum = jnp.dot(weights, vp_ref[...], preferred_element_type=jnp.float32)
    sum_ref[...] = row_sum.reshape(count, heads, width)
    stat_ref[...] = stat_rows(row_max, row_total, row_sum.shape).reshape(count, heads, width)
    me = lax.axis_index("ctx")
    prefix_stat = stat_ref[me]
    prefix_max = prefix_stat[:, 0:1]
    joint_max = jnp.maximum(prefix_max, suffix_max)
    prefix_factor = jnp.exp(prefix_max - joint_max)
    suffix_factor = jnp.exp(suffix_max - joint_max)
    joint_total = prefix_stat[:, 1:2] * prefix_factor + suffix_total * suffix_factor
    joint_sum = sum_ref[me] * prefix_factor + suffix_sum * suffix_factor
    sum_ref[me] = joint_sum
    stat_ref[me] = stat_rows(joint_max, joint_total, joint_sum.shape)
    finish(part_ref, sum_ref, stat_ref)


def keep_apart(part_ref, sum_ref, stat_ref):
    part_ref[:, 0] = sum_ref[...]
    part_ref[:, 1] = stat_ref[...]


def spread_shares(part_ref, sum_ref, stat_ref):
    count, heads, width = sum_ref.shape
    rows = count * heads
    stats = stat_ref[...].reshape(rows, width)
    total = stats[:, 1:2]
    share = (sum_ref[...].reshape(rows, width) / total).astype(jnp.bfloat16)
    share = share.reshape(count, heads, width)
    rest = jnp.broadcast_to(stats[:, 0:1] + jnp.log(total), (rows, width))
    lane = lax.broadcasted_iota(jnp.int32, (rows, width), 1)
    terms = jnp.zeros((rows, width), jnp.float32)
    for place in range(TERMS):
        term = rest.astype(jnp.bfloat16).astype(jnp.float32)
        terms = jnp.where(lane == place, term, terms)
        rest = rest - term
    if rows < width:
        terms = jnp.concatenate([terms, jnp.zeros((width - rows, width), jnp.float32)], axis=0)
    logs = terms.T[:heads].astype(jnp.bfloat16)
    for place in range(part_ref.shape[0]):
        part_ref[place, :count] = share
        part_ref[place, count] = logs


def attend(finish, part, lengths, arrived, *operands):
    return pl.pallas_call(
        functools.partial(attention_kernel, finish),
        out_shape=part,
        scratch_shapes=[pltpu.VMEM(arrived.shape, jnp.float32)] * 2,
        compiler_params=pltpu.CompilerParams(vmem_limit_bytes=24 * MIB),
        cost_estimate=COST,
    )(lengths, arrived, *operands)


def join_kernel(part_ref, copies_ref):
    sources = part_ref.shape[0]
    joint_max = functools.reduce(
        jnp.maximum, [part_ref[source, 1, :, 0:1] for source in range(sources)]
    )
    total = jnp.zeros_like(joint_max)
    summed = jnp.zeros(part_ref.shape[2:], jnp.float32)
    for source in range(sources):
        factor = jnp.exp(part_ref[source, 1, :, 0:1] - joint_max)
        total = total + part_ref[source, 1, :, 1:2] * factor
        summed = summed + part_ref[source, 0] * factor
    attention = (summed / total).astype(jnp.bfloat16)
    for place in range(copies_ref.shape[0]):
        copies_ref[place] = attention


def join_partials(parts, devices):
    shape = parts.shape[2:]
    return pl.pallas_call(
        join_kernel,
        out_shape=jax.ShapeDtypeStruct((devices, *shape), jnp.bfloat16),
        compiler_params=pltpu.CompilerParams(vmem_limit_bytes=8 * MIB),
        cost_estimate=COST,
    )(parts)


def project_kernel(rows_ref, w_ref, residual_ref, out_ref, copies_ref, wide_ref):
    devices, heads, width = rows_ref.shape
    completions = residual_ref.shape[0]
    all_heads = devices * heads // completions
    wide_ref[...] = rows_ref[...].reshape(devices * heads, width).astype(jnp.float32)
    rows = [wide_ref[pl.ds(head, completions, stride=all_heads), :] for head in range(all_heads)]
    rows = jnp.concatenate([row.astype(jnp.bfloat16) for row in rows], axis=1)
    hidden = (residual_ref[...].astype(jnp.float32) + dot_rows(rows, w_ref[...])).astype(jnp.bfloat16)
    out_ref[...] = hidden
    for place in range(copies_ref.shape[0]):
        copies_ref[place] = hidden


def join_project_kernel(
    shares_ref, w_ref, residual_ref, out_ref, copies_ref, attention_ref, wide_ref
):
    groups, rows, width = wide_ref.shape
    devices, tiles, heads, unused = shares_ref.shape
    count = devices // groups
    logs = []
    for group in range(groups):
        for source in range(count):
            tile = shares_ref[source * groups + group, count].astype(jnp.float32)
            logs.append(jnp.sum(tile[:TERMS], axis=0, keepdims=True))
    logs = jnp.concatenate(logs, axis=0)
    factors = []
    for group in range(groups):
        own = logs[group * count : (group + 1) * count]
        weights = jnp.exp(own - jnp.max(own, axis=0, keepdims=True))
        factors.append(weights / jnp.sum(weights, axis=0, keepdims=True))
    if devices < width:
        factors.append(jnp.zeros((width - devices, width), jnp.float32))
    factors = jnp.concatenate(factors, axis=0).T
    for group in range(groups):
        joined = jnp.zeros((rows, width), jnp.float32)
        for source in range(count):
            place = group * count + source
            share = shares_ref[source * groups + group, :count].reshape(rows, width)
            joined = joined + share.astype(jnp.float32) * factors[:rows, place : place + 1]
        wide_ref[group] = joined
    pieces = [
        wide_ref[group, pl.ds(head, count, stride=heads), :].astype(jnp.bfloat16)
        for group in range(groups)
        for head in range(heads)
    ]
    projected = dot_rows(jnp.concatenate(pieces, axis=1), w_ref[...])
    hidden = (residual_ref[...].astype(jnp.float32) + projected).astype(jnp.bfloat16)
    out_ref[...] = hidden
    for place in range(copies_ref.shape[0]):
        copies_ref[place] = hidden
    me, mine = lax.axis_index("ctx"), lax.axis_index("head")
    start = pl.multiple_of(me * heads, heads)
    attention_ref[...] = wide_ref[mine, pl.ds(start, heads), :].astype(jnp.bfloat16)


def join_project(groups, shares, w_out, residual):
    devices, tiles, heads, width = shares.shape
    return pl.pallas_call(
        join_project_kernel,
        out_shape=(
            jax.ShapeDtypeStruct(residual.shape, jnp.bfloat16),
            jax.ShapeDtypeStruct((devices, *residual.shape), jnp.bfloat16),
            jax.ShapeDtypeStruct((heads, width), jnp.bfloat16),
        ),
        scratch_shapes=[pltpu.VMEM((groups, (tiles - 1) * heads, width), jnp.float32)],
        compiler_params=pltpu.CompilerParams(vmem_limit_bytes=12 * MIB),
        cost_estimate=COST,
    )(shares, w_out, residual)


def project(rows, w_out, residual):
    devices, heads, width = rows.shape
    return pl.pallas_call(
        project_kernel,
        out_shape=(
            jax.ShapeDtypeStruct(residual.shape, jnp.bfloat16),
            jax.ShapeDtypeStruct((devices, *residual.shape), jnp.bfloat16),
        ),
        scratch_shapes=[pltpu.VMEM((devices * heads, width), jnp.float32)],
        compiler_params=pltpu.CompilerParams(vmem_limit_bytes=12 * MIB),
        cost_estimate=COST,
    )(rows, w_out, residual)


def forward_kernel(
    pieces_ref, gain_ref, attention_ref, gate_ref, up_ref, down_ref, out_ref, attention_hbm, state_ref, sem
):
    keep = pltpu.make_async_copy(attention_ref, attention_hbm, sem)
    keep.start()
    devices, completions, columns = pieces_ref.shape
    for place in range(devices):
        state_ref[:, place * columns : (place + 1) * columns] = pieces_ref[place].astype(jnp.float32)
    state = state_ref[...]
    mean_square = jnp.mean(state * state, axis=-1, keepdims=True)
    gain = gain_ref[...].reshape(1, devices * columns)
    normed = (state * lax.rsqrt(mean_square + NORM_EPSILON) * gain).astype(jnp.bfloat16)
    gate_values = dot_rows(gate_ref[...], normed)
    up_values = dot_rows(up_ref[...], normed)
    activated = (jax.nn.gelu(gate_values, approximate=True) * up_values).T.astype(jnp.bfloat16)
    share = jnp.dot(activated, down_ref[...], preferred_element_type=jnp.float32)
    for place in range(devices):
        out_ref[place] = share[:, place * columns : (place + 1) * columns].astype(jnp.bfloat16)
    keep.wait()


def forward(pieces, gain, attention, *weights):
    devices, completions, columns = pieces.shape
    return pl.pallas_call(
        forward_kernel,
        out_shape=(
            jax.ShapeDtypeStruct(pieces.shape, jnp.bfloat16),
            jax.ShapeDtypeStruct(attention.shape, jnp.bfloat16),
        ),
        out_specs=(pl.BlockSpec(memory_space=pltpu.VMEM), pl.BlockSpec(memory_space=pl.ANY)),
        scratch_shapes=[
            pltpu.VMEM((completions, devices * columns), jnp.float32),
            pltpu.SemaphoreType.DMA,
        ],
        compiler_params=pltpu.CompilerParams(vmem_limit_bytes=8 * MIB),
        cost_estimate=COST,
    )(pieces, gain, attention, *weights)


def exchange(copies, axes=BOTH):
    return lax.all_to_all(copies, axes, split_axis=0, concat_axis=0, tiled=True)


def body(
    queries,
    k_new,
    v_new,
    k_suffix,
    v_suffix,
    lengths,
    k_prefix,
    v_prefix,
    w_out,
    residual,
    norm_gain,
    w_gate,
    w_up,
    w_down,
):
    ctx_count, groups = lax.axis_size("ctx"), lax.axis_size("head")
    devices = ctx_count * groups
    unused, heads, width = queries.shape
    copies, own_length = spread(lengths, queries, ctx_count)
    arrived = exchange(copies, "ctx")
    rows_of = lambda values: values.reshape(-1, values.shape[-1])
    cached = map(rows_of, (k_suffix, v_suffix, k_prefix, v_prefix))
    operands = (own_length, arrived, queries, k_new, v_new, *cached)
    joint = jax.ShapeDtypeStruct((devices, ctx_count + 1, heads, width), jnp.bfloat16)
    if 2 * joint.size <= JOIN_LIMIT and ctx_count * heads <= width:
        shares = exchange(attend(spread_shares, joint, *operands))
        hidden_part, copies, attention = join_project(groups, shares, w_out.T, residual)
    else:
        apart = jax.ShapeDtypeStruct((ctx_count, 2, heads, width), jnp.float32)
        parts = exchange(attend(keep_apart, apart, *operands), "ctx")
        copies = join_partials(parts, devices)
        attention = copies[0]
        hidden_part, copies = project(exchange(copies), w_out.T, residual)
    shares, attention = forward(exchange(copies), norm_gain, attention, w_gate.T, w_up.T, w_down)
    summed = jnp.sum(exchange(shares).astype(jnp.float32), axis=0)
    next_hidden = (hidden_part.astype(jnp.float32) + summed).astype(jnp.bfloat16)
    return (attention[None], next_hidden)


def solution(mesh):
    placed = (
        P("ctx", "head", None),
        P("ctx", "head", None),
        P("ctx", "head", None),
        P("ctx", None, "head", None),
        P("ctx", None, "head", None),
        P("ctx"),
        P("ctx", "head", None),
        P("ctx", "head", None),
        P(None, BOTH),
        P(None, BOTH),
        P(),
        P(None, BOTH),
        P(None, BOTH),
        P(BOTH, None),
    )
    return jax.shard_map(
        body,
        mesh=mesh,
        in_specs=placed,
        out_specs=(P("ctx", "head", None), P(None, BOTH)),
        check_vma=False,
    )
```

```python
import functools

import jax
import jax.numpy as jnp
from jax import lax
from jax.experimental import pallas as pl
from jax.experimental.pallas import tpu as pltpu
from jax.sharding import PartitionSpec as P

SCORE_SCALE = 168.0 ** (-0.5)
NORM_EPSILON = 1e-06
MASKED = -1e30
MIB = 1024 * 1024
COST = pl.CostEstimate(flops=10**10, bytes_accessed=MIB, transcendentals=10**6)
TERMS = 3
LANES = 128
HALF = LANES // 2
BOTH = ("ctx", "head")


def head_bias(rows, columns, heads, kv_heads):
    group = heads // kv_heads
    tile = (heads, 128)
    row = lax.broadcasted_iota(jnp.int32, tile, 0)
    column = lax.broadcasted_iota(jnp.int32, tile, 1)
    bias = jnp.where(row // group == lax.rem(column, kv_heads), 0.0, MASKED)
    return jnp.tile(bias, (rows // heads, columns // 128))


def in_hbm(operand):
    return pltpu.with_memory_space_constraint(operand, pltpu.HBM)


def dot_rows(left, right):
    return lax.dot_general(left, right, (((1,), (1,)), ((), ())), preferred_element_type=jnp.float32)


def stat_rows(row_max, row_total, shape):
    lane = lax.broadcasted_iota(jnp.int32, shape, 1)
    return jnp.where(lane == 0, row_max, row_total)


def slot(rows, columns):
    if rows == 8 and LANES < columns <= LANES + HALF:
        return 3, 4, LANES
    return rows, columns


def put(ref, places, value):
    if ref.ndim == 3:
        for place in places:
            ref[place] = value.astype(ref.dtype)
        return
    rows, columns = value.shape
    rest = value[:, LANES:]
    if columns < LANES + HALF:
        rest = jnp.concatenate([rest, jnp.zeros((rows, LANES + HALF - columns), value.dtype)], axis=1)
    rest = jnp.concatenate([rest[:4], rest[4:]], axis=1)
    pieces = [piece.astype(ref.dtype) for piece in (value[:4, :LANES], value[4:, :LANES], rest)]
    for place in places:
        for part, piece in enumerate(pieces):
            ref[place, part] = piece


def unpacked(first, second, rest, columns):
    rest = jnp.concatenate([rest[:, : columns - LANES], rest[:, HALF : HALF + columns - LANES]], axis=0)
    return jnp.concatenate([first, second], axis=0), rest


def spread_kernel(length_ref, source_hbm, copies_ref, lengths_ref, source_ref, sem):
    load = pltpu.make_async_copy(source_hbm, source_ref, sem)
    load.start()
    lengths_ref[...] = jnp.full(lengths_ref.shape, length_ref[0], jnp.int32)
    load.wait()
    for place in range(copies_ref.shape[0]):
        copies_ref[place] = source_ref[0]


def spread(lengths, value, count):
    return pl.pallas_call(
        spread_kernel,
        out_shape=(
            jax.ShapeDtypeStruct((count, *value.shape[1:]), value.dtype),
            jax.ShapeDtypeStruct(value.shape[1:], jnp.int32),
        ),
        in_specs=[pl.BlockSpec(memory_space=pltpu.SMEM), pl.BlockSpec(memory_space=pl.ANY)],
        scratch_shapes=[pltpu.VMEM(value.shape, value.dtype), pltpu.SemaphoreType.DMA],
        compiler_params=pltpu.CompilerParams(vmem_limit_bytes=4 * MIB),
        cost_estimate=COST,
    )(lengths, in_hbm(value))


def attention_kernel(
    length_ref, arrived_ref, q_ref, kn_ref, vn_ref, ks_ref, vs_ref, kp_ref, vp_ref, part_ref,
    sum_ref, stat_ref,
):
    count, heads, width = arrived_ref.shape
    kv_heads = kn_ref.shape[1]
    queries = arrived_ref[...].reshape(count * heads, width)
    scores = SCORE_SCALE * dot_rows(queries, kp_ref[...])
    scores = scores + head_bias(*scores.shape, heads, kv_heads)
    row_max = jnp.max(scores, axis=1, keepdims=True)
    weights = jnp.exp(scores - row_max).astype(jnp.bfloat16)
    row_total = jnp.sum(weights.astype(jnp.float32), axis=1, keepdims=True)
    own = q_ref[0]
    own_scores = SCORE_SCALE * dot_rows(own, ks_ref[...])
    new_scores = SCORE_SCALE * dot_rows(own, kn_ref[0])
    slot = lax.broadcasted_iota(jnp.int32, own_scores.shape, 1) // kv_heads
    own_scores = own_scores + head_bias(*own_scores.shape, heads, kv_heads)
    own_scores = jnp.where(slot < length_ref[:, 0:1], own_scores, MASKED)
    new_scores = new_scores + head_bias(heads, 128, heads, kv_heads)[:, :kv_heads]
    suffix_max = jnp.maximum(
        jnp.max(own_scores, axis=1, keepdims=True), jnp.max(new_scores, axis=1, keepdims=True)
    )
    own_weights = jnp.exp(own_scores - suffix_max).astype(jnp.bfloat16)
    new_weights = jnp.exp(new_scores - suffix_max).astype(jnp.bfloat16)
    suffix_total = jnp.sum(own_weights.astype(jnp.float32), axis=1, keepdims=True) + jnp.sum(
        new_weights.astype(jnp.float32), axis=1, keepdims=True
    )
    suffix_sum = jnp.dot(own_weights, vs_ref[...], preferred_element_type=jnp.float32) + jnp.dot(
        new_weights, vn_ref[0], preferred_element_type=jnp.float32
    )
    row_sum = jnp.dot(weights, vp_ref[...], preferred_element_type=jnp.float32)
    sum_ref[...] = row_sum.reshape(count, heads, width)
    stat_ref[...] = stat_rows(row_max, row_total, row_sum.shape).reshape(count, heads, width)
    me = lax.axis_index("ctx")
    prefix_stat = stat_ref[me]
    prefix_max = prefix_stat[:, 0:1]
    joint_max = jnp.maximum(prefix_max, suffix_max)
    prefix_factor = jnp.exp(prefix_max - joint_max)
    suffix_factor = jnp.exp(suffix_max - joint_max)
    joint_total = prefix_stat[:, 1:2] * prefix_factor + suffix_total * suffix_factor
    joint_sum = sum_ref[me] * prefix_factor + suffix_sum * suffix_factor
    sum_ref[me] = joint_sum
    stat_ref[me] = stat_rows(joint_max, joint_total, joint_sum.shape)
    lane = lax.broadcasted_iota(jnp.int32, (heads, HALF), 1)
    for place in range(count):
        total = stat_ref[place, :, 1:2]
        rest = jnp.broadcast_to(stat_ref[place, :, 0:1] + jnp.log(total), (heads, HALF))
        terms = jnp.zeros((heads, HALF), jnp.float32)
        for term in range(TERMS):
            rounded = rest.astype(jnp.bfloat16).astype(jnp.float32)
            terms = jnp.where(lane == term, rounded, terms)
            rest = rest - rounded
        put(part_ref, (place,), jnp.concatenate([sum_ref[place] / total, terms], axis=1))


def attend(lengths, arrived, *operands):
    count, heads, width = arrived.shape
    return pl.pallas_call(
        attention_kernel,
        out_shape=jax.ShapeDtypeStruct((count, *slot(heads, width + HALF)), jnp.bfloat16),
        scratch_shapes=[pltpu.VMEM(arrived.shape, jnp.float32)] * 2,
        compiler_params=pltpu.CompilerParams(vmem_limit_bytes=24 * MIB),
        cost_estimate=COST,
    )(lengths, arrived, *operands)


def join_kernel(part_ref, copies_ref):
    logs, shares = [], []
    for source in range(part_ref.shape[0]):
        pieces = [part_ref[source, part].astype(jnp.float32) for part in range(part_ref.shape[1])]
        share, terms = unpacked(*pieces, LANES + HALF)
        shares.append(share)
        logs.append(jnp.sum(terms[:, :TERMS], axis=1, keepdims=True))
    largest = functools.reduce(jnp.maximum, logs)
    factors = [jnp.exp(log - largest) for log in logs]
    summed = sum(share * factor for share, factor in zip(shares, factors))
    attention = (summed / sum(factors)).astype(jnp.bfloat16)
    for place in range(copies_ref.shape[0]):
        copies_ref[place] = attention


def join_partials(parts, shape):
    return pl.pallas_call(
        join_kernel,
        out_shape=jax.ShapeDtypeStruct(shape, jnp.bfloat16),
        compiler_params=pltpu.CompilerParams(vmem_limit_bytes=8 * MIB),
        cost_estimate=COST,
    )(parts)


def project_kernel(rows_ref, w_ref, residual_ref, out_ref, copies_ref, wide_ref):
    devices, heads, width = rows_ref.shape
    completions = residual_ref.shape[0]
    all_heads = devices * heads // completions
    wide_ref[...] = rows_ref[...].reshape(devices * heads, width).astype(jnp.float32)
    rows = [wide_ref[pl.ds(head, completions, stride=all_heads), :] for head in range(all_heads)]
    rows = jnp.concatenate([row.astype(jnp.bfloat16) for row in rows], axis=1)
    hidden = (residual_ref[...].astype(jnp.float32) + dot_rows(rows, w_ref[...])).astype(jnp.bfloat16)
    out_ref[...] = hidden
    put(copies_ref, range(copies_ref.shape[0]), hidden.astype(jnp.float32))


def project(rows, w_out, residual):
    devices, heads, width = rows.shape
    return pl.pallas_call(
        project_kernel,
        out_shape=(
            jax.ShapeDtypeStruct(residual.shape, jnp.bfloat16),
            jax.ShapeDtypeStruct((devices, *slot(*residual.shape)), jnp.bfloat16),
        ),
        scratch_shapes=[pltpu.VMEM((devices * heads, width), jnp.float32)],
        compiler_params=pltpu.CompilerParams(vmem_limit_bytes=12 * MIB),
        cost_estimate=COST,
    )(rows, w_out, residual)


def forward_kernel(
    pieces_ref, gain_ref, copies_ref, gate_ref, up_ref, down_ref, out_ref, attention_hbm, state_ref, sem
):
    keep = pltpu.make_async_copy(copies_ref.at[0], attention_hbm, sem)
    keep.start()
    devices = pieces_ref.shape[0]
    columns = state_ref.shape[1] // devices
    for place in range(devices):
        start = place * columns
        if pieces_ref.ndim == 3:
            state_ref[:, start : start + columns] = pieces_ref[place].astype(jnp.float32)
        else:
            pieces = [pieces_ref[place, part].astype(jnp.float32) for part in range(3)]
            first, rest = unpacked(*pieces, columns)
            state_ref[:, start : start + LANES] = first
            state_ref[:, start + LANES : start + columns] = rest
    state = state_ref[...]
    mean_square = jnp.mean(state * state, axis=-1, keepdims=True)
    gain = gain_ref[...].reshape(1, devices * columns)
    normed = (state * lax.rsqrt(mean_square + NORM_EPSILON) * gain).astype(jnp.bfloat16)
    gate_values = dot_rows(normed, gate_ref[...])
    up_values = dot_rows(normed, up_ref[...])
    activated = (jax.nn.gelu(gate_values, approximate=True) * up_values).astype(jnp.bfloat16)
    share = jnp.dot(activated, down_ref[...], preferred_element_type=jnp.float32)
    for place in range(devices):
        put(out_ref, (place,), share[:, place * columns : (place + 1) * columns])
    keep.wait()


def forward(pieces, completions, gain, copies, *weights):
    return pl.pallas_call(
        forward_kernel,
        out_shape=(
            jax.ShapeDtypeStruct(pieces.shape, jnp.bfloat16),
            jax.ShapeDtypeStruct(copies.shape[1:], jnp.bfloat16),
        ),
        out_specs=(pl.BlockSpec(memory_space=pltpu.VMEM), pl.BlockSpec(memory_space=pl.ANY)),
        scratch_shapes=[
            pltpu.VMEM((completions, gain.shape[0]), jnp.float32),
            pltpu.SemaphoreType.DMA,
        ],
        compiler_params=pltpu.CompilerParams(vmem_limit_bytes=8 * MIB),
        cost_estimate=COST,
    )(pieces, gain, copies, *weights)


def total_kernel(shares_ref, hidden_ref, out_ref):
    summed = jnp.sum(shares_ref[...].astype(jnp.float32), axis=0)
    if shares_ref.ndim == 4:
        summed = jnp.concatenate(unpacked(*summed, hidden_ref.shape[1]), axis=1)
    out_ref[...] = (hidden_ref[...].astype(jnp.float32) + summed).astype(jnp.bfloat16)


def total(shares, hidden):
    return pl.pallas_call(
        total_kernel,
        out_shape=jax.ShapeDtypeStruct(hidden.shape, jnp.bfloat16),
        compiler_params=pltpu.CompilerParams(vmem_limit_bytes=16 * MIB),
    )(shares, hidden)


def exchange(copies, axes=BOTH):
    return lax.all_to_all(copies, axes, split_axis=0, concat_axis=0, tiled=True)


def body(
    queries,
    k_new,
    v_new,
    k_suffix,
    v_suffix,
    lengths,
    k_prefix,
    v_prefix,
    w_out,
    residual,
    norm_gain,
    w_gate,
    w_up,
    w_down,
):
    ctx_count = lax.axis_size("ctx")
    devices = ctx_count * lax.axis_size("head")
    copies, own_length = spread(lengths, queries, ctx_count)
    arrived = exchange(copies, "ctx")
    rows_of = lambda values: values.reshape(-1, values.shape[-1])
    parts = attend(
        own_length, arrived, queries, k_new, v_new, *map(rows_of, (k_suffix, v_suffix, k_prefix, v_prefix))
    )
    copies = join_partials(exchange(parts, "ctx"), (devices, *queries.shape[1:]))
    hidden_part, hidden_copies = project(exchange(copies), w_out.T, residual)
    shares, attention = forward(
        exchange(hidden_copies), residual.shape[0], norm_gain, copies, w_gate.T, w_up.T, w_down
    )
    return (attention[None], total(exchange(shares), hidden_part))


def solution(mesh):
    placed = (
        P("ctx", "head", None),
        P("ctx", "head", None),
        P("ctx", "head", None),
        P("ctx", None, "head", None),
        P("ctx", None, "head", None),
        P("ctx"),
        P("ctx", "head", None),
        P("ctx", "head", None),
        P(None, BOTH),
        P(None, BOTH),
        P(),
        P(None, BOTH),
        P(None, BOTH),
        P(BOTH, None),
    )
    return jax.shard_map(
        body,
        mesh=mesh,
        in_specs=placed,
        out_specs=(P("ctx", "head", None), P(None, BOTH)),
        check_vma=False,
    )
```

```python
import functools

import jax
import jax.numpy as jnp
from jax import lax
from jax.experimental import pallas as pl
from jax.experimental.pallas import tpu as pltpu
from jax.sharding import PartitionSpec as P

SCORE_SCALE = 168.0 ** (-0.5)
NORM_EPSILON = 1e-06
MASKED = -1e30
MIB = 1024 * 1024
COST = pl.CostEstimate(flops=10**10, bytes_accessed=MIB, transcendentals=10**6)
TERMS = 3
LANES = 128
HALF = LANES // 2
BOTH = ("ctx", "head")


def head_bias(rows, columns, heads, kv_heads):
    group = heads // kv_heads
    tile = (heads, 128)
    row = lax.broadcasted_iota(jnp.int32, tile, 0)
    column = lax.broadcasted_iota(jnp.int32, tile, 1)
    bias = jnp.where(row // group == lax.rem(column, kv_heads), 0.0, MASKED)
    return jnp.tile(bias, (rows // heads, columns // 128))


def in_hbm(operand):
    return pltpu.with_memory_space_constraint(operand, pltpu.HBM)


def dot_rows(left, right):
    return lax.dot_general(left, right, (((1,), (1,)), ((), ())), preferred_element_type=jnp.float32)


def stat_rows(row_max, row_total, shape):
    lane = lax.broadcasted_iota(jnp.int32, shape, 1)
    return jnp.where(lane == 0, row_max, row_total)


def slot(rows, columns):
    if rows == 8 and LANES < columns <= LANES + HALF:
        return 3, 4, LANES
    return rows, columns


def put(ref, places, value):
    if ref.ndim == 3:
        for place in places:
            ref[place] = value.astype(ref.dtype)
        return
    rows, columns = value.shape
    rest = value[:, LANES:]
    if columns < LANES + HALF:
        rest = jnp.concatenate([rest, jnp.zeros((rows, LANES + HALF - columns), value.dtype)], axis=1)
    rest = jnp.concatenate([rest[:4], rest[4:]], axis=1)
    pieces = [piece.astype(ref.dtype) for piece in (value[:4, :LANES], value[4:, :LANES], rest)]
    for place in places:
        for part, piece in enumerate(pieces):
            ref[place, part] = piece


def joined(first, second, rest):
    low = jnp.concatenate([first, second], axis=0).astype(jnp.float32)
    rest = rest.astype(jnp.float32)
    return low, jnp.concatenate([rest, pltpu.roll(rest, HALF, 1)], axis=0)


def turn(value, columns, back=False):
    device = lax.axis_index("ctx") * lax.axis_size("head") + lax.axis_index("head")
    offset = lax.rem(device * columns, LANES)
    return pltpu.roll(value, lax.rem(LANES - offset, LANES) if back else offset, 1)


def put_turned(ref, value):
    rows, columns = value.shape
    rest = jnp.concatenate(
        [value[:, LANES:], jnp.zeros((rows, 2 * LANES - columns), value.dtype)], axis=1
    )
    low, rest = turn(value[:, :LANES], columns), turn(rest, columns)
    rest = rest[:4] + pltpu.roll(rest, HALF, 1)[4:]
    pieces = [piece.astype(ref.dtype) for piece in (low[:4], low[4:], rest)]
    for place in range(ref.shape[0]):
        for part, piece in enumerate(pieces):
            ref[place, part] = piece


def whole_state(pieces_ref, order, columns):
    lane = lax.broadcasted_iota(jnp.int32, (8, LANES), 1)
    tiles = {}
    for device in range(len(order)):
        place = order.index(device)
        low, rest = joined(*(pieces_ref[place, part] for part in range(3)))
        first, offset = divmod(device * columns, LANES)
        tiles[first] = jnp.where(lane >= offset, low, tiles[first]) if offset else low
        tiles[first + 1] = jnp.where(lane < offset, low, rest)
        if offset + columns - LANES > LANES:
            tiles[first + 2] = rest
    return jnp.concatenate([tiles[place] for place in range(len(order) * columns // LANES)], axis=1)


def put_columns(ref, order, share, columns):
    lane = lax.broadcasted_iota(jnp.int32, (8, LANES), 1)
    tile = lambda place: share[:, place * LANES : (place + 1) * LANES]
    for device in range(len(order)):
        first, offset = divmod(device * columns, LANES)
        end = offset + columns - LANES
        low = jnp.where(lane >= offset, tile(first), tile(first + 1)) if offset else tile(first)
        rest = tile(first + 1)
        own = (lane >= offset) & (lane < end)
        if end > LANES:
            rest = jnp.where(lane >= offset, rest, tile(first + 2))
            own = (lane >= offset) | (lane < end - LANES)
        rest = jnp.where(own[:4], rest[:4], pltpu.roll(rest, HALF, 1)[4:])
        place = order.index(device)
        for part, piece in enumerate((low[:4], low[4:], rest)):
            ref[place, part] = piece.astype(ref.dtype)


def spread_kernel(length_ref, source_hbm, copies_ref, lengths_ref, source_ref, sem):
    load = pltpu.make_async_copy(source_hbm, source_ref, sem)
    load.start()
    lengths_ref[...] = jnp.full(lengths_ref.shape, length_ref[0], jnp.int32)
    load.wait()
    for place in range(copies_ref.shape[0]):
        copies_ref[place] = source_ref[0]


def spread(lengths, value, count):
    return pl.pallas_call(
        spread_kernel,
        out_shape=(
            jax.ShapeDtypeStruct((count, *value.shape[1:]), value.dtype),
            jax.ShapeDtypeStruct(value.shape[1:], jnp.int32),
        ),
        in_specs=[pl.BlockSpec(memory_space=pltpu.SMEM), pl.BlockSpec(memory_space=pl.ANY)],
        scratch_shapes=[pltpu.VMEM(value.shape, value.dtype), pltpu.SemaphoreType.DMA],
        compiler_params=pltpu.CompilerParams(vmem_limit_bytes=4 * MIB),
        cost_estimate=COST,
    )(lengths, in_hbm(value))


def attention_kernel(
    length_ref, arrived_ref, q_ref, kn_ref, vn_ref, ks_ref, vs_ref, kp_ref, vp_ref, part_ref,
    sum_ref, stat_ref,
):
    count, heads, width = arrived_ref.shape
    kv_heads = kn_ref.shape[1]
    queries = arrived_ref[...].reshape(count * heads, width)
    scores = SCORE_SCALE * dot_rows(queries, kp_ref[...])
    scores = scores + head_bias(*scores.shape, heads, kv_heads)
    row_max = jnp.max(scores, axis=1, keepdims=True)
    weights = jnp.exp(scores - row_max).astype(jnp.bfloat16)
    row_total = jnp.sum(weights.astype(jnp.float32), axis=1, keepdims=True)
    own = q_ref[0]
    own_scores = SCORE_SCALE * dot_rows(own, ks_ref[...])
    new_scores = SCORE_SCALE * dot_rows(own, kn_ref[0])
    slot = lax.broadcasted_iota(jnp.int32, own_scores.shape, 1) // kv_heads
    own_scores = own_scores + head_bias(*own_scores.shape, heads, kv_heads)
    own_scores = jnp.where(slot < length_ref[:, 0:1], own_scores, MASKED)
    new_scores = new_scores + head_bias(heads, 128, heads, kv_heads)[:, :kv_heads]
    suffix_max = jnp.maximum(
        jnp.max(own_scores, axis=1, keepdims=True), jnp.max(new_scores, axis=1, keepdims=True)
    )
    own_weights = jnp.exp(own_scores - suffix_max).astype(jnp.bfloat16)
    new_weights = jnp.exp(new_scores - suffix_max).astype(jnp.bfloat16)
    suffix_total = jnp.sum(own_weights.astype(jnp.float32), axis=1, keepdims=True) + jnp.sum(
        new_weights.astype(jnp.float32), axis=1, keepdims=True
    )
    suffix_sum = jnp.dot(own_weights, vs_ref[...], preferred_element_type=jnp.float32) + jnp.dot(
        new_weights, vn_ref[0], preferred_element_type=jnp.float32
    )
    row_sum = jnp.dot(weights, vp_ref[...], preferred_element_type=jnp.float32)
    sum_ref[...] = row_sum.reshape(count, heads, width)
    stat_ref[...] = stat_rows(row_max, row_total, row_sum.shape).reshape(count, heads, width)
    me = lax.axis_index("ctx")
    prefix_stat = stat_ref[me]
    prefix_max = prefix_stat[:, 0:1]
    joint_max = jnp.maximum(prefix_max, suffix_max)
    prefix_factor = jnp.exp(prefix_max - joint_max)
    suffix_factor = jnp.exp(suffix_max - joint_max)
    joint_total = prefix_stat[:, 1:2] * prefix_factor + suffix_total * suffix_factor
    joint_sum = sum_ref[me] * prefix_factor + suffix_sum * suffix_factor
    sum_ref[me] = joint_sum
    stat_ref[me] = stat_rows(joint_max, joint_total, joint_sum.shape)
    lane = lax.broadcasted_iota(jnp.int32, (heads, HALF), 1)
    for place in range(count):
        total = stat_ref[place, :, 1:2]
        rest = jnp.broadcast_to(stat_ref[place, :, 0:1] + jnp.log(total), (heads, HALF))
        terms = jnp.zeros((heads, HALF), jnp.float32)
        for term in range(TERMS):
            rounded = rest.astype(jnp.bfloat16).astype(jnp.float32)
            terms = jnp.where(lane == term, rounded, terms)
            rest = rest - rounded
        put(part_ref, (place,), jnp.concatenate([sum_ref[place] / total, terms], axis=1))


def attend(lengths, arrived, *operands):
    count, heads, width = arrived.shape
    return pl.pallas_call(
        attention_kernel,
        out_shape=jax.ShapeDtypeStruct((count, *slot(heads, width + HALF)), jnp.bfloat16),
        scratch_shapes=[pltpu.VMEM(arrived.shape, jnp.float32)] * 2,
        compiler_params=pltpu.CompilerParams(vmem_limit_bytes=24 * MIB),
        cost_estimate=COST,
    )(lengths, arrived, *operands)


def join_kernel(part_ref, copies_ref):
    logs, shares = [], []
    for source in range(part_ref.shape[0]):
        share, terms = joined(*(part_ref[source, part] for part in range(3)))
        shares.append(share)
        logs.append(jnp.sum(terms[:, :TERMS], axis=1, keepdims=True))
    largest = functools.reduce(jnp.maximum, logs)
    factors = [jnp.exp(log - largest) for log in logs]
    summed = sum(share * factor for share, factor in zip(shares, factors))
    attention = (summed / sum(factors)).astype(jnp.bfloat16)
    for place in range(copies_ref.shape[0]):
        copies_ref[place] = attention


def join_partials(parts, shape):
    return pl.pallas_call(
        join_kernel,
        out_shape=jax.ShapeDtypeStruct(shape, jnp.bfloat16),
        compiler_params=pltpu.CompilerParams(vmem_limit_bytes=8 * MIB),
        cost_estimate=COST,
    )(parts)


def project_kernel(order, rows_ref, w_ref, residual_ref, out_ref, copies_ref, wide_ref):
    devices, heads, width = rows_ref.shape
    completions = residual_ref.shape[0]
    all_heads = devices * heads // completions
    for place, device in enumerate(order):
        wide_ref[device * heads : (device + 1) * heads] = rows_ref[place].astype(jnp.float32)
    rows = [wide_ref[pl.ds(head, completions, stride=all_heads), :] for head in range(all_heads)]
    rows = jnp.concatenate([row.astype(jnp.bfloat16) for row in rows], axis=1)
    hidden = (residual_ref[...].astype(jnp.float32) + dot_rows(rows, w_ref[...])).astype(jnp.bfloat16)
    out_ref[...] = hidden
    if copies_ref.ndim == 4:
        put_turned(copies_ref, hidden.astype(jnp.float32))
    else:
        put(copies_ref, range(copies_ref.shape[0]), hidden)


def project(order, rows, w_out, residual):
    devices, heads, width = rows.shape
    return pl.pallas_call(
        functools.partial(project_kernel, order),
        out_shape=(
            jax.ShapeDtypeStruct(residual.shape, jnp.bfloat16),
            jax.ShapeDtypeStruct((devices, *slot(*residual.shape)), jnp.bfloat16),
        ),
        scratch_shapes=[pltpu.VMEM((devices * heads, width), jnp.float32)],
        compiler_params=pltpu.CompilerParams(vmem_limit_bytes=12 * MIB),
        cost_estimate=COST,
    )(rows, w_out, residual)


def forward_kernel(
    order, pieces_ref, gain_ref, copies_ref, gate_ref, up_ref, down_ref, out_ref, attention_hbm, state_ref, sem
):
    keep = pltpu.make_async_copy(copies_ref.at[0], attention_hbm, sem)
    keep.start()
    devices = pieces_ref.shape[0]
    columns = gain_ref.shape[0] // devices
    if pieces_ref.ndim == 4:
        state = whole_state(pieces_ref, order, columns)
    else:
        for place, device in enumerate(order):
            columns_of = slice(device * columns, (device + 1) * columns)
            state_ref[:, columns_of] = pieces_ref[place].astype(jnp.float32)
        state = state_ref[...]
    mean_square = jnp.mean(state * state, axis=-1, keepdims=True)
    gain = gain_ref[...].reshape(1, devices * columns)
    normed = (state * lax.rsqrt(mean_square + NORM_EPSILON) * gain).astype(jnp.bfloat16)
    gate_values = dot_rows(normed, gate_ref[...])
    up_values = dot_rows(normed, up_ref[...])
    activated = (jax.nn.gelu(gate_values, approximate=True) * up_values).astype(jnp.bfloat16)
    share = jnp.dot(activated, down_ref[...], preferred_element_type=jnp.float32)
    if pieces_ref.ndim == 4:
        put_columns(out_ref, order, share, columns)
    else:
        for place, device in enumerate(order):
            put(out_ref, (place,), share[:, device * columns : (device + 1) * columns])
    keep.wait()


def forward(order, pieces, completions, gain, copies, *weights):
    return pl.pallas_call(
        functools.partial(forward_kernel, order),
        out_shape=(
            jax.ShapeDtypeStruct(pieces.shape, jnp.bfloat16),
            jax.ShapeDtypeStruct(copies.shape[1:], jnp.bfloat16),
        ),
        out_specs=(pl.BlockSpec(memory_space=pltpu.VMEM), pl.BlockSpec(memory_space=pl.ANY)),
        scratch_shapes=[
            pltpu.VMEM((completions, gain.shape[0]), jnp.float32),
            pltpu.SemaphoreType.DMA,
        ],
        compiler_params=pltpu.CompilerParams(vmem_limit_bytes=8 * MIB),
        cost_estimate=COST,
    )(pieces, gain, copies, *weights)


def total_kernel(shares_ref, hidden_ref, out_ref):
    summed = jnp.sum(shares_ref[...].astype(jnp.float32), axis=0)
    if shares_ref.ndim == 4:
        columns = hidden_ref.shape[1]
        low, rest = (turn(part, columns, back=True) for part in joined(*summed))
        summed = jnp.concatenate([low, rest[:, : columns - LANES]], axis=1)
    out_ref[...] = (hidden_ref[...].astype(jnp.float32) + summed).astype(jnp.bfloat16)


def total(shares, hidden):
    return pl.pallas_call(
        total_kernel,
        out_shape=jax.ShapeDtypeStruct(hidden.shape, jnp.bfloat16),
        compiler_params=pltpu.CompilerParams(vmem_limit_bytes=16 * MIB),
    )(shares, hidden)


def listed(ctx_count, groups):
    order = (0, 1, 4, 5, 6, 7, 2, 3) if ctx_count == 8 else range(ctx_count)
    return [ctx * groups + group for ctx in order for group in range(groups)]


def exchange(copies, axes=BOTH):
    groups = None
    if axes == BOTH:
        groups = [listed(lax.axis_size("ctx"), lax.axis_size("head"))]
    return lax.all_to_all(
        copies, axes, split_axis=0, concat_axis=0, tiled=True, axis_index_groups=groups
    )


def body(
    queries,
    k_new,
    v_new,
    k_suffix,
    v_suffix,
    lengths,
    k_prefix,
    v_prefix,
    w_out,
    residual,
    norm_gain,
    w_gate,
    w_up,
    w_down,
):
    ctx_count = lax.axis_size("ctx")
    devices = ctx_count * lax.axis_size("head")
    copies, own_length = spread(lengths, queries, ctx_count)
    arrived = exchange(copies, "ctx")
    rows_of = lambda values: values.reshape(-1, values.shape[-1])
    parts = attend(
        own_length, arrived, queries, k_new, v_new, *map(rows_of, (k_suffix, v_suffix, k_prefix, v_prefix))
    )
    copies = join_partials(exchange(parts, "ctx"), (devices, *queries.shape[1:]))
    order = listed(ctx_count, devices // ctx_count)
    hidden_part, hidden_copies = project(order, exchange(copies), w_out.T, residual)
    shares, attention = forward(
        order, exchange(hidden_copies), residual.shape[0], norm_gain, copies, w_gate.T, w_up.T, w_down
    )
    return (attention[None], total(exchange(shares), hidden_part))


def solution(mesh):
    placed = (
        P("ctx", "head", None),
        P("ctx", "head", None),
        P("ctx", "head", None),
        P("ctx", None, "head", None),
        P("ctx", None, "head", None),
        P("ctx"),
        P("ctx", "head", None),
        P("ctx", "head", None),
        P(None, BOTH),
        P(None, BOTH),
        P(),
        P(None, BOTH),
        P(None, BOTH),
        P(BOTH, None),
    )
    return jax.shard_map(
        body,
        mesh=mesh,
        in_specs=placed,
        out_specs=(P("ctx", "head", None), P(None, BOTH)),
        check_vma=False,
    )
```

```python
import functools

import jax
import jax.numpy as jnp
from jax import lax
from jax.experimental import pallas as pl
from jax.experimental.pallas import tpu as pltpu
from jax.sharding import PartitionSpec as P

SCORE_SCALE = 168.0 ** (-0.5)
NORM_EPSILON = 1e-06
MASKED = -1e30
MIB = 1024 * 1024
COST = pl.CostEstimate(flops=10**10, bytes_accessed=MIB, transcendentals=10**6)
TERMS = 3
LANES = 128
HALF = LANES // 2
BOTH = ("ctx", "head")


def head_bias(rows, columns, heads, kv_heads):
    group = heads // kv_heads
    tile = (heads, 128)
    row = lax.broadcasted_iota(jnp.int32, tile, 0)
    column = lax.broadcasted_iota(jnp.int32, tile, 1)
    bias = jnp.where(row // group == lax.rem(column, kv_heads), 0.0, MASKED)
    return jnp.tile(bias, (rows // heads, columns // 128))


def in_hbm(operand):
    return pltpu.with_memory_space_constraint(operand, pltpu.HBM)


def dot_rows(left, right):
    return lax.dot_general(left, right, (((1,), (1,)), ((), ())), preferred_element_type=jnp.float32)


def stat_rows(row_max, row_total, shape):
    lane = lax.broadcasted_iota(jnp.int32, shape, 1)
    return jnp.where(lane == 0, row_max, row_total)


def slot(rows, columns):
    if rows == 8 and LANES < columns <= LANES + HALF:
        return 3, 4, LANES
    return rows, columns


def put(ref, places, value):
    if ref.ndim == 3:
        for place in places:
            ref[place] = value.astype(ref.dtype)
        return
    rows, columns = value.shape
    rest = value[:, LANES:]
    if columns < LANES + HALF:
        rest = jnp.concatenate([rest, jnp.zeros((rows, LANES + HALF - columns), value.dtype)], axis=1)
    rest = jnp.concatenate([rest[:4], rest[4:]], axis=1)
    pieces = [piece.astype(ref.dtype) for piece in (value[:4, :LANES], value[4:, :LANES], rest)]
    for place in places:
        for part, piece in enumerate(pieces):
            ref[place, part] = piece


def joined(first, second, rest):
    low = jnp.concatenate([first, second], axis=0).astype(jnp.float32)
    rest = rest.astype(jnp.float32)
    return low, jnp.concatenate([rest, pltpu.roll(rest, HALF, 1)], axis=0)


def turn(value, columns, back=False):
    device = lax.axis_index("ctx") * lax.axis_size("head") + lax.axis_index("head")
    offset = lax.rem(device * columns, LANES)
    return pltpu.roll(value, lax.rem(LANES - offset, LANES) if back else offset, 1)


def put_turned(ref, value):
    rows, columns = value.shape
    rest = jnp.concatenate(
        [value[:, LANES:], jnp.zeros((rows, 2 * LANES - columns), value.dtype)], axis=1
    )
    low, rest = turn(value[:, :LANES], columns), turn(rest, columns)
    rest = rest[:4] + pltpu.roll(rest, HALF, 1)[4:]
    pieces = [piece.astype(ref.dtype) for piece in (low[:4], low[4:], rest)]
    for place in range(ref.shape[0]):
        for part, piece in enumerate(pieces):
            ref[place, part] = piece


def whole_state(pieces_ref, order, columns):
    lane = lax.broadcasted_iota(jnp.int32, (8, LANES), 1)
    tiles = {}
    for device in range(len(order)):
        place = order.index(device)
        low, rest = joined(*(pieces_ref[place, part] for part in range(3)))
        first, offset = divmod(device * columns, LANES)
        tiles[first] = jnp.where(lane >= offset, low, tiles[first]) if offset else low
        tiles[first + 1] = jnp.where(lane < offset, low, rest)
        if offset + columns - LANES > LANES:
            tiles[first + 2] = rest
    return jnp.concatenate([tiles[place] for place in range(len(order) * columns // LANES)], axis=1)


def put_columns(ref, order, share, columns):
    lane = lax.broadcasted_iota(jnp.int32, (8, LANES), 1)
    tile = lambda place: share[:, place * LANES : (place + 1) * LANES]
    for device in range(len(order)):
        first, offset = divmod(device * columns, LANES)
        end = offset + columns - LANES
        low = jnp.where(lane >= offset, tile(first), tile(first + 1)) if offset else tile(first)
        rest = tile(first + 1)
        own = (lane >= offset) & (lane < end)
        if end > LANES:
            rest = jnp.where(lane >= offset, rest, tile(first + 2))
            own = (lane >= offset) | (lane < end - LANES)
        rest = jnp.where(own[:4], rest[:4], pltpu.roll(rest, HALF, 1)[4:])
        place = order.index(device)
        for part, piece in enumerate((low[:4], low[4:], rest)):
            ref[place, part] = piece.astype(ref.dtype)


def spread_kernel(length_ref, source_hbm, copies_ref, lengths_ref, source_ref, sem):
    load = pltpu.make_async_copy(source_hbm, source_ref, sem)
    load.start()
    lengths_ref[...] = jnp.full(lengths_ref.shape, length_ref[0], jnp.int32)
    load.wait()
    for place in range(copies_ref.shape[0]):
        copies_ref[place] = source_ref[0]


def spread(lengths, value, count):
    return pl.pallas_call(
        spread_kernel,
        out_shape=(
            jax.ShapeDtypeStruct((count, *value.shape[1:]), value.dtype),
            jax.ShapeDtypeStruct(value.shape[1:], jnp.int32),
        ),
        in_specs=[pl.BlockSpec(memory_space=pltpu.SMEM), pl.BlockSpec(memory_space=pl.ANY)],
        scratch_shapes=[pltpu.VMEM(value.shape, value.dtype), pltpu.SemaphoreType.DMA],
        compiler_params=pltpu.CompilerParams(vmem_limit_bytes=4 * MIB),
        cost_estimate=COST,
    )(lengths, in_hbm(value))


def attention_kernel(
    length_ref, arrived_ref, kn_ref, vn_ref, ks_ref, vs_ref, kp_ref, vp_ref, part_ref, sum_ref, stat_ref
):
    count, heads, width = arrived_ref.shape
    kv_heads = kn_ref.shape[1]
    rows = count * heads
    queries = arrived_ref[...].reshape(rows, width)
    row = lax.broadcasted_iota(jnp.int32, (rows, LANES), 0)
    own = jnp.where(row // heads == lax.axis_index("ctx"), 0.0, MASKED)
    prompt_scores = SCORE_SCALE * dot_rows(queries, kp_ref[...])
    prompt_scores = prompt_scores + head_bias(*prompt_scores.shape, heads, kv_heads)
    cached_scores = SCORE_SCALE * dot_rows(queries, ks_ref[...])
    column = lax.broadcasted_iota(jnp.int32, (heads, cached_scores.shape[1]), 1)
    unused = jnp.where(column // kv_heads < length_ref[:, 0:1], 0.0, MASKED)
    bias = head_bias(heads, cached_scores.shape[1], heads, kv_heads) + unused
    bias = jnp.tile(bias, (count, 1)) + own[:, 0:1]
    cached_scores = cached_scores + bias
    new_scores = SCORE_SCALE * dot_rows(queries, kn_ref[0])
    new_scores = new_scores + head_bias(rows, LANES, heads, kv_heads)[:, :kv_heads] + own[:, :kv_heads]
    scores = (prompt_scores, cached_scores, new_scores)
    row_max = functools.reduce(jnp.maximum, [jnp.max(part, axis=1, keepdims=True) for part in scores])
    weights = [jnp.exp(part - row_max).astype(jnp.bfloat16) for part in scores]
    row_total = sum(jnp.sum(part.astype(jnp.float32), axis=1, keepdims=True) for part in weights)
    row_sum = sum(
        jnp.dot(part, values, preferred_element_type=jnp.float32)
        for part, values in zip(weights, (vp_ref[...], vs_ref[...], vn_ref[0]))
    )
    sum_ref[...] = row_sum.reshape(count, heads, width)
    stat_ref[...] = stat_rows(row_max, row_total, row_sum.shape).reshape(count, heads, width)
    lane = lax.broadcasted_iota(jnp.int32, (heads, HALF), 1)
    for place in range(count):
        total = stat_ref[place, :, 1:2]
        rest = jnp.broadcast_to(stat_ref[place, :, 0:1] + jnp.log(total), (heads, HALF))
        terms = jnp.zeros((heads, HALF), jnp.float32)
        for term in range(TERMS):
            rounded = rest.astype(jnp.bfloat16).astype(jnp.float32)
            terms = jnp.where(lane == term, rounded, terms)
            rest = rest - rounded
        put(part_ref, (place,), jnp.concatenate([sum_ref[place] / total, terms], axis=1))


def attend(lengths, arrived, *operands):
    count, heads, width = arrived.shape
    return pl.pallas_call(
        attention_kernel,
        out_shape=jax.ShapeDtypeStruct((count, *slot(heads, width + HALF)), jnp.bfloat16),
        scratch_shapes=[pltpu.VMEM(arrived.shape, jnp.float32)] * 2,
        compiler_params=pltpu.CompilerParams(vmem_limit_bytes=24 * MIB),
        cost_estimate=COST,
    )(lengths, arrived, *operands)


def join_kernel(part_ref, copies_ref):
    logs, shares = [], []
    for source in range(part_ref.shape[0]):
        share, terms = joined(*(part_ref[source, part] for part in range(3)))
        shares.append(share)
        logs.append(jnp.sum(terms[:, :TERMS], axis=1, keepdims=True))
    largest = functools.reduce(jnp.maximum, logs)
    factors = [jnp.exp(log - largest) for log in logs]
    summed = sum(share * factor for share, factor in zip(shares, factors))
    attention = (summed / sum(factors)).astype(jnp.bfloat16)
    for place in range(copies_ref.shape[0]):
        copies_ref[place] = attention


def join_partials(parts, shape):
    return pl.pallas_call(
        join_kernel,
        out_shape=jax.ShapeDtypeStruct(shape, jnp.bfloat16),
        compiler_params=pltpu.CompilerParams(vmem_limit_bytes=8 * MIB),
        cost_estimate=COST,
    )(parts)


def project_kernel(order, rows_ref, w_ref, residual_ref, out_ref, copies_ref, wide_ref):
    devices, heads, width = rows_ref.shape
    completions = residual_ref.shape[0]
    all_heads = devices * heads // completions
    for place, device in enumerate(order):
        wide_ref[device * heads : (device + 1) * heads] = rows_ref[place].astype(jnp.float32)
    rows = [wide_ref[pl.ds(head, completions, stride=all_heads), :] for head in range(all_heads)]
    rows = jnp.concatenate([row.astype(jnp.bfloat16) for row in rows], axis=1)
    hidden = (residual_ref[...].astype(jnp.float32) + dot_rows(rows, w_ref[...])).astype(jnp.bfloat16)
    out_ref[...] = hidden
    if copies_ref.ndim == 4:
        put_turned(copies_ref, hidden.astype(jnp.float32))
    else:
        put(copies_ref, range(copies_ref.shape[0]), hidden)


def project(order, rows, w_out, residual):
    devices, heads, width = rows.shape
    return pl.pallas_call(
        functools.partial(project_kernel, order),
        out_shape=(
            jax.ShapeDtypeStruct(residual.shape, jnp.bfloat16),
            jax.ShapeDtypeStruct((devices, *slot(*residual.shape)), jnp.bfloat16),
        ),
        scratch_shapes=[pltpu.VMEM((devices * heads, width), jnp.float32)],
        compiler_params=pltpu.CompilerParams(vmem_limit_bytes=12 * MIB),
        cost_estimate=COST,
    )(rows, w_out, residual)


def forward_kernel(
    order, pieces_ref, gain_ref, copies_ref, gate_ref, up_ref, down_ref, out_ref, attention_hbm, state_ref, sem
):
    keep = pltpu.make_async_copy(copies_ref.at[0], attention_hbm, sem)
    keep.start()
    devices = pieces_ref.shape[0]
    columns = gain_ref.shape[0] // devices
    if pieces_ref.ndim == 4:
        state = whole_state(pieces_ref, order, columns)
    else:
        for place, device in enumerate(order):
            columns_of = slice(device * columns, (device + 1) * columns)
            state_ref[:, columns_of] = pieces_ref[place].astype(jnp.float32)
        state = state_ref[...]
    mean_square = jnp.mean(state * state, axis=-1, keepdims=True)
    gain = gain_ref[...].reshape(1, devices * columns)
    normed = (state * lax.rsqrt(mean_square + NORM_EPSILON) * gain).astype(jnp.bfloat16)
    gate_values = dot_rows(gate_ref[...], normed).T
    up_values = dot_rows(normed, up_ref[...])
    activated = (jax.nn.gelu(gate_values, approximate=True) * up_values).astype(jnp.bfloat16)
    share = jnp.dot(activated, down_ref[...], preferred_element_type=jnp.float32)
    if pieces_ref.ndim == 4:
        put_columns(out_ref, order, share, columns)
    else:
        for place, device in enumerate(order):
            put(out_ref, (place,), share[:, device * columns : (device + 1) * columns])
    keep.wait()


def forward(order, pieces, completions, gain, copies, *weights):
    return pl.pallas_call(
        functools.partial(forward_kernel, order),
        out_shape=(
            jax.ShapeDtypeStruct(pieces.shape, jnp.bfloat16),
            jax.ShapeDtypeStruct(copies.shape[1:], jnp.bfloat16),
        ),
        out_specs=(pl.BlockSpec(memory_space=pltpu.VMEM), pl.BlockSpec(memory_space=pl.ANY)),
        scratch_shapes=[
            pltpu.VMEM((completions, gain.shape[0]), jnp.float32),
            pltpu.SemaphoreType.DMA,
        ],
        compiler_params=pltpu.CompilerParams(vmem_limit_bytes=8 * MIB),
        cost_estimate=COST,
    )(pieces, gain, copies, *weights)


def total_kernel(shares_ref, hidden_ref, out_ref):
    summed = jnp.sum(shares_ref[...].astype(jnp.float32), axis=0)
    if shares_ref.ndim == 4:
        columns = hidden_ref.shape[1]
        low, rest = (turn(part, columns, back=True) for part in joined(*summed))
        summed = jnp.concatenate([low, rest[:, : columns - LANES]], axis=1)
    out_ref[...] = (hidden_ref[...].astype(jnp.float32) + summed).astype(jnp.bfloat16)


def total(shares, hidden):
    return pl.pallas_call(
        total_kernel,
        out_shape=jax.ShapeDtypeStruct(hidden.shape, jnp.bfloat16),
        compiler_params=pltpu.CompilerParams(vmem_limit_bytes=16 * MIB),
    )(shares, hidden)


def listed(ctx_count, groups):
    order = (0, 1, 4, 5, 6, 7, 2, 3) if ctx_count == 8 else range(ctx_count)
    return [ctx * groups + group for ctx in order for group in range(groups)]


def exchange(copies, axes=BOTH):
    groups = None
    if axes == BOTH:
        groups = [listed(lax.axis_size("ctx"), lax.axis_size("head"))]
    return lax.all_to_all(
        copies, axes, split_axis=0, concat_axis=0, tiled=True, axis_index_groups=groups
    )


def body(
    queries,
    k_new,
    v_new,
    k_suffix,
    v_suffix,
    lengths,
    k_prefix,
    v_prefix,
    w_out,
    residual,
    norm_gain,
    w_gate,
    w_up,
    w_down,
):
    ctx_count = lax.axis_size("ctx")
    devices = ctx_count * lax.axis_size("head")
    copies, own_length = spread(lengths, queries, ctx_count)
    arrived = exchange(copies, "ctx")
    rows_of = lambda values: values.reshape(-1, values.shape[-1])
    parts = attend(
        own_length, arrived, k_new, v_new, *map(rows_of, (k_suffix, v_suffix, k_prefix, v_prefix))
    )
    copies = join_partials(exchange(parts, "ctx"), (devices, *queries.shape[1:]))
    order = listed(ctx_count, devices // ctx_count)
    hidden_part, hidden_copies = project(order, exchange(copies), w_out.T, residual)
    shares, attention = forward(
        order, exchange(hidden_copies), residual.shape[0], norm_gain, copies, w_gate.T, w_up.T, w_down
    )
    return (attention[None], total(exchange(shares), hidden_part))


def solution(mesh):
    placed = (
        P("ctx", "head", None),
        P("ctx", "head", None),
        P("ctx", "head", None),
        P("ctx", None, "head", None),
        P("ctx", None, "head", None),
        P("ctx"),
        P("ctx", "head", None),
        P("ctx", "head", None),
        P(None, BOTH),
        P(None, BOTH),
        P(),
        P(None, BOTH),
        P(None, BOTH),
        P(BOTH, None),
    )
    return jax.shard_map(
        body,
        mesh=mesh,
        in_specs=placed,
        out_specs=(P("ctx", "head", None), P(None, BOTH)),
        check_vma=False,
    )
```

```python
import functools

import jax
import jax.numpy as jnp
from jax import lax
from jax.experimental import pallas as pl
from jax.experimental.pallas import tpu as pltpu
from jax.sharding import PartitionSpec as P

SCORE_SCALE = 168.0 ** (-0.5)
NORM_EPSILON = 1e-06
MASKED = -1e30
MIB = 1024 * 1024
COST = pl.CostEstimate(flops=10**10, bytes_accessed=MIB, transcendentals=10**6)
TERMS = 3
LANES = 128
HALF = LANES // 2
BOTH = ("ctx", "head")


def head_bias(rows, columns, heads, kv_heads):
    group = heads // kv_heads
    tile = (heads, 128)
    row = lax.broadcasted_iota(jnp.int32, tile, 0)
    column = lax.broadcasted_iota(jnp.int32, tile, 1)
    bias = jnp.where(row // group == lax.rem(column, kv_heads), 0.0, MASKED)
    return jnp.tile(bias, (rows // heads, columns // 128))


def in_hbm(operand):
    return pltpu.with_memory_space_constraint(operand, pltpu.HBM)


def dot_rows(left, right):
    return lax.dot_general(left, right, (((1,), (1,)), ((), ())), preferred_element_type=jnp.float32)


def stat_rows(row_max, row_total, shape):
    lane = lax.broadcasted_iota(jnp.int32, shape, 1)
    return jnp.where(lane == 0, row_max, row_total)


def slot(rows, columns):
    if rows == 8 and LANES < columns <= LANES + HALF:
        return 3, 4, LANES
    return rows, columns


def put(ref, places, value):
    if ref.ndim == 3:
        for place in places:
            ref[place] = value.astype(ref.dtype)
        return
    rows, columns = value.shape
    rest = value[:, LANES:]
    if columns < LANES + HALF:
        rest = jnp.concatenate([rest, jnp.zeros((rows, LANES + HALF - columns), value.dtype)], axis=1)
    rest = jnp.concatenate([rest[:4], rest[4:]], axis=1)
    pieces = [piece.astype(ref.dtype) for piece in (value[:4, :LANES], value[4:, :LANES], rest)]
    for place in places:
        for part, piece in enumerate(pieces):
            ref[place, part] = piece


def joined(first, second, rest):
    low = jnp.concatenate([first, second], axis=0).astype(jnp.float32)
    rest = rest.astype(jnp.float32)
    return low, jnp.concatenate([rest, pltpu.roll(rest, HALF, 1)], axis=0)


def turn(value, columns, back=False):
    device = lax.axis_index("ctx") * lax.axis_size("head") + lax.axis_index("head")
    offset = lax.rem(device * columns, LANES)
    return pltpu.roll(value, lax.rem(LANES - offset, LANES) if back else offset, 1)


def put_turned(ref, value):
    rows, columns = value.shape
    rest = jnp.concatenate(
        [value[:, LANES:], jnp.zeros((rows, 2 * LANES - columns), value.dtype)], axis=1
    )
    low, rest = turn(value[:, :LANES], columns), turn(rest, columns)
    rest = rest[:4] + pltpu.roll(rest, HALF, 1)[4:]
    pieces = [piece.astype(ref.dtype) for piece in (low[:4], low[4:], rest)]
    for place in range(ref.shape[0]):
        for part, piece in enumerate(pieces):
            ref[place, part] = piece


def whole_state(pieces_ref, order, columns):
    lane = lax.broadcasted_iota(jnp.int32, (8, LANES), 1)
    tiles = {}
    for device in range(len(order)):
        place = order.index(device)
        low, rest = joined(*(pieces_ref[place, part] for part in range(3)))
        first, offset = divmod(device * columns, LANES)
        tiles[first] = jnp.where(lane >= offset, low, tiles[first]) if offset else low
        tiles[first + 1] = jnp.where(lane < offset, low, rest)
        if offset + columns - LANES > LANES:
            tiles[first + 2] = rest
    return jnp.concatenate([tiles[place] for place in range(len(order) * columns // LANES)], axis=1)


def put_columns(ref, order, share, columns):
    lane = lax.broadcasted_iota(jnp.int32, (8, LANES), 1)
    tile = lambda place: share[:, place * LANES : (place + 1) * LANES]
    for device in range(len(order)):
        first, offset = divmod(device * columns, LANES)
        end = offset + columns - LANES
        low = jnp.where(lane >= offset, tile(first), tile(first + 1)) if offset else tile(first)
        rest = tile(first + 1)
        own = (lane >= offset) & (lane < end)
        if end > LANES:
            rest = jnp.where(lane >= offset, rest, tile(first + 2))
            own = (lane >= offset) | (lane < end - LANES)
        rest = jnp.where(own[:4], rest[:4], pltpu.roll(rest, HALF, 1)[4:])
        place = order.index(device)
        for part, piece in enumerate((low[:4], low[4:], rest)):
            ref[place, part] = piece.astype(ref.dtype)


def spread_kernel(length_ref, source_hbm, copies_ref, lengths_ref, source_ref, sem):
    load = pltpu.make_async_copy(source_hbm, source_ref, sem)
    load.start()
    lengths_ref[...] = jnp.full(lengths_ref.shape, length_ref[0], jnp.int32)
    load.wait()
    for place in range(copies_ref.shape[0]):
        copies_ref[place] = source_ref[0]


def spread(lengths, value, count):
    return pl.pallas_call(
        spread_kernel,
        out_shape=(
            jax.ShapeDtypeStruct((count, *value.shape[1:]), value.dtype),
            jax.ShapeDtypeStruct(value.shape[1:], jnp.int32),
        ),
        in_specs=[pl.BlockSpec(memory_space=pltpu.SMEM), pl.BlockSpec(memory_space=pl.ANY)],
        scratch_shapes=[pltpu.VMEM(value.shape, value.dtype), pltpu.SemaphoreType.DMA],
        compiler_params=pltpu.CompilerParams(vmem_limit_bytes=4 * MIB),
        cost_estimate=COST,
    )(lengths, in_hbm(value))


def attention_kernel(
    length_ref, arrived_ref, kn_ref, vn_ref, ks_ref, vs_ref, kp_ref, vp_ref, part_ref, sum_ref, stat_ref
):
    count, heads, width = arrived_ref.shape
    kv_heads = kn_ref.shape[1]
    rows = count * heads
    queries = arrived_ref[...].reshape(rows, width)
    row = lax.broadcasted_iota(jnp.int32, (rows, LANES), 0)
    own = jnp.where(row // heads == lax.axis_index("ctx"), 0.0, MASKED)
    prompt_scores = SCORE_SCALE * dot_rows(queries, kp_ref[...])
    prompt_scores = prompt_scores + head_bias(*prompt_scores.shape, heads, kv_heads)
    cached_scores = SCORE_SCALE * dot_rows(queries, ks_ref[...])
    column = lax.broadcasted_iota(jnp.int32, (heads, cached_scores.shape[1]), 1)
    unused = jnp.where(column // kv_heads < length_ref[:, 0:1], 0.0, MASKED)
    bias = head_bias(heads, cached_scores.shape[1], heads, kv_heads) + unused
    bias = jnp.tile(bias, (count, 1)) + own[:, 0:1]
    cached_scores = cached_scores + bias
    new_scores = SCORE_SCALE * dot_rows(queries, kn_ref[0])
    new_scores = new_scores + head_bias(rows, LANES, heads, kv_heads)[:, :kv_heads] + own[:, :kv_heads]
    scores = (prompt_scores, cached_scores, new_scores)
    row_max = functools.reduce(jnp.maximum, [jnp.max(part, axis=1, keepdims=True) for part in scores])
    weights = [jnp.exp(part - row_max).astype(jnp.bfloat16) for part in scores]
    row_total = sum(jnp.sum(part.astype(jnp.float32), axis=1, keepdims=True) for part in weights)
    row_sum = sum(
        jnp.dot(part, values, preferred_element_type=jnp.float32)
        for part, values in zip(weights, (vp_ref[...], vs_ref[...], vn_ref[0]))
    )
    sum_ref[...] = row_sum.reshape(count, heads, width)
    stat_ref[...] = stat_rows(row_max, row_total, row_sum.shape).reshape(count, heads, width)
    lane = lax.broadcasted_iota(jnp.int32, (heads, HALF), 1)
    for place in range(count):
        total = stat_ref[place, :, 1:2]
        rest = jnp.broadcast_to(stat_ref[place, :, 0:1] + jnp.log(total), (heads, HALF))
        terms = jnp.zeros((heads, HALF), jnp.float32)
        for term in range(TERMS):
            rounded = rest.astype(jnp.bfloat16).astype(jnp.float32)
            terms = jnp.where(lane == term, rounded, terms)
            rest = rest - rounded
        put(part_ref, (place,), jnp.concatenate([sum_ref[place] / total, terms], axis=1))


def attend(lengths, arrived, *operands):
    count, heads, width = arrived.shape
    return pl.pallas_call(
        attention_kernel,
        out_shape=jax.ShapeDtypeStruct((count, *slot(heads, width + HALF)), jnp.bfloat16),
        scratch_shapes=[pltpu.VMEM(arrived.shape, jnp.float32)] * 2,
        compiler_params=pltpu.CompilerParams(vmem_limit_bytes=24 * MIB),
        cost_estimate=COST,
    )(lengths, arrived, *operands)


def join_kernel(part_ref, copies_ref):
    logs, shares = [], []
    for source in range(part_ref.shape[0]):
        share, terms = joined(*(part_ref[source, part] for part in range(3)))
        shares.append(share)
        logs.append(jnp.sum(terms[:, :TERMS], axis=1, keepdims=True))
    largest = functools.reduce(jnp.maximum, logs)
    factors = [jnp.exp(log - largest) for log in logs]
    summed = sum(share * factor for share, factor in zip(shares, factors))
    attention = (summed / sum(factors)).astype(jnp.bfloat16)
    for place in range(copies_ref.shape[0]):
        copies_ref[place] = attention


def join_partials(parts, shape):
    return pl.pallas_call(
        join_kernel,
        out_shape=jax.ShapeDtypeStruct(shape, jnp.bfloat16),
        compiler_params=pltpu.CompilerParams(vmem_limit_bytes=8 * MIB),
        cost_estimate=COST,
    )(parts)


def project_kernel(order, rows_ref, w_ref, residual_ref, out_ref, copies_ref, wide_ref):
    devices, heads, width = rows_ref.shape
    completions = residual_ref.shape[0]
    all_heads = devices * heads // completions
    for place, device in enumerate(order):
        wide_ref[device * heads : (device + 1) * heads] = rows_ref[place].astype(jnp.float32)
    rows = [wide_ref[pl.ds(head, completions, stride=all_heads), :] for head in range(all_heads)]
    rows = jnp.concatenate([row.astype(jnp.bfloat16) for row in rows], axis=1)
    projected = dot_rows(w_ref[...], rows).T
    hidden = (residual_ref[...].astype(jnp.float32) + projected).astype(jnp.bfloat16)
    out_ref[...] = hidden
    if copies_ref.ndim == 4:
        put_turned(copies_ref, hidden.astype(jnp.float32))
    else:
        put(copies_ref, range(copies_ref.shape[0]), hidden)


def project(order, rows, w_out, residual):
    devices, heads, width = rows.shape
    return pl.pallas_call(
        functools.partial(project_kernel, order),
        out_shape=(
            jax.ShapeDtypeStruct(residual.shape, jnp.bfloat16),
            jax.ShapeDtypeStruct((devices, *slot(*residual.shape)), jnp.bfloat16),
        ),
        scratch_shapes=[pltpu.VMEM((devices * heads, width), jnp.float32)],
        compiler_params=pltpu.CompilerParams(vmem_limit_bytes=12 * MIB),
        cost_estimate=COST,
    )(rows, w_out, residual)


def forward_kernel(
    order, pieces_ref, gain_ref, copies_ref, gate_ref, up_ref, down_ref, out_ref, attention_hbm, state_ref, sem
):
    keep = pltpu.make_async_copy(copies_ref.at[0], attention_hbm, sem)
    keep.start()
    devices = pieces_ref.shape[0]
    columns = gain_ref.shape[0] // devices
    if pieces_ref.ndim == 4:
        state = whole_state(pieces_ref, order, columns)
    else:
        for place, device in enumerate(order):
            columns_of = slice(device * columns, (device + 1) * columns)
            state_ref[:, columns_of] = pieces_ref[place].astype(jnp.float32)
        state = state_ref[...]
    mean_square = jnp.mean(state * state, axis=-1, keepdims=True)
    gain = gain_ref[...].reshape(1, devices * columns)
    normed = (state * lax.rsqrt(mean_square + NORM_EPSILON) * gain).astype(jnp.bfloat16)
    gate_values = dot_rows(gate_ref[...], normed).T
    up_values = dot_rows(up_ref[...], normed).T
    activated = (jax.nn.gelu(gate_values, approximate=True) * up_values).astype(jnp.bfloat16)
    share = jnp.dot(activated, down_ref[...], preferred_element_type=jnp.float32)
    if pieces_ref.ndim == 4:
        put_columns(out_ref, order, share, columns)
    else:
        for place, device in enumerate(order):
            put(out_ref, (place,), share[:, device * columns : (device + 1) * columns])
    keep.wait()


def forward(order, pieces, completions, gain, copies, *weights):
    return pl.pallas_call(
        functools.partial(forward_kernel, order),
        out_shape=(
            jax.ShapeDtypeStruct(pieces.shape, jnp.bfloat16),
            jax.ShapeDtypeStruct(copies.shape[1:], jnp.bfloat16),
        ),
        out_specs=(pl.BlockSpec(memory_space=pltpu.VMEM), pl.BlockSpec(memory_space=pl.ANY)),
        scratch_shapes=[
            pltpu.VMEM((completions, gain.shape[0]), jnp.float32),
            pltpu.SemaphoreType.DMA,
        ],
        compiler_params=pltpu.CompilerParams(vmem_limit_bytes=8 * MIB),
        cost_estimate=COST,
    )(pieces, gain, copies, *weights)


def total_kernel(shares_ref, hidden_ref, out_ref):
    summed = jnp.sum(shares_ref[...].astype(jnp.float32), axis=0)
    if shares_ref.ndim == 4:
        columns = hidden_ref.shape[1]
        low, rest = (turn(part, columns, back=True) for part in joined(*summed))
        summed = jnp.concatenate([low, rest[:, : columns - LANES]], axis=1)
    out_ref[...] = (hidden_ref[...].astype(jnp.float32) + summed).astype(jnp.bfloat16)


def total(shares, hidden):
    return pl.pallas_call(
        total_kernel,
        out_shape=jax.ShapeDtypeStruct(hidden.shape, jnp.bfloat16),
        compiler_params=pltpu.CompilerParams(vmem_limit_bytes=16 * MIB),
    )(shares, hidden)


def listed(ctx_count, groups):
    order = (0, 1, 4, 5, 6, 7, 2, 3) if ctx_count == 8 else range(ctx_count)
    return [ctx * groups + group for ctx in order for group in range(groups)]


def exchange(copies, axes=BOTH):
    groups = None
    if axes == BOTH:
        groups = [listed(lax.axis_size("ctx"), lax.axis_size("head"))]
    return lax.all_to_all(
        copies, axes, split_axis=0, concat_axis=0, tiled=True, axis_index_groups=groups
    )


def body(
    queries,
    k_new,
    v_new,
    k_suffix,
    v_suffix,
    lengths,
    k_prefix,
    v_prefix,
    w_out,
    residual,
    norm_gain,
    w_gate,
    w_up,
    w_down,
):
    ctx_count = lax.axis_size("ctx")
    devices = ctx_count * lax.axis_size("head")
    copies, own_length = spread(lengths, queries, ctx_count)
    arrived = exchange(copies, "ctx")
    rows_of = lambda values: values.reshape(-1, values.shape[-1])
    parts = attend(
        own_length, arrived, k_new, v_new, *map(rows_of, (k_suffix, v_suffix, k_prefix, v_prefix))
    )
    copies = join_partials(exchange(parts, "ctx"), (devices, *queries.shape[1:]))
    order = listed(ctx_count, devices // ctx_count)
    hidden_part, hidden_copies = project(order, exchange(copies), w_out.T, residual)
    shares, attention = forward(
        order, exchange(hidden_copies), residual.shape[0], norm_gain, copies, w_gate.T, w_up.T, w_down
    )
    return (attention[None], total(exchange(shares), hidden_part))


def solution(mesh):
    placed = (
        P("ctx", "head", None),
        P("ctx", "head", None),
        P("ctx", "head", None),
        P("ctx", None, "head", None),
        P("ctx", None, "head", None),
        P("ctx"),
        P("ctx", "head", None),
        P("ctx", "head", None),
        P(None, BOTH),
        P(None, BOTH),
        P(),
        P(None, BOTH),
        P(None, BOTH),
        P(BOTH, None),
    )
    return jax.shard_map(
        body,
        mesh=mesh,
        in_specs=placed,
        out_specs=(P("ctx", "head", None), P(None, BOTH)),
        check_vma=False,
    )
```

```python
import functools

import jax
import jax.numpy as jnp
from jax import lax
from jax.experimental import pallas as pl
from jax.experimental.pallas import tpu as pltpu
from jax.sharding import PartitionSpec as P

SCORE_SCALE = 168.0 ** (-0.5)
NORM_EPSILON = 1e-06
MASKED = -1e30
MIB = 1024 * 1024
COST = pl.CostEstimate(flops=10**10, bytes_accessed=MIB, transcendentals=10**6)
TERMS = 3
CHUNKS = 3
LANES = 128
HALF = LANES // 2
BOTH = ("ctx", "head")


def head_bias(rows, columns, heads, kv_heads):
    group = heads // kv_heads
    tile = (heads, 128)
    row = lax.broadcasted_iota(jnp.int32, tile, 0)
    column = lax.broadcasted_iota(jnp.int32, tile, 1)
    bias = jnp.where(row // group == lax.rem(column, kv_heads), 0.0, MASKED)
    return jnp.tile(bias, (rows // heads, columns // 128))


def in_hbm(operand):
    return pltpu.with_memory_space_constraint(operand, pltpu.HBM)


def dot_rows(left, right):
    return lax.dot_general(left, right, (((1,), (1,)), ((), ())), preferred_element_type=jnp.float32)


def stat_rows(row_max, row_total, shape):
    lane = lax.broadcasted_iota(jnp.int32, shape, 1)
    return jnp.where(lane == 0, row_max, row_total)


def slot(rows, columns):
    if rows == 8 and LANES < columns <= LANES + HALF:
        return 3, 4, LANES
    return rows, columns


def put(ref, places, value):
    if ref.ndim == 3:
        for place in places:
            ref[place] = value.astype(ref.dtype)
        return
    rows, columns = value.shape
    rest = value[:, LANES:]
    if columns < LANES + HALF:
        rest = jnp.concatenate([rest, jnp.zeros((rows, LANES + HALF - columns), value.dtype)], axis=1)
    rest = jnp.concatenate([rest[:4], rest[4:]], axis=1)
    pieces = [piece.astype(ref.dtype) for piece in (value[:4, :LANES], value[4:, :LANES], rest)]
    for place in places:
        for part, piece in enumerate(pieces):
            ref[place, part] = piece


def joined(first, second, rest):
    low = jnp.concatenate([first, second], axis=0).astype(jnp.float32)
    rest = rest.astype(jnp.float32)
    return low, jnp.concatenate([rest, pltpu.roll(rest, HALF, 1)], axis=0)


def turn(value, columns, back=False):
    device = lax.axis_index("ctx") * lax.axis_size("head") + lax.axis_index("head")
    offset = lax.rem(device * columns, LANES)
    return pltpu.roll(value, lax.rem(LANES - offset, LANES) if back else offset, 1)


def put_turned(ref, value):
    rows, columns = value.shape
    rest = jnp.concatenate(
        [value[:, LANES:], jnp.zeros((rows, 2 * LANES - columns), value.dtype)], axis=1
    )
    low, rest = turn(value[:, :LANES], columns), turn(rest, columns)
    rest = rest[:4] + pltpu.roll(rest, HALF, 1)[4:]
    pieces = [piece.astype(ref.dtype) for piece in (low[:4], low[4:], rest)]
    for place in range(ref.shape[0]):
        for part, piece in enumerate(pieces):
            ref[place, part] = piece


def whole_state(pieces_ref, order, columns):
    lane = lax.broadcasted_iota(jnp.int32, (8, LANES), 1)
    tiles = {}
    for device in range(len(order)):
        place = order.index(device)
        low, rest = joined(*(pieces_ref[place, part] for part in range(3)))
        first, offset = divmod(device * columns, LANES)
        tiles[first] = jnp.where(lane >= offset, low, tiles[first]) if offset else low
        tiles[first + 1] = jnp.where(lane < offset, low, rest)
        if offset + columns - LANES > LANES:
            tiles[first + 2] = rest
    return jnp.concatenate([tiles[place] for place in range(len(order) * columns // LANES)], axis=1)


def put_columns(ref, order, share, columns):
    lane = lax.broadcasted_iota(jnp.int32, (8, LANES), 1)
    tile = lambda place: share[:, place * LANES : (place + 1) * LANES]
    for device in range(len(order)):
        first, offset = divmod(device * columns, LANES)
        end = offset + columns - LANES
        low = jnp.where(lane >= offset, tile(first), tile(first + 1)) if offset else tile(first)
        rest = tile(first + 1)
        own = (lane >= offset) & (lane < end)
        if end > LANES:
            rest = jnp.where(lane >= offset, rest, tile(first + 2))
            own = (lane >= offset) | (lane < end - LANES)
        rest = jnp.where(own[:4], rest[:4], pltpu.roll(rest, HALF, 1)[4:])
        place = order.index(device)
        for part, piece in enumerate((low[:4], low[4:], rest)):
            ref[place, part] = piece.astype(ref.dtype)


def spread_kernel(length_ref, source_hbm, copies_ref, lengths_ref, source_ref, sem):
    load = pltpu.make_async_copy(source_hbm, source_ref, sem)
    load.start()
    lengths_ref[...] = jnp.full(lengths_ref.shape, length_ref[0], jnp.int32)
    load.wait()
    for place in range(copies_ref.shape[0]):
        copies_ref[place] = source_ref[0]


def spread(lengths, value, count):
    return pl.pallas_call(
        spread_kernel,
        out_shape=(
            jax.ShapeDtypeStruct((count, *value.shape[1:]), value.dtype),
            jax.ShapeDtypeStruct(value.shape[1:], jnp.int32),
        ),
        in_specs=[pl.BlockSpec(memory_space=pltpu.SMEM), pl.BlockSpec(memory_space=pl.ANY)],
        scratch_shapes=[pltpu.VMEM(value.shape, value.dtype), pltpu.SemaphoreType.DMA],
        compiler_params=pltpu.CompilerParams(vmem_limit_bytes=4 * MIB),
        cost_estimate=COST,
    )(lengths, in_hbm(value))


def attention_kernel(
    length_ref, arrived_ref, kn_ref, vn_ref, ks_ref, vs_ref, kp_ref, vp_ref, part_ref, sum_ref, stat_ref
):
    count, heads, width = arrived_ref.shape
    kv_heads = kn_ref.shape[1]
    rows = count * heads
    queries = arrived_ref[...].reshape(rows, width)
    row = lax.broadcasted_iota(jnp.int32, (rows, LANES), 0)
    own = jnp.where(row // heads == lax.axis_index("ctx"), 0.0, MASKED)
    prompt_scores = SCORE_SCALE * dot_rows(queries, kp_ref[...])
    prompt_scores = prompt_scores + head_bias(*prompt_scores.shape, heads, kv_heads)
    cached_scores = SCORE_SCALE * dot_rows(queries, ks_ref[...])
    column = lax.broadcasted_iota(jnp.int32, (heads, cached_scores.shape[1]), 1)
    unused = jnp.where(column // kv_heads < length_ref[:, 0:1], 0.0, MASKED)
    bias = head_bias(heads, cached_scores.shape[1], heads, kv_heads) + unused
    bias = jnp.tile(bias, (count, 1)) + own[:, 0:1]
    cached_scores = cached_scores + bias
    new_scores = SCORE_SCALE * dot_rows(queries, kn_ref[0])
    new_scores = new_scores + head_bias(rows, LANES, heads, kv_heads)[:, :kv_heads] + own[:, :kv_heads]
    scores = (prompt_scores, cached_scores, new_scores)
    row_max = functools.reduce(jnp.maximum, [jnp.max(part, axis=1, keepdims=True) for part in scores])
    weights = [jnp.exp(part - row_max).astype(jnp.bfloat16) for part in scores]
    row_total = sum(jnp.sum(part.astype(jnp.float32), axis=1, keepdims=True) for part in weights)
    row_sum = sum(
        jnp.dot(part, values, preferred_element_type=jnp.float32)
        for part, values in zip(weights, (vp_ref[...], vs_ref[...], vn_ref[0]))
    )
    sum_ref[...] = row_sum.reshape(count, heads, width)
    stat_ref[...] = stat_rows(row_max, row_total, row_sum.shape).reshape(count, heads, width)
    lane = lax.broadcasted_iota(jnp.int32, (heads, HALF), 1)
    for place in range(count):
        total = stat_ref[place, :, 1:2]
        rest = jnp.broadcast_to(stat_ref[place, :, 0:1] + jnp.log(total), (heads, HALF))
        terms = jnp.zeros((heads, HALF), jnp.float32)
        for term in range(TERMS):
            rounded = rest.astype(jnp.bfloat16).astype(jnp.float32)
            terms = jnp.where(lane == term, rounded, terms)
            rest = rest - rounded
        put(part_ref, (place,), jnp.concatenate([sum_ref[place] / total, terms], axis=1))


def attend(lengths, arrived, *operands):
    count, heads, width = arrived.shape
    return pl.pallas_call(
        attention_kernel,
        out_shape=jax.ShapeDtypeStruct((count, *slot(heads, width + HALF)), jnp.bfloat16),
        scratch_shapes=[pltpu.VMEM(arrived.shape, jnp.float32)] * 2,
        compiler_params=pltpu.CompilerParams(vmem_limit_bytes=24 * MIB),
        cost_estimate=COST,
    )(lengths, arrived, *operands)


def join_kernel(part_ref, copies_ref):
    logs, shares = [], []
    for source in range(part_ref.shape[0]):
        share, terms = joined(*(part_ref[source, part] for part in range(3)))
        shares.append(share)
        logs.append(jnp.sum(terms[:, :TERMS], axis=1, keepdims=True))
    largest = functools.reduce(jnp.maximum, logs)
    factors = [jnp.exp(log - largest) for log in logs]
    summed = sum(share * factor for share, factor in zip(shares, factors))
    attention = (summed / sum(factors)).astype(jnp.bfloat16)
    for place in range(copies_ref.shape[0]):
        copies_ref[place] = attention


def join_partials(parts, shape):
    return pl.pallas_call(
        join_kernel,
        out_shape=jax.ShapeDtypeStruct(shape, jnp.bfloat16),
        compiler_params=pltpu.CompilerParams(vmem_limit_bytes=8 * MIB),
        cost_estimate=COST,
    )(parts)


def project_kernel(order, rows_ref, w_ref, residual_ref, out_ref, copies_ref, wide_ref):
    devices, heads, width = rows_ref.shape
    completions = residual_ref.shape[0]
    all_heads = devices * heads // completions
    for place, device in enumerate(order):
        wide_ref[device * heads : (device + 1) * heads] = rows_ref[place].astype(jnp.float32)
    rows = [wide_ref[pl.ds(head, completions, stride=all_heads), :] for head in range(all_heads)]
    rows = jnp.concatenate([row.astype(jnp.bfloat16) for row in rows], axis=1)
    hidden = (residual_ref[...].astype(jnp.float32) + dot_rows(rows, w_ref[...])).astype(jnp.bfloat16)
    out_ref[...] = hidden
    if copies_ref.ndim == 4:
        put_turned(copies_ref, hidden.astype(jnp.float32))
    else:
        put(copies_ref, range(copies_ref.shape[0]), hidden)


def project(order, rows, w_out, residual):
    devices, heads, width = rows.shape
    return pl.pallas_call(
        functools.partial(project_kernel, order),
        out_shape=(
            jax.ShapeDtypeStruct(residual.shape, jnp.bfloat16),
            jax.ShapeDtypeStruct((devices, *slot(*residual.shape)), jnp.bfloat16),
        ),
        scratch_shapes=[pltpu.VMEM((devices * heads, width), jnp.float32)],
        compiler_params=pltpu.CompilerParams(vmem_limit_bytes=12 * MIB),
        cost_estimate=COST,
    )(rows, w_out, residual)


def forward_kernel(
    order, pieces_ref, gain_ref, copies_ref, gate_ref, up_ref, down_ref, out_ref, attention_hbm, state_ref, sem
):
    keep = pltpu.make_async_copy(copies_ref.at[0], attention_hbm, sem)
    keep.start()
    devices = pieces_ref.shape[0]
    columns = gain_ref.shape[0] // devices
    if pieces_ref.ndim == 4:
        state = whole_state(pieces_ref, order, columns)
    else:
        for place, device in enumerate(order):
            columns_of = slice(device * columns, (device + 1) * columns)
            state_ref[:, columns_of] = pieces_ref[place].astype(jnp.float32)
        state = state_ref[...]
    mean_square = jnp.mean(state * state, axis=-1, keepdims=True)
    gain = gain_ref[...].reshape(1, devices * columns)
    normed = (state * lax.rsqrt(mean_square + NORM_EPSILON) * gain).astype(jnp.bfloat16)
    units = gate_ref.shape[0]
    count = CHUNKS if units % (16 * CHUNKS) == 0 else 1
    size = units // count
    share = jnp.zeros((normed.shape[0], down_ref.shape[1]), jnp.float32)
    ready = None
    for chunk in range(count + 1):
        if chunk < count:
            rows = slice(chunk * size, (chunk + 1) * size)
            gate_values = dot_rows(gate_ref[rows], normed)
            up_values = dot_rows(normed, up_ref[rows])
        if ready is not None:
            activated, held = ready
            share += jnp.dot(activated, down_ref[held], preferred_element_type=jnp.float32)
        if chunk < count:
            activated = jax.nn.gelu(gate_values.T, approximate=True) * up_values
            ready = activated.astype(jnp.bfloat16), rows
    if pieces_ref.ndim == 4:
        put_columns(out_ref, order, share, columns)
    else:
        for place, device in enumerate(order):
            put(out_ref, (place,), share[:, device * columns : (device + 1) * columns])
    keep.wait()


def forward(order, pieces, completions, gain, copies, *weights):
    return pl.pallas_call(
        functools.partial(forward_kernel, order),
        out_shape=(
            jax.ShapeDtypeStruct(pieces.shape, jnp.bfloat16),
            jax.ShapeDtypeStruct(copies.shape[1:], jnp.bfloat16),
        ),
        out_specs=(pl.BlockSpec(memory_space=pltpu.VMEM), pl.BlockSpec(memory_space=pl.ANY)),
        scratch_shapes=[
            pltpu.VMEM((completions, gain.shape[0]), jnp.float32),
            pltpu.SemaphoreType.DMA,
        ],
        compiler_params=pltpu.CompilerParams(vmem_limit_bytes=8 * MIB),
        cost_estimate=COST,
    )(pieces, gain, copies, *weights)


def total_kernel(shares_ref, hidden_ref, out_ref):
    summed = jnp.sum(shares_ref[...].astype(jnp.float32), axis=0)
    if shares_ref.ndim == 4:
        columns = hidden_ref.shape[1]
        low, rest = (turn(part, columns, back=True) for part in joined(*summed))
        summed = jnp.concatenate([low, rest[:, : columns - LANES]], axis=1)
    out_ref[...] = (hidden_ref[...].astype(jnp.float32) + summed).astype(jnp.bfloat16)


def total(shares, hidden):
    return pl.pallas_call(
        total_kernel,
        out_shape=jax.ShapeDtypeStruct(hidden.shape, jnp.bfloat16),
        compiler_params=pltpu.CompilerParams(vmem_limit_bytes=16 * MIB),
    )(shares, hidden)


def listed(ctx_count, groups):
    order = (0, 1, 4, 5, 6, 7, 2, 3) if ctx_count == 8 else range(ctx_count)
    return [ctx * groups + group for ctx in order for group in range(groups)]


def exchange(copies, axes=BOTH):
    groups = None
    if axes == BOTH:
        groups = [listed(lax.axis_size("ctx"), lax.axis_size("head"))]
    return lax.all_to_all(
        copies, axes, split_axis=0, concat_axis=0, tiled=True, axis_index_groups=groups
    )


def body(
    queries,
    k_new,
    v_new,
    k_suffix,
    v_suffix,
    lengths,
    k_prefix,
    v_prefix,
    w_out,
    residual,
    norm_gain,
    w_gate,
    w_up,
    w_down,
):
    ctx_count = lax.axis_size("ctx")
    devices = ctx_count * lax.axis_size("head")
    copies, own_length = spread(lengths, queries, ctx_count)
    arrived = exchange(copies, "ctx")
    rows_of = lambda values: values.reshape(-1, values.shape[-1])
    parts = attend(
        own_length, arrived, k_new, v_new, *map(rows_of, (k_suffix, v_suffix, k_prefix, v_prefix))
    )
    copies = join_partials(exchange(parts, "ctx"), (devices, *queries.shape[1:]))
    order = listed(ctx_count, devices // ctx_count)
    hidden_part, hidden_copies = project(order, exchange(copies), w_out.T, residual)
    shares, attention = forward(
        order, exchange(hidden_copies), residual.shape[0], norm_gain, copies, w_gate.T, w_up.T, w_down
    )
    return (attention[None], total(exchange(shares), hidden_part))


def solution(mesh):
    placed = (
        P("ctx", "head", None),
        P("ctx", "head", None),
        P("ctx", "head", None),
        P("ctx", None, "head", None),
        P("ctx", None, "head", None),
        P("ctx"),
        P("ctx", "head", None),
        P("ctx", "head", None),
        P(None, BOTH),
        P(None, BOTH),
        P(),
        P(None, BOTH),
        P(None, BOTH),
        P(BOTH, None),
    )
    return jax.shard_map(
        body,
        mesh=mesh,
        in_specs=placed,
        out_specs=(P("ctx", "head", None), P(None, BOTH)),
        check_vma=False,
    )
```

```python
import functools

import jax
import jax.numpy as jnp
from jax import lax
from jax.experimental import pallas as pl
from jax.experimental.pallas import tpu as pltpu
from jax.sharding import PartitionSpec as P

SCORE_SCALE = 168.0 ** (-0.5)
NORM_EPSILON = 1e-06
MASKED = -1e30
MIB = 1024 * 1024
COST = pl.CostEstimate(flops=10**10, bytes_accessed=MIB, transcendentals=10**6)
TERMS = 3
CHUNKS = 3
PARTS = 7
LANES = 128
HALF = LANES // 2
BOTH = ("ctx", "head")


def head_bias(rows, columns, heads, kv_heads):
    group = heads // kv_heads
    tile = (heads, 128)
    row = lax.broadcasted_iota(jnp.int32, tile, 0)
    column = lax.broadcasted_iota(jnp.int32, tile, 1)
    bias = jnp.where(row // group == lax.rem(column, kv_heads), 0.0, MASKED)
    return jnp.tile(bias, (rows // heads, columns // 128))


def in_hbm(operand):
    return pltpu.with_memory_space_constraint(operand, pltpu.HBM)


def dot_rows(left, right):
    return lax.dot_general(left, right, (((1,), (1,)), ((), ())), preferred_element_type=jnp.float32)


def stat_rows(row_max, row_total, shape):
    lane = lax.broadcasted_iota(jnp.int32, shape, 1)
    return jnp.where(lane == 0, row_max, row_total)


def slot(rows, columns):
    if rows == 8 and LANES < columns <= LANES + HALF:
        return 3, 4, LANES
    return rows, columns


def put(ref, places, value):
    if ref.ndim == 3:
        for place in places:
            ref[place] = value.astype(ref.dtype)
        return
    rows, columns = value.shape
    rest = value[:, LANES:]
    if columns < LANES + HALF:
        rest = jnp.concatenate([rest, jnp.zeros((rows, LANES + HALF - columns), value.dtype)], axis=1)
    rest = jnp.concatenate([rest[:4], rest[4:]], axis=1)
    pieces = [piece.astype(ref.dtype) for piece in (value[:4, :LANES], value[4:, :LANES], rest)]
    for place in places:
        for part, piece in enumerate(pieces):
            ref[place, part] = piece


def joined(first, second, rest):
    low = jnp.concatenate([first, second], axis=0).astype(jnp.float32)
    rest = rest.astype(jnp.float32)
    return low, jnp.concatenate([rest, pltpu.roll(rest, HALF, 1)], axis=0)


def turn(value, columns, back=False):
    device = lax.axis_index("ctx") * lax.axis_size("head") + lax.axis_index("head")
    offset = lax.rem(device * columns, LANES)
    return pltpu.roll(value, lax.rem(LANES - offset, LANES) if back else offset, 1)


def put_turned(ref, value):
    rows, columns = value.shape
    rest = jnp.concatenate(
        [value[:, LANES:], jnp.zeros((rows, 2 * LANES - columns), value.dtype)], axis=1
    )
    low, rest = turn(value[:, :LANES], columns), turn(rest, columns)
    rest = rest[:4] + pltpu.roll(rest, HALF, 1)[4:]
    pieces = [piece.astype(ref.dtype) for piece in (low[:4], low[4:], rest)]
    for place in range(ref.shape[0]):
        for part, piece in enumerate(pieces):
            ref[place, part] = piece


def whole_state(pieces_ref, order, columns):
    lane = lax.broadcasted_iota(jnp.int32, (8, LANES), 1)
    tiles = {}
    for device in range(len(order)):
        place = order.index(device)
        low, rest = joined(*(pieces_ref[place, part] for part in range(3)))
        first, offset = divmod(device * columns, LANES)
        tiles[first] = jnp.where(lane >= offset, low, tiles[first]) if offset else low
        tiles[first + 1] = jnp.where(lane < offset, low, rest)
        if offset + columns - LANES > LANES:
            tiles[first + 2] = rest
    return jnp.concatenate([tiles[place] for place in range(len(order) * columns // LANES)], axis=1)


def put_columns(ref, order, share, columns):
    lane = lax.broadcasted_iota(jnp.int32, (8, LANES), 1)
    tile = lambda place: share[:, place * LANES : (place + 1) * LANES]
    for device in range(len(order)):
        first, offset = divmod(device * columns, LANES)
        end = offset + columns - LANES
        low = jnp.where(lane >= offset, tile(first), tile(first + 1)) if offset else tile(first)
        rest = tile(first + 1)
        own = (lane >= offset) & (lane < end)
        if end > LANES:
            rest = jnp.where(lane >= offset, rest, tile(first + 2))
            own = (lane >= offset) | (lane < end - LANES)
        rest = jnp.where(own[:4], rest[:4], pltpu.roll(rest, HALF, 1)[4:])
        place = order.index(device)
        for part, piece in enumerate((low[:4], low[4:], rest)):
            ref[place, part] = piece.astype(ref.dtype)


def spread_kernel(length_ref, source_hbm, copies_ref, lengths_ref, source_ref, sem):
    load = pltpu.make_async_copy(source_hbm, source_ref, sem)
    load.start()
    lengths_ref[...] = jnp.full(lengths_ref.shape, length_ref[0], jnp.int32)
    load.wait()
    for place in range(copies_ref.shape[0]):
        copies_ref[place] = source_ref[0]


def spread(lengths, value, count):
    return pl.pallas_call(
        spread_kernel,
        out_shape=(
            jax.ShapeDtypeStruct((count, *value.shape[1:]), value.dtype),
            jax.ShapeDtypeStruct(value.shape[1:], jnp.int32),
        ),
        in_specs=[pl.BlockSpec(memory_space=pltpu.SMEM), pl.BlockSpec(memory_space=pl.ANY)],
        scratch_shapes=[pltpu.VMEM(value.shape, value.dtype), pltpu.SemaphoreType.DMA],
        compiler_params=pltpu.CompilerParams(vmem_limit_bytes=4 * MIB),
        cost_estimate=COST,
    )(lengths, in_hbm(value))


def attention_kernel(
    length_ref, arrived_ref, kn_ref, vn_ref, ks_ref, vs_ref, kp_ref, vp_ref, part_ref, sum_ref, stat_ref
):
    count, heads, width = arrived_ref.shape
    kv_heads = kn_ref.shape[1]
    rows = count * heads
    queries = arrived_ref[...].reshape(rows, width)
    row = lax.broadcasted_iota(jnp.int32, (rows, LANES), 0)
    own = jnp.where(row // heads == lax.axis_index("ctx"), 0.0, MASKED)
    prompt_scores = SCORE_SCALE * dot_rows(queries, kp_ref[...])
    prompt_scores = prompt_scores + head_bias(*prompt_scores.shape, heads, kv_heads)
    cached_scores = SCORE_SCALE * dot_rows(queries, ks_ref[...])
    column = lax.broadcasted_iota(jnp.int32, (heads, cached_scores.shape[1]), 1)
    unused = jnp.where(column // kv_heads < length_ref[:, 0:1], 0.0, MASKED)
    bias = head_bias(heads, cached_scores.shape[1], heads, kv_heads) + unused
    bias = jnp.tile(bias, (count, 1)) + own[:, 0:1]
    cached_scores = cached_scores + bias
    new_scores = SCORE_SCALE * dot_rows(queries, kn_ref[0])
    new_scores = new_scores + head_bias(rows, LANES, heads, kv_heads)[:, :kv_heads] + own[:, :kv_heads]
    scores = (prompt_scores, cached_scores, new_scores)
    row_max = functools.reduce(jnp.maximum, [jnp.max(part, axis=1, keepdims=True) for part in scores])
    weights = [jnp.exp(part - row_max).astype(jnp.bfloat16) for part in scores]
    row_total = sum(jnp.sum(part.astype(jnp.float32), axis=1, keepdims=True) for part in weights)
    row_sum = sum(
        jnp.dot(part, values, preferred_element_type=jnp.float32)
        for part, values in zip(weights, (vp_ref[...], vs_ref[...], vn_ref[0]))
    )
    sum_ref[...] = row_sum.reshape(count, heads, width)
    stat_ref[...] = stat_rows(row_max, row_total, row_sum.shape).reshape(count, heads, width)
    lane = lax.broadcasted_iota(jnp.int32, (heads, HALF), 1)
    for place in range(count):
        total = stat_ref[place, :, 1:2]
        rest = jnp.broadcast_to(stat_ref[place, :, 0:1] + jnp.log(total), (heads, HALF))
        terms = jnp.zeros((heads, HALF), jnp.float32)
        for term in range(TERMS):
            rounded = rest.astype(jnp.bfloat16).astype(jnp.float32)
            terms = jnp.where(lane == term, rounded, terms)
            rest = rest - rounded
        put(part_ref, (place,), jnp.concatenate([sum_ref[place] / total, terms], axis=1))


def attend(lengths, arrived, *operands):
    count, heads, width = arrived.shape
    return pl.pallas_call(
        attention_kernel,
        out_shape=jax.ShapeDtypeStruct((count, *slot(heads, width + HALF)), jnp.bfloat16),
        scratch_shapes=[pltpu.VMEM(arrived.shape, jnp.float32)] * 2,
        compiler_params=pltpu.CompilerParams(vmem_limit_bytes=24 * MIB),
        cost_estimate=COST,
    )(lengths, arrived, *operands)


def join_kernel(part_ref, copies_ref):
    logs, shares = [], []
    for source in range(part_ref.shape[0]):
        share, terms = joined(*(part_ref[source, part] for part in range(3)))
        shares.append(share)
        logs.append(jnp.sum(terms[:, :TERMS], axis=1, keepdims=True))
    largest = functools.reduce(jnp.maximum, logs)
    factors = [jnp.exp(log - largest) for log in logs]
    summed = sum(share * factor for share, factor in zip(shares, factors))
    attention = (summed / sum(factors)).astype(jnp.bfloat16)
    for place in range(copies_ref.shape[0]):
        copies_ref[place] = attention


def join_partials(parts, shape):
    return pl.pallas_call(
        join_kernel,
        out_shape=jax.ShapeDtypeStruct(shape, jnp.bfloat16),
        compiler_params=pltpu.CompilerParams(vmem_limit_bytes=8 * MIB),
        cost_estimate=COST,
    )(parts)


def project_kernel(order, rows_ref, w_ref, residual_ref, out_ref, copies_ref, wide_ref):
    devices, heads, width = rows_ref.shape
    completions = residual_ref.shape[0]
    all_heads = devices * heads // completions
    for place, device in enumerate(order):
        wide_ref[device * heads : (device + 1) * heads] = rows_ref[place].astype(jnp.float32)
    rows = [wide_ref[pl.ds(head, completions, stride=all_heads), :] for head in range(all_heads)]
    rows = jnp.concatenate([row.astype(jnp.bfloat16) for row in rows], axis=1)
    hidden = (residual_ref[...].astype(jnp.float32) + dot_rows(rows, w_ref[...])).astype(jnp.bfloat16)
    out_ref[...] = hidden
    if copies_ref.ndim == 4:
        put_turned(copies_ref, hidden.astype(jnp.float32))
    else:
        put(copies_ref, range(copies_ref.shape[0]), hidden)


def project(order, rows, w_out, residual):
    devices, heads, width = rows.shape
    return pl.pallas_call(
        functools.partial(project_kernel, order),
        out_shape=(
            jax.ShapeDtypeStruct(residual.shape, jnp.bfloat16),
            jax.ShapeDtypeStruct((devices, *slot(*residual.shape)), jnp.bfloat16),
        ),
        scratch_shapes=[pltpu.VMEM((devices * heads, width), jnp.float32)],
        compiler_params=pltpu.CompilerParams(vmem_limit_bytes=12 * MIB),
        cost_estimate=COST,
    )(rows, w_out, residual)


def forward_kernel(
    order, pieces_ref, gain_ref, copies_ref, gate_ref, up_ref, down_ref, out_ref, attention_hbm, state_ref, sem
):
    keep = pltpu.make_async_copy(copies_ref.at[0], attention_hbm, sem)
    keep.start()
    devices = pieces_ref.shape[0]
    columns = gain_ref.shape[0] // devices
    if pieces_ref.ndim == 4:
        state = whole_state(pieces_ref, order, columns)
    else:
        for place, device in enumerate(order):
            columns_of = slice(device * columns, (device + 1) * columns)
            state_ref[:, columns_of] = pieces_ref[place].astype(jnp.float32)
        state = state_ref[...]
    mean_square = jnp.mean(state * state, axis=-1, keepdims=True)
    gain = gain_ref[...].reshape(1, devices * columns)
    normed = (state * lax.rsqrt(mean_square + NORM_EPSILON) * gain).astype(jnp.bfloat16)
    units = gate_ref.shape[0]
    count = CHUNKS if units % (16 * CHUNKS) == 0 else 1
    size = units // count
    features = normed.shape[1]
    parts = PARTS if features % (LANES * PARTS) == 0 else 1
    cuts = [slice(part * (features // parts), (part + 1) * (features // parts)) for part in range(parts)]
    shares = [0.0] * parts
    ready = None
    for chunk in range(count + 1):
        rows = slice(chunk * size, (chunk + 1) * size)
        gate_values = up_values = 0.0
        for part, cut in enumerate(cuts):
            if chunk < count:
                up_values += dot_rows(normed[:, cut], up_ref[rows, cut])
                gate_values += dot_rows(gate_ref[rows, cut], normed[:, cut])
            if ready is not None:
                activated, held = ready
                shares[part] += jnp.dot(
                    activated, down_ref[held, cut], preferred_element_type=jnp.float32
                )
        if chunk < count:
            activated = jax.nn.gelu(gate_values.T, approximate=True) * up_values
            ready = activated.astype(jnp.bfloat16), rows
    share = jnp.concatenate(shares, axis=1)
    if pieces_ref.ndim == 4:
        put_columns(out_ref, order, share, columns)
    else:
        for place, device in enumerate(order):
            put(out_ref, (place,), share[:, device * columns : (device + 1) * columns])
    keep.wait()


def forward(order, pieces, completions, gain, copies, *weights):
    return pl.pallas_call(
        functools.partial(forward_kernel, order),
        out_shape=(
            jax.ShapeDtypeStruct(pieces.shape, jnp.bfloat16),
            jax.ShapeDtypeStruct(copies.shape[1:], jnp.bfloat16),
        ),
        out_specs=(pl.BlockSpec(memory_space=pltpu.VMEM), pl.BlockSpec(memory_space=pl.ANY)),
        scratch_shapes=[
            pltpu.VMEM((completions, gain.shape[0]), jnp.float32),
            pltpu.SemaphoreType.DMA,
        ],
        compiler_params=pltpu.CompilerParams(vmem_limit_bytes=8 * MIB),
        cost_estimate=COST,
    )(pieces, gain, copies, *weights)


def total_kernel(shares_ref, hidden_ref, out_ref):
    summed = jnp.sum(shares_ref[...].astype(jnp.float32), axis=0)
    if shares_ref.ndim == 4:
        columns = hidden_ref.shape[1]
        low, rest = (turn(part, columns, back=True) for part in joined(*summed))
        summed = jnp.concatenate([low, rest[:, : columns - LANES]], axis=1)
    out_ref[...] = (hidden_ref[...].astype(jnp.float32) + summed).astype(jnp.bfloat16)


def total(shares, hidden):
    return pl.pallas_call(
        total_kernel,
        out_shape=jax.ShapeDtypeStruct(hidden.shape, jnp.bfloat16),
        compiler_params=pltpu.CompilerParams(vmem_limit_bytes=16 * MIB),
    )(shares, hidden)


def listed(ctx_count, groups):
    order = (0, 1, 4, 5, 6, 7, 2, 3) if ctx_count == 8 else range(ctx_count)
    return [ctx * groups + group for ctx in order for group in range(groups)]


def exchange(copies, axes=BOTH):
    groups = None
    if axes == BOTH:
        groups = [listed(lax.axis_size("ctx"), lax.axis_size("head"))]
    return lax.all_to_all(
        copies, axes, split_axis=0, concat_axis=0, tiled=True, axis_index_groups=groups
    )


def body(
    queries,
    k_new,
    v_new,
    k_suffix,
    v_suffix,
    lengths,
    k_prefix,
    v_prefix,
    w_out,
    residual,
    norm_gain,
    w_gate,
    w_up,
    w_down,
):
    ctx_count = lax.axis_size("ctx")
    devices = ctx_count * lax.axis_size("head")
    copies, own_length = spread(lengths, queries, ctx_count)
    arrived = exchange(copies, "ctx")
    rows_of = lambda values: values.reshape(-1, values.shape[-1])
    parts = attend(
        own_length, arrived, k_new, v_new, *map(rows_of, (k_suffix, v_suffix, k_prefix, v_prefix))
    )
    copies = join_partials(exchange(parts, "ctx"), (devices, *queries.shape[1:]))
    order = listed(ctx_count, devices // ctx_count)
    hidden_part, hidden_copies = project(order, exchange(copies), w_out.T, residual)
    shares, attention = forward(
        order, exchange(hidden_copies), residual.shape[0], norm_gain, copies, w_gate.T, w_up.T, w_down
    )
    return (attention[None], total(exchange(shares), hidden_part))


def solution(mesh):
    placed = (
        P("ctx", "head", None),
        P("ctx", "head", None),
        P("ctx", "head", None),
        P("ctx", None, "head", None),
        P("ctx", None, "head", None),
        P("ctx"),
        P("ctx", "head", None),
        P("ctx", "head", None),
        P(None, BOTH),
        P(None, BOTH),
        P(),
        P(None, BOTH),
        P(None, BOTH),
        P(BOTH, None),
    )
    return jax.shard_map(
        body,
        mesh=mesh,
        in_specs=placed,
        out_specs=(P("ctx", "head", None), P(None, BOTH)),
        check_vma=False,
    )
```

```python
import functools

import jax
import jax.numpy as jnp
from jax import lax
from jax.experimental import pallas as pl
from jax.experimental.pallas import tpu as pltpu
from jax.sharding import PartitionSpec as P

SCORE_SCALE = 168.0 ** (-0.5)
NORM_EPSILON = 1e-06
MASKED = -1e30
MIB = 1024 * 1024
COST = pl.CostEstimate(flops=10**10, bytes_accessed=MIB, transcendentals=10**6)
TERMS = 3
CHUNKS = 3
BLOCK_ROWS = 1024
LANES = 128
HALF = LANES // 2
BOTH = ("ctx", "head")


def head_bias(rows, columns, heads, kv_heads):
    group = heads // kv_heads
    tile = (heads, 128)
    row = lax.broadcasted_iota(jnp.int32, tile, 0)
    column = lax.broadcasted_iota(jnp.int32, tile, 1)
    bias = jnp.where(row // group == lax.rem(column, kv_heads), 0.0, MASKED)
    return jnp.tile(bias, (rows // heads, columns // 128))


def in_hbm(operand):
    return pltpu.with_memory_space_constraint(operand, pltpu.HBM)


def dot_rows(left, right):
    return lax.dot_general(left, right, (((1,), (1,)), ((), ())), preferred_element_type=jnp.float32)


def stat_rows(row_max, row_total, shape):
    lane = lax.broadcasted_iota(jnp.int32, shape, 1)
    return jnp.where(lane == 0, row_max, row_total)


def slot(rows, columns):
    if rows == 8 and LANES < columns <= LANES + HALF:
        return 3, 4, LANES
    return rows, columns


def put(ref, places, value):
    if ref.ndim == 3:
        for place in places:
            ref[place] = value.astype(ref.dtype)
        return
    rows, columns = value.shape
    rest = value[:, LANES:]
    if columns < LANES + HALF:
        rest = jnp.concatenate([rest, jnp.zeros((rows, LANES + HALF - columns), value.dtype)], axis=1)
    rest = jnp.concatenate([rest[:4], rest[4:]], axis=1)
    pieces = [piece.astype(ref.dtype) for piece in (value[:4, :LANES], value[4:, :LANES], rest)]
    for place in places:
        for part, piece in enumerate(pieces):
            ref[place, part] = piece


def joined(first, second, rest):
    low = jnp.concatenate([first, second], axis=0).astype(jnp.float32)
    rest = rest.astype(jnp.float32)
    return low, jnp.concatenate([rest, pltpu.roll(rest, HALF, 1)], axis=0)


def turn(value, columns, back=False):
    device = lax.axis_index("ctx") * lax.axis_size("head") + lax.axis_index("head")
    offset = lax.rem(device * columns, LANES)
    return pltpu.roll(value, lax.rem(LANES - offset, LANES) if back else offset, 1)


def put_turned(ref, value):
    rows, columns = value.shape
    rest = jnp.concatenate(
        [value[:, LANES:], jnp.zeros((rows, 2 * LANES - columns), value.dtype)], axis=1
    )
    low, rest = turn(value[:, :LANES], columns), turn(rest, columns)
    rest = rest[:4] + pltpu.roll(rest, HALF, 1)[4:]
    pieces = [piece.astype(ref.dtype) for piece in (low[:4], low[4:], rest)]
    for place in range(ref.shape[0]):
        for part, piece in enumerate(pieces):
            ref[place, part] = piece


def whole_state(pieces_ref, order, columns):
    lane = lax.broadcasted_iota(jnp.int32, (8, LANES), 1)
    tiles = {}
    for device in range(len(order)):
        place = order.index(device)
        low, rest = joined(*(pieces_ref[place, part] for part in range(3)))
        first, offset = divmod(device * columns, LANES)
        tiles[first] = jnp.where(lane >= offset, low, tiles[first]) if offset else low
        tiles[first + 1] = jnp.where(lane < offset, low, rest)
        if offset + columns - LANES > LANES:
            tiles[first + 2] = rest
    return jnp.concatenate([tiles[place] for place in range(len(order) * columns // LANES)], axis=1)


def put_columns(ref, order, share, columns):
    lane = lax.broadcasted_iota(jnp.int32, (8, LANES), 1)
    tile = lambda place: share[:, place * LANES : (place + 1) * LANES]
    for device in range(len(order)):
        first, offset = divmod(device * columns, LANES)
        end = offset + columns - LANES
        low = jnp.where(lane >= offset, tile(first), tile(first + 1)) if offset else tile(first)
        rest = tile(first + 1)
        own = (lane >= offset) & (lane < end)
        if end > LANES:
            rest = jnp.where(lane >= offset, rest, tile(first + 2))
            own = (lane >= offset) | (lane < end - LANES)
        rest = jnp.where(own[:4], rest[:4], pltpu.roll(rest, HALF, 1)[4:])
        place = order.index(device)
        for part, piece in enumerate((low[:4], low[4:], rest)):
            ref[place, part] = piece.astype(ref.dtype)


def spread_kernel(length_ref, source_hbm, copies_ref, lengths_ref, source_ref, sem):
    load = pltpu.make_async_copy(source_hbm, source_ref, sem)
    load.start()
    lengths_ref[...] = jnp.full(lengths_ref.shape, length_ref[0], jnp.int32)
    load.wait()
    for place in range(copies_ref.shape[0]):
        copies_ref[place] = source_ref[0]


def spread(lengths, value, count):
    return pl.pallas_call(
        spread_kernel,
        out_shape=(
            jax.ShapeDtypeStruct((count, *value.shape[1:]), value.dtype),
            jax.ShapeDtypeStruct(value.shape[1:], jnp.int32),
        ),
        in_specs=[pl.BlockSpec(memory_space=pltpu.SMEM), pl.BlockSpec(memory_space=pl.ANY)],
        scratch_shapes=[pltpu.VMEM(value.shape, value.dtype), pltpu.SemaphoreType.DMA],
        compiler_params=pltpu.CompilerParams(vmem_limit_bytes=4 * MIB),
        cost_estimate=COST,
    )(lengths, in_hbm(value))


def attention_kernel(
    length_ref, arrived_ref, kn_ref, vn_ref, ks_ref, vs_ref, kp_ref, vp_ref, part_ref, sum_ref, stat_ref
):
    count, heads, width = arrived_ref.shape
    kv_heads = kn_ref.shape[1]
    rows = count * heads
    queries = arrived_ref[...].reshape(rows, width)
    row = lax.broadcasted_iota(jnp.int32, (rows, LANES), 0)
    own = jnp.where(row // heads == lax.axis_index("ctx"), 0.0, MASKED)
    prompt_rows = kp_ref.shape[0]
    size = BLOCK_ROWS if prompt_rows % BLOCK_ROWS == 0 else prompt_rows
    prompt_bias = head_bias(rows, size, heads, kv_heads)
    blocks = []
    for start in range(0, prompt_rows, size):
        block = slice(start, start + size)
        scores = SCORE_SCALE * dot_rows(queries, kp_ref[block]) + prompt_bias
        blocks.append((scores, vp_ref[block], None, None))
    cached_scores = SCORE_SCALE * dot_rows(queries, ks_ref[...])
    column = lax.broadcasted_iota(jnp.int32, (heads, cached_scores.shape[1]), 1)
    unused = jnp.where(column // kv_heads < length_ref[:, 0:1], 0.0, MASKED)
    bias = head_bias(heads, cached_scores.shape[1], heads, kv_heads) + unused
    bias = jnp.tile(bias, (count, 1)) + own[:, 0:1]
    cached_scores = cached_scores + bias
    new_scores = SCORE_SCALE * dot_rows(queries, kn_ref[0])
    new_scores = new_scores + head_bias(rows, LANES, heads, kv_heads)[:, :kv_heads] + own[:, :kv_heads]
    blocks.append((cached_scores, vs_ref[...], new_scores, vn_ref[0]))
    parts = []
    for block_scores, values, more_scores, more_values in blocks:
        block_max = jnp.max(block_scores, axis=1, keepdims=True)
        if more_scores is not None:
            block_max = jnp.maximum(block_max, jnp.max(more_scores, axis=1, keepdims=True))
        weights = jnp.exp(block_scores - block_max).astype(jnp.bfloat16)
        block_total = jnp.sum(weights.astype(jnp.float32), axis=1, keepdims=True)
        block_sum = jnp.dot(weights, values, preferred_element_type=jnp.float32)
        if more_scores is not None:
            weights = jnp.exp(more_scores - block_max).astype(jnp.bfloat16)
            block_total += jnp.sum(weights.astype(jnp.float32), axis=1, keepdims=True)
            block_sum += jnp.dot(weights, more_values, preferred_element_type=jnp.float32)
        parts.append((block_max, block_total, block_sum))
    row_max = functools.reduce(jnp.maximum, [part[0] for part in parts])
    factors = [jnp.exp(part[0] - row_max) for part in parts]
    row_total = sum(part[1] * factor for part, factor in zip(parts, factors))
    row_sum = sum(part[2] * factor for part, factor in zip(parts, factors))
    sum_ref[...] = row_sum.reshape(count, heads, width)
    stat_ref[...] = stat_rows(row_max, row_total, row_sum.shape).reshape(count, heads, width)
    lane = lax.broadcasted_iota(jnp.int32, (heads, HALF), 1)
    for place in range(count):
        total = stat_ref[place, :, 1:2]
        rest = jnp.broadcast_to(stat_ref[place, :, 0:1] + jnp.log(total), (heads, HALF))
        terms = jnp.zeros((heads, HALF), jnp.float32)
        for term in range(TERMS):
            rounded = rest.astype(jnp.bfloat16).astype(jnp.float32)
            terms = jnp.where(lane == term, rounded, terms)
            rest = rest - rounded
        put(part_ref, (place,), jnp.concatenate([sum_ref[place] / total, terms], axis=1))


def attend(lengths, arrived, *operands):
    count, heads, width = arrived.shape
    return pl.pallas_call(
        attention_kernel,
        out_shape=jax.ShapeDtypeStruct((count, *slot(heads, width + HALF)), jnp.bfloat16),
        scratch_shapes=[pltpu.VMEM(arrived.shape, jnp.float32)] * 2,
        compiler_params=pltpu.CompilerParams(vmem_limit_bytes=24 * MIB),
        cost_estimate=COST,
    )(lengths, arrived, *operands)


def join_kernel(part_ref, copies_ref):
    logs, shares = [], []
    for source in range(part_ref.shape[0]):
        share, terms = joined(*(part_ref[source, part] for part in range(3)))
        shares.append(share)
        logs.append(jnp.sum(terms[:, :TERMS], axis=1, keepdims=True))
    largest = functools.reduce(jnp.maximum, logs)
    factors = [jnp.exp(log - largest) for log in logs]
    summed = sum(share * factor for share, factor in zip(shares, factors))
    attention = (summed / sum(factors)).astype(jnp.bfloat16)
    for place in range(copies_ref.shape[0]):
        copies_ref[place] = attention


def join_partials(parts, shape):
    return pl.pallas_call(
        join_kernel,
        out_shape=jax.ShapeDtypeStruct(shape, jnp.bfloat16),
        compiler_params=pltpu.CompilerParams(vmem_limit_bytes=8 * MIB),
        cost_estimate=COST,
    )(parts)


def project_kernel(order, rows_ref, w_ref, residual_ref, out_ref, copies_ref, wide_ref):
    devices, heads, width = rows_ref.shape
    completions = residual_ref.shape[0]
    all_heads = devices * heads // completions
    for place, device in enumerate(order):
        wide_ref[device * heads : (device + 1) * heads] = rows_ref[place].astype(jnp.float32)
    rows = [wide_ref[pl.ds(head, completions, stride=all_heads), :] for head in range(all_heads)]
    rows = jnp.concatenate([row.astype(jnp.bfloat16) for row in rows], axis=1)
    held = w_ref.shape[0] // 32 * 16
    projected = dot_rows(w_ref[held:], rows).T
    if held:
        projected = jnp.concatenate([dot_rows(rows, w_ref[:held]), projected], axis=1)
    hidden = (residual_ref[...].astype(jnp.float32) + projected).astype(jnp.bfloat16)
    out_ref[...] = hidden
    if copies_ref.ndim == 4:
        put_turned(copies_ref, hidden.astype(jnp.float32))
    else:
        put(copies_ref, range(copies_ref.shape[0]), hidden)


def project(order, rows, w_out, residual):
    devices, heads, width = rows.shape
    return pl.pallas_call(
        functools.partial(project_kernel, order),
        out_shape=(
            jax.ShapeDtypeStruct(residual.shape, jnp.bfloat16),
            jax.ShapeDtypeStruct((devices, *slot(*residual.shape)), jnp.bfloat16),
        ),
        scratch_shapes=[pltpu.VMEM((devices * heads, width), jnp.float32)],
        compiler_params=pltpu.CompilerParams(vmem_limit_bytes=12 * MIB),
        cost_estimate=COST,
    )(rows, w_out, residual)


def forward_kernel(
    order, pieces_ref, gain_ref, copies_ref, gate_ref, up_ref, down_ref, out_ref, attention_hbm, state_ref, sem
):
    keep = pltpu.make_async_copy(copies_ref.at[0], attention_hbm, sem)
    keep.start()
    devices = pieces_ref.shape[0]
    columns = gain_ref.shape[0] // devices
    if pieces_ref.ndim == 4:
        state = whole_state(pieces_ref, order, columns)
    else:
        for place, device in enumerate(order):
            columns_of = slice(device * columns, (device + 1) * columns)
            state_ref[:, columns_of] = pieces_ref[place].astype(jnp.float32)
        state = state_ref[...]
    mean_square = jnp.mean(state * state, axis=-1, keepdims=True)
    gain = gain_ref[...].reshape(1, devices * columns)
    normed = (state * lax.rsqrt(mean_square + NORM_EPSILON) * gain).astype(jnp.bfloat16)
    units = gate_ref.shape[0]
    count = CHUNKS if units % (16 * CHUNKS) == 0 else 1
    size = units // count
    share = jnp.zeros((normed.shape[0], down_ref.shape[1]), jnp.float32)
    ready = None
    for chunk in range(count + 1):
        if chunk < count:
            rows = slice(chunk * size, (chunk + 1) * size)
            gate_values = dot_rows(gate_ref[rows], normed)
            up_values = dot_rows(normed, up_ref[rows])
        if ready is not None:
            activated, held = ready
            share += jnp.dot(activated, down_ref[held], preferred_element_type=jnp.float32)
        if chunk < count:
            activated = jax.nn.gelu(gate_values.T, approximate=True) * up_values
            ready = activated.astype(jnp.bfloat16), rows
    if pieces_ref.ndim == 4:
        put_columns(out_ref, order, share, columns)
    else:
        for place, device in enumerate(order):
            put(out_ref, (place,), share[:, device * columns : (device + 1) * columns])
    keep.wait()


def forward(order, pieces, completions, gain, copies, *weights):
    return pl.pallas_call(
        functools.partial(forward_kernel, order),
        out_shape=(
            jax.ShapeDtypeStruct(pieces.shape, jnp.bfloat16),
            jax.ShapeDtypeStruct(copies.shape[1:], jnp.bfloat16),
        ),
        out_specs=(pl.BlockSpec(memory_space=pltpu.VMEM), pl.BlockSpec(memory_space=pl.ANY)),
        scratch_shapes=[
            pltpu.VMEM((completions, gain.shape[0]), jnp.float32),
            pltpu.SemaphoreType.DMA,
        ],
        compiler_params=pltpu.CompilerParams(vmem_limit_bytes=8 * MIB),
        cost_estimate=COST,
    )(pieces, gain, copies, *weights)


def total_kernel(shares_ref, hidden_ref, out_ref):
    summed = jnp.sum(shares_ref[...].astype(jnp.float32), axis=0)
    if shares_ref.ndim == 4:
        columns = hidden_ref.shape[1]
        low, rest = (turn(part, columns, back=True) for part in joined(*summed))
        summed = jnp.concatenate([low, rest[:, : columns - LANES]], axis=1)
    out_ref[...] = (hidden_ref[...].astype(jnp.float32) + summed).astype(jnp.bfloat16)


def total(shares, hidden):
    return pl.pallas_call(
        total_kernel,
        out_shape=jax.ShapeDtypeStruct(hidden.shape, jnp.bfloat16),
        compiler_params=pltpu.CompilerParams(vmem_limit_bytes=16 * MIB),
    )(shares, hidden)


def listed(ctx_count, groups):
    order = (0, 1, 4, 5, 6, 7, 2, 3) if ctx_count == 8 else range(ctx_count)
    return [ctx * groups + group for ctx in order for group in range(groups)]


def exchange(copies, axes=BOTH):
    groups = None
    if axes == BOTH:
        groups = [listed(lax.axis_size("ctx"), lax.axis_size("head"))]
    return lax.all_to_all(
        copies, axes, split_axis=0, concat_axis=0, tiled=True, axis_index_groups=groups
    )


def body(
    queries,
    k_new,
    v_new,
    k_suffix,
    v_suffix,
    lengths,
    k_prefix,
    v_prefix,
    w_out,
    residual,
    norm_gain,
    w_gate,
    w_up,
    w_down,
):
    ctx_count = lax.axis_size("ctx")
    devices = ctx_count * lax.axis_size("head")
    copies, own_length = spread(lengths, queries, ctx_count)
    arrived = exchange(copies, "ctx")
    rows_of = lambda values: values.reshape(-1, values.shape[-1])
    parts = attend(
        own_length, arrived, k_new, v_new, *map(rows_of, (k_suffix, v_suffix, k_prefix, v_prefix))
    )
    copies = join_partials(exchange(parts, "ctx"), (devices, *queries.shape[1:]))
    order = listed(ctx_count, devices // ctx_count)
    hidden_part, hidden_copies = project(order, exchange(copies), w_out.T, residual)
    shares, attention = forward(
        order, exchange(hidden_copies), residual.shape[0], norm_gain, copies, w_gate.T, w_up.T, w_down
    )
    return (attention[None], total(exchange(shares), hidden_part))


def solution(mesh):
    placed = (
        P("ctx", "head", None),
        P("ctx", "head", None),
        P("ctx", "head", None),
        P("ctx", None, "head", None),
        P("ctx", None, "head", None),
        P("ctx"),
        P("ctx", "head", None),
        P("ctx", "head", None),
        P(None, BOTH),
        P(None, BOTH),
        P(),
        P(None, BOTH),
        P(None, BOTH),
        P(BOTH, None),
    )
    return jax.shard_map(
        body,
        mesh=mesh,
        in_specs=placed,
        out_specs=(P("ctx", "head", None), P(None, BOTH)),
        check_vma=False,
    )
```

```python
import functools

import jax
import jax.numpy as jnp
from jax import lax
from jax.experimental import pallas as pl
from jax.experimental.pallas import tpu as pltpu
from jax.sharding import PartitionSpec as P

SCORE_SCALE = 168.0 ** (-0.5)
NORM_EPSILON = 1e-06
MASKED = -1e30
MIB = 1024 * 1024
COST = pl.CostEstimate(flops=10**10, bytes_accessed=MIB, transcendentals=10**6)
TERMS = 3
CHUNKS = 3
BLOCK_ROWS = 1024
LANES = 128
HALF = LANES // 2
BOTH = ("ctx", "head")


def head_bias(rows, columns, heads, kv_heads):
    group = heads // kv_heads
    tile = (heads, 128)
    row = lax.broadcasted_iota(jnp.int32, tile, 0)
    column = lax.broadcasted_iota(jnp.int32, tile, 1)
    bias = jnp.where(row // group == lax.rem(column, kv_heads), 0.0, MASKED)
    return jnp.tile(bias, (rows // heads, columns // 128))


def in_hbm(operand):
    return pltpu.with_memory_space_constraint(operand, pltpu.HBM)


def dot_rows(left, right):
    return lax.dot_general(left, right, (((1,), (1,)), ((), ())), preferred_element_type=jnp.float32)


def stat_rows(row_max, row_total, shape):
    lane = lax.broadcasted_iota(jnp.int32, shape, 1)
    return jnp.where(lane == 0, row_max, row_total)


def slot(rows, columns):
    if rows == 8 and LANES < columns <= LANES + HALF:
        return 3, 4, LANES
    return rows, columns


def put(ref, places, value):
    if ref.ndim == 3:
        for place in places:
            ref[place] = value.astype(ref.dtype)
        return
    rows, columns = value.shape
    rest = value[:, LANES:]
    if columns < LANES + HALF:
        rest = jnp.concatenate([rest, jnp.zeros((rows, LANES + HALF - columns), value.dtype)], axis=1)
    rest = jnp.concatenate([rest[:4], rest[4:]], axis=1)
    pieces = [piece.astype(ref.dtype) for piece in (value[:4, :LANES], value[4:, :LANES], rest)]
    for place in places:
        for part, piece in enumerate(pieces):
            ref[place, part] = piece


def joined(first, second, rest):
    low = jnp.concatenate([first, second], axis=0).astype(jnp.float32)
    rest = rest.astype(jnp.float32)
    return low, jnp.concatenate([rest, pltpu.roll(rest, HALF, 1)], axis=0)


def turn(value, columns, back=False):
    device = lax.axis_index("ctx") * lax.axis_size("head") + lax.axis_index("head")
    offset = lax.rem(device * columns, LANES)
    return pltpu.roll(value, lax.rem(LANES - offset, LANES) if back else offset, 1)


def put_turned(ref, value):
    rows, columns = value.shape
    rest = jnp.concatenate(
        [value[:, LANES:], jnp.zeros((rows, 2 * LANES - columns), value.dtype)], axis=1
    )
    low, rest = turn(value[:, :LANES], columns), turn(rest, columns)
    rest = rest[:4] + pltpu.roll(rest, HALF, 1)[4:]
    pieces = [piece.astype(ref.dtype) for piece in (low[:4], low[4:], rest)]
    for place in range(ref.shape[0]):
        for part, piece in enumerate(pieces):
            ref[place, part] = piece


def whole_state(pieces_ref, order, columns):
    lane = lax.broadcasted_iota(jnp.int32, (8, LANES), 1)
    tiles = {}
    for device in range(len(order)):
        place = order.index(device)
        low, rest = joined(*(pieces_ref[place, part] for part in range(3)))
        first, offset = divmod(device * columns, LANES)
        tiles[first] = jnp.where(lane >= offset, low, tiles[first]) if offset else low
        tiles[first + 1] = jnp.where(lane < offset, low, rest)
        if offset + columns - LANES > LANES:
            tiles[first + 2] = rest
    return jnp.concatenate([tiles[place] for place in range(len(order) * columns // LANES)], axis=1)


def put_columns(ref, order, share, columns):
    lane = lax.broadcasted_iota(jnp.int32, (8, LANES), 1)
    tile = lambda place: share[:, place * LANES : (place + 1) * LANES]
    for device in range(len(order)):
        first, offset = divmod(device * columns, LANES)
        end = offset + columns - LANES
        low = jnp.where(lane >= offset, tile(first), tile(first + 1)) if offset else tile(first)
        rest = tile(first + 1)
        own = (lane >= offset) & (lane < end)
        if end > LANES:
            rest = jnp.where(lane >= offset, rest, tile(first + 2))
            own = (lane >= offset) | (lane < end - LANES)
        rest = jnp.where(own[:4], rest[:4], pltpu.roll(rest, HALF, 1)[4:])
        place = order.index(device)
        for part, piece in enumerate((low[:4], low[4:], rest)):
            ref[place, part] = piece.astype(ref.dtype)


def spread_kernel(length_ref, source_hbm, copies_ref, lengths_ref, source_ref, sem):
    load = pltpu.make_async_copy(source_hbm, source_ref, sem)
    load.start()
    lengths_ref[...] = jnp.full(lengths_ref.shape, length_ref[0], jnp.int32)
    load.wait()
    for place in range(copies_ref.shape[0]):
        copies_ref[place] = source_ref[0]


def spread(lengths, value, count):
    return pl.pallas_call(
        spread_kernel,
        out_shape=(
            jax.ShapeDtypeStruct((count, *value.shape[1:]), value.dtype),
            jax.ShapeDtypeStruct(value.shape[1:], jnp.int32),
        ),
        in_specs=[pl.BlockSpec(memory_space=pltpu.SMEM), pl.BlockSpec(memory_space=pl.ANY)],
        scratch_shapes=[pltpu.VMEM(value.shape, value.dtype), pltpu.SemaphoreType.DMA],
        compiler_params=pltpu.CompilerParams(vmem_limit_bytes=4 * MIB),
        cost_estimate=COST,
    )(lengths, in_hbm(value))


def attention_kernel(
    length_ref, arrived_ref, kn_ref, vn_ref, ks_ref, vs_ref, kp_ref, vp_ref, part_ref, sum_ref, stat_ref
):
    count, heads, width = arrived_ref.shape
    kv_heads = kn_ref.shape[1]
    rows = count * heads
    queries = arrived_ref[...].reshape(rows, width)
    row = lax.broadcasted_iota(jnp.int32, (rows, LANES), 0)
    own = jnp.where(row // heads == lax.axis_index("ctx"), 0.0, MASKED)
    prompt_rows = kp_ref.shape[0]
    size = BLOCK_ROWS if prompt_rows % BLOCK_ROWS == 0 else prompt_rows
    prompt_bias = head_bias(rows, size, heads, kv_heads)
    blocks = []
    for start in range(0, prompt_rows, size):
        block = slice(start, start + size)
        scores = SCORE_SCALE * dot_rows(queries, kp_ref[block]) + prompt_bias
        blocks.append((scores, vp_ref[block], None, None))
    cached_scores = SCORE_SCALE * dot_rows(queries, ks_ref[...])
    column = lax.broadcasted_iota(jnp.int32, (heads, cached_scores.shape[1]), 1)
    unused = jnp.where(column // kv_heads < length_ref[:, 0:1], 0.0, MASKED)
    bias = head_bias(heads, cached_scores.shape[1], heads, kv_heads) + unused
    bias = jnp.tile(bias, (count, 1)) + own[:, 0:1]
    cached_scores = cached_scores + bias
    new_scores = SCORE_SCALE * dot_rows(queries, kn_ref[0])
    new_scores = new_scores + head_bias(rows, LANES, heads, kv_heads)[:, :kv_heads] + own[:, :kv_heads]
    blocks.append((cached_scores, vs_ref[...], new_scores, vn_ref[0]))
    parts = []
    for block_scores, values, more_scores, more_values in blocks:
        block_max = jnp.max(block_scores, axis=1, keepdims=True)
        if more_scores is not None:
            block_max = jnp.maximum(block_max, jnp.max(more_scores, axis=1, keepdims=True))
        weights = jnp.exp(block_scores - block_max).astype(jnp.bfloat16)
        block_total = jnp.sum(weights.astype(jnp.float32), axis=1, keepdims=True)
        block_sum = jnp.dot(weights, values, preferred_element_type=jnp.float32)
        if more_scores is not None:
            weights = jnp.exp(more_scores - block_max).astype(jnp.bfloat16)
            block_total += jnp.sum(weights.astype(jnp.float32), axis=1, keepdims=True)
            block_sum += jnp.dot(weights, more_values, preferred_element_type=jnp.float32)
        parts.append((block_max, block_total, block_sum))
    row_max = functools.reduce(jnp.maximum, [part[0] for part in parts])
    factors = [jnp.exp(part[0] - row_max) for part in parts]
    row_total = sum(part[1] * factor for part, factor in zip(parts, factors))
    row_sum = sum(part[2] * factor for part, factor in zip(parts, factors))
    sum_ref[...] = row_sum.reshape(count, heads, width)
    stat_ref[...] = stat_rows(row_max, row_total, row_sum.shape).reshape(count, heads, width)
    lane = lax.broadcasted_iota(jnp.int32, (heads, HALF), 1)
    for place in range(count):
        total = stat_ref[place, :, 1:2]
        rest = jnp.broadcast_to(stat_ref[place, :, 0:1] + jnp.log(total), (heads, HALF))
        terms = jnp.zeros((heads, HALF), jnp.float32)
        for term in range(TERMS):
            rounded = rest.astype(jnp.bfloat16).astype(jnp.float32)
            terms = jnp.where(lane == term, rounded, terms)
            rest = rest - rounded
        put(part_ref, (place,), jnp.concatenate([sum_ref[place] / total, terms], axis=1))


def attend(lengths, arrived, *operands):
    count, heads, width = arrived.shape
    return pl.pallas_call(
        attention_kernel,
        out_shape=jax.ShapeDtypeStruct((count, *slot(heads, width + HALF)), jnp.bfloat16),
        scratch_shapes=[pltpu.VMEM(arrived.shape, jnp.float32)] * 2,
        compiler_params=pltpu.CompilerParams(vmem_limit_bytes=24 * MIB),
        cost_estimate=COST,
    )(lengths, arrived, *operands)


def join_kernel(part_ref, copies_ref):
    logs, shares = [], []
    for source in range(part_ref.shape[0]):
        share, terms = joined(*(part_ref[source, part] for part in range(3)))
        shares.append(share)
        logs.append(jnp.sum(terms[:, :TERMS], axis=1, keepdims=True))
    largest = functools.reduce(jnp.maximum, logs)
    factors = [jnp.exp(log - largest) for log in logs]
    summed = sum(share * factor for share, factor in zip(shares, factors))
    attention = (summed / sum(factors)).astype(jnp.bfloat16)
    for place in range(copies_ref.shape[0]):
        copies_ref[place] = attention


def join_partials(parts, shape):
    return pl.pallas_call(
        join_kernel,
        out_shape=jax.ShapeDtypeStruct(shape, jnp.bfloat16),
        compiler_params=pltpu.CompilerParams(vmem_limit_bytes=8 * MIB),
        cost_estimate=COST,
    )(parts)


def project_kernel(order, rows_ref, w_ref, residual_ref, out_ref, copies_ref, wide_ref):
    devices, heads, width = rows_ref.shape
    completions = residual_ref.shape[0]
    all_heads = devices * heads // completions
    for place, device in enumerate(order):
        wide_ref[device * heads : (device + 1) * heads] = rows_ref[place].astype(jnp.float32)
    rows = [wide_ref[pl.ds(head, completions, stride=all_heads), :] for head in range(all_heads)]
    rows = jnp.concatenate([row.astype(jnp.bfloat16) for row in rows], axis=1)
    projected = dot_rows(rows, w_ref[...])
    hidden = (residual_ref[...].astype(jnp.float32) + projected).astype(jnp.bfloat16)
    out_ref[...] = hidden
    if copies_ref.ndim == 4:
        put_turned(copies_ref, hidden.astype(jnp.float32))
    else:
        put(copies_ref, range(copies_ref.shape[0]), hidden)


def project(order, rows, w_out, residual):
    devices, heads, width = rows.shape
    return pl.pallas_call(
        functools.partial(project_kernel, order),
        out_shape=(
            jax.ShapeDtypeStruct(residual.shape, jnp.bfloat16),
            jax.ShapeDtypeStruct((devices, *slot(*residual.shape)), jnp.bfloat16),
        ),
        scratch_shapes=[pltpu.VMEM((devices * heads, width), jnp.float32)],
        compiler_params=pltpu.CompilerParams(vmem_limit_bytes=12 * MIB),
        cost_estimate=COST,
    )(rows, w_out, residual)


def forward_kernel(
    order, pieces_ref, gain_ref, copies_ref, gate_ref, up_ref, down_ref, out_ref, attention_hbm, state_ref, sem
):
    keep = pltpu.make_async_copy(copies_ref.at[0], attention_hbm, sem)
    keep.start()
    devices = pieces_ref.shape[0]
    columns = gain_ref.shape[0] // devices
    if pieces_ref.ndim == 4:
        state = whole_state(pieces_ref, order, columns)
    else:
        for place, device in enumerate(order):
            columns_of = slice(device * columns, (device + 1) * columns)
            state_ref[:, columns_of] = pieces_ref[place].astype(jnp.float32)
        state = state_ref[...]
    mean_square = jnp.mean(state * state, axis=-1, keepdims=True)
    gain = gain_ref[...].reshape(1, devices * columns)
    normed = (state * lax.rsqrt(mean_square + NORM_EPSILON) * gain).astype(jnp.bfloat16)
    units = gate_ref.shape[0]
    count = CHUNKS if units % (16 * CHUNKS) == 0 else 1
    size = units // count
    share = jnp.zeros((normed.shape[0], down_ref.shape[1]), jnp.float32)
    ready = None
    for chunk in range(count + 1):
        if chunk < count:
            rows = slice(chunk * size, (chunk + 1) * size)
            gate_values = dot_rows(gate_ref[rows], normed)
            if chunk % 2:
                up_values = dot_rows(up_ref[rows], normed).T
            else:
                up_values = dot_rows(normed, up_ref[rows])
        if ready is not None:
            activated, held = ready
            share += jnp.dot(activated, down_ref[held], preferred_element_type=jnp.float32)
        if chunk < count:
            activated = jax.nn.gelu(gate_values.T, approximate=True) * up_values
            ready = activated.astype(jnp.bfloat16), rows
    if pieces_ref.ndim == 4:
        put_columns(out_ref, order, share, columns)
    else:
        for place, device in enumerate(order):
            put(out_ref, (place,), share[:, device * columns : (device + 1) * columns])
    keep.wait()


def forward(order, pieces, completions, gain, copies, *weights):
    return pl.pallas_call(
        functools.partial(forward_kernel, order),
        out_shape=(
            jax.ShapeDtypeStruct(pieces.shape, jnp.bfloat16),
            jax.ShapeDtypeStruct(copies.shape[1:], jnp.bfloat16),
        ),
        out_specs=(pl.BlockSpec(memory_space=pltpu.VMEM), pl.BlockSpec(memory_space=pl.ANY)),
        scratch_shapes=[
            pltpu.VMEM((completions, gain.shape[0]), jnp.float32),
            pltpu.SemaphoreType.DMA,
        ],
        compiler_params=pltpu.CompilerParams(vmem_limit_bytes=8 * MIB),
        cost_estimate=COST,
    )(pieces, gain, copies, *weights)


def total_kernel(shares_ref, hidden_ref, out_ref):
    summed = jnp.sum(shares_ref[...].astype(jnp.float32), axis=0)
    if shares_ref.ndim == 4:
        columns = hidden_ref.shape[1]
        low, rest = (turn(part, columns, back=True) for part in joined(*summed))
        summed = jnp.concatenate([low, rest[:, : columns - LANES]], axis=1)
    out_ref[...] = (hidden_ref[...].astype(jnp.float32) + summed).astype(jnp.bfloat16)


def total(shares, hidden):
    return pl.pallas_call(
        total_kernel,
        out_shape=jax.ShapeDtypeStruct(hidden.shape, jnp.bfloat16),
        compiler_params=pltpu.CompilerParams(vmem_limit_bytes=16 * MIB),
    )(shares, hidden)


def listed(ctx_count, groups):
    order = (0, 1, 4, 5, 6, 7, 2, 3) if ctx_count == 8 else range(ctx_count)
    return [ctx * groups + group for ctx in order for group in range(groups)]


def exchange(copies, axes=BOTH):
    groups = None
    if axes == BOTH:
        groups = [listed(lax.axis_size("ctx"), lax.axis_size("head"))]
    return lax.all_to_all(
        copies, axes, split_axis=0, concat_axis=0, tiled=True, axis_index_groups=groups
    )


def body(
    queries,
    k_new,
    v_new,
    k_suffix,
    v_suffix,
    lengths,
    k_prefix,
    v_prefix,
    w_out,
    residual,
    norm_gain,
    w_gate,
    w_up,
    w_down,
):
    ctx_count = lax.axis_size("ctx")
    devices = ctx_count * lax.axis_size("head")
    copies, own_length = spread(lengths, queries, ctx_count)
    arrived = exchange(copies, "ctx")
    rows_of = lambda values: values.reshape(-1, values.shape[-1])
    parts = attend(
        own_length, arrived, k_new, v_new, *map(rows_of, (k_suffix, v_suffix, k_prefix, v_prefix))
    )
    copies = join_partials(exchange(parts, "ctx"), (devices, *queries.shape[1:]))
    order = listed(ctx_count, devices // ctx_count)
    hidden_part, hidden_copies = project(order, exchange(copies), w_out.T, residual)
    shares, attention = forward(
        order, exchange(hidden_copies), residual.shape[0], norm_gain, copies, w_gate.T, w_up.T, w_down
    )
    return (attention[None], total(exchange(shares), hidden_part))


def solution(mesh):
    placed = (
        P("ctx", "head", None),
        P("ctx", "head", None),
        P("ctx", "head", None),
        P("ctx", None, "head", None),
        P("ctx", None, "head", None),
        P("ctx"),
        P("ctx", "head", None),
        P("ctx", "head", None),
        P(None, BOTH),
        P(None, BOTH),
        P(),
        P(None, BOTH),
        P(None, BOTH),
        P(BOTH, None),
    )
    return jax.shard_map(
        body,
        mesh=mesh,
        in_specs=placed,
        out_specs=(P("ctx", "head", None), P(None, BOTH)),
        check_vma=False,
    )
```

```python
import functools

import jax
import jax.numpy as jnp
from jax import lax
from jax.experimental import pallas as pl
from jax.experimental.pallas import tpu as pltpu
from jax.sharding import PartitionSpec as P

SCORE_SCALE = 168.0 ** (-0.5)
NORM_EPSILON = 1e-06
MASKED = -1e30
MIB = 1024 * 1024
COST = pl.CostEstimate(flops=10**10, bytes_accessed=MIB, transcendentals=10**6)
TERMS = 3
CHUNKS = 3
BLOCK_ROWS = 1024
LANES = 128
HALF = LANES // 2
BOTH = ("ctx", "head")


def head_bias(rows, columns, heads, kv_heads):
    group = heads // kv_heads
    tile = (heads, 128)
    row = lax.broadcasted_iota(jnp.int32, tile, 0)
    column = lax.broadcasted_iota(jnp.int32, tile, 1)
    bias = jnp.where(row // group == lax.rem(column, kv_heads), 0.0, MASKED)
    return jnp.tile(bias, (rows // heads, columns // 128))


def in_hbm(operand):
    return pltpu.with_memory_space_constraint(operand, pltpu.HBM)


def dot_rows(left, right):
    return lax.dot_general(left, right, (((1,), (1,)), ((), ())), preferred_element_type=jnp.float32)


def stat_rows(row_max, row_total, shape):
    lane = lax.broadcasted_iota(jnp.int32, shape, 1)
    return jnp.where(lane == 0, row_max, row_total)


def slot(rows, columns):
    if rows == 8 and LANES < columns <= LANES + HALF:
        return 3, 4, LANES
    return rows, columns


def put(ref, places, value):
    if ref.ndim == 3:
        for place in places:
            ref[place] = value.astype(ref.dtype)
        return
    rows, columns = value.shape
    rest = value[:, LANES:]
    if columns < LANES + HALF:
        rest = jnp.concatenate([rest, jnp.zeros((rows, LANES + HALF - columns), value.dtype)], axis=1)
    rest = jnp.concatenate([rest[:4], rest[4:]], axis=1)
    pieces = [piece.astype(ref.dtype) for piece in (value[:4, :LANES], value[4:, :LANES], rest)]
    for place in places:
        for part, piece in enumerate(pieces):
            ref[place, part] = piece


def joined(first, second, rest):
    low = jnp.concatenate([first.astype(jnp.float32), second.astype(jnp.float32)], axis=0)
    rest = rest.astype(jnp.float32)
    return low, jnp.concatenate([rest, pltpu.roll(rest, HALF, 1)], axis=0)


def turn(value, columns, back=False):
    device = lax.axis_index("ctx") * lax.axis_size("head") + lax.axis_index("head")
    offset = lax.rem(device * columns, LANES)
    return pltpu.roll(value, lax.rem(LANES - offset, LANES) if back else offset, 1)


def put_turned(ref, value):
    rows, columns = value.shape
    rest = jnp.concatenate(
        [value[:, LANES:], jnp.zeros((rows, 2 * LANES - columns), value.dtype)], axis=1
    )
    low, rest = turn(value[:, :LANES], columns), turn(rest, columns)
    rest = rest[:4] + pltpu.roll(rest, HALF, 1)[4:]
    pieces = [piece.astype(ref.dtype) for piece in (low[:4], low[4:], rest)]
    for place in range(ref.shape[0]):
        for part, piece in enumerate(pieces):
            ref[place, part] = piece


def whole_state(pieces_ref, order, columns):
    lane = lax.broadcasted_iota(jnp.int32, (8, LANES), 1)
    tiles = {}
    for device in range(len(order)):
        place = order.index(device)
        low, rest = joined(*(pieces_ref[place, part] for part in range(3)))
        first, offset = divmod(device * columns, LANES)
        tiles[first] = jnp.where(lane >= offset, low, tiles[first]) if offset else low
        tiles[first + 1] = jnp.where(lane < offset, low, rest)
        if offset + columns - LANES > LANES:
            tiles[first + 2] = rest
    return jnp.concatenate([tiles[place] for place in range(len(order) * columns // LANES)], axis=1)


def put_columns(ref, order, share, columns):
    lane = lax.broadcasted_iota(jnp.int32, (8, LANES), 1)
    tile = lambda place: share[:, place * LANES : (place + 1) * LANES]
    for device in range(len(order)):
        first, offset = divmod(device * columns, LANES)
        end = offset + columns - LANES
        low = jnp.where(lane >= offset, tile(first), tile(first + 1)) if offset else tile(first)
        rest = tile(first + 1)
        own = (lane >= offset) & (lane < end)
        if end > LANES:
            rest = jnp.where(lane >= offset, rest, tile(first + 2))
            own = (lane >= offset) | (lane < end - LANES)
        rest = jnp.where(own[:4], rest[:4], pltpu.roll(rest, HALF, 1)[4:])
        place = order.index(device)
        for part, piece in enumerate((low[:4], low[4:], rest)):
            ref[place, part] = piece.astype(ref.dtype)


def spread_kernel(length_ref, source_hbm, copies_ref, lengths_ref, source_ref, sem):
    load = pltpu.make_async_copy(source_hbm, source_ref, sem)
    load.start()
    lengths_ref[...] = jnp.full(lengths_ref.shape, length_ref[0], jnp.int32)
    load.wait()
    for place in range(copies_ref.shape[0]):
        copies_ref[place] = source_ref[0]


def spread(lengths, value, count):
    return pl.pallas_call(
        spread_kernel,
        out_shape=(
            jax.ShapeDtypeStruct((count, *value.shape[1:]), value.dtype),
            jax.ShapeDtypeStruct(value.shape[1:], jnp.int32),
        ),
        in_specs=[pl.BlockSpec(memory_space=pltpu.SMEM), pl.BlockSpec(memory_space=pl.ANY)],
        scratch_shapes=[pltpu.VMEM(value.shape, value.dtype), pltpu.SemaphoreType.DMA],
        compiler_params=pltpu.CompilerParams(vmem_limit_bytes=4 * MIB),
        cost_estimate=COST,
    )(lengths, in_hbm(value))


def attention_kernel(
    length_ref, arrived_ref, kn_ref, vn_ref, ks_ref, vs_ref, kp_ref, vp_ref, part_ref, sum_ref, stat_ref
):
    count, heads, width = arrived_ref.shape
    kv_heads = kn_ref.shape[1]
    rows = count * heads
    queries = arrived_ref[...].reshape(rows, width)
    row = lax.broadcasted_iota(jnp.int32, (rows, LANES), 0)
    own = jnp.where(row // heads == lax.axis_index("ctx"), 0.0, MASKED)
    prompt_rows = kp_ref.shape[0]
    size = BLOCK_ROWS if prompt_rows % BLOCK_ROWS == 0 else prompt_rows
    prompt_bias = head_bias(rows, size, heads, kv_heads)
    blocks = []
    for start in range(0, prompt_rows, size):
        block = slice(start, start + size)
        scores = SCORE_SCALE * dot_rows(queries, kp_ref[block]) + prompt_bias
        blocks.append((scores, vp_ref[block], None, None))
    cached_scores = SCORE_SCALE * dot_rows(queries, ks_ref[...])
    column = lax.broadcasted_iota(jnp.int32, (heads, cached_scores.shape[1]), 1)
    unused = jnp.where(column // kv_heads < length_ref[:, 0:1], 0.0, MASKED)
    bias = head_bias(heads, cached_scores.shape[1], heads, kv_heads) + unused
    bias = jnp.tile(bias, (count, 1)) + own[:, 0:1]
    cached_scores = cached_scores + bias
    new_scores = SCORE_SCALE * dot_rows(queries, kn_ref[0])
    new_scores = new_scores + head_bias(rows, LANES, heads, kv_heads)[:, :kv_heads] + own[:, :kv_heads]
    blocks.append((cached_scores, vs_ref[...], new_scores, vn_ref[0]))
    parts = []
    for block_scores, values, more_scores, more_values in blocks:
        block_max = jnp.max(block_scores, axis=1, keepdims=True)
        if more_scores is not None:
            block_max = jnp.maximum(block_max, jnp.max(more_scores, axis=1, keepdims=True))
        weights = jnp.exp(block_scores - block_max).astype(jnp.bfloat16)
        block_total = jnp.sum(weights.astype(jnp.float32), axis=1, keepdims=True)
        block_sum = jnp.dot(weights, values, preferred_element_type=jnp.float32)
        if more_scores is not None:
            weights = jnp.exp(more_scores - block_max).astype(jnp.bfloat16)
            block_total += jnp.sum(weights.astype(jnp.float32), axis=1, keepdims=True)
            block_sum += jnp.dot(weights, more_values, preferred_element_type=jnp.float32)
        parts.append((block_max, block_total, block_sum))
    row_max = functools.reduce(jnp.maximum, [part[0] for part in parts])
    factors = [jnp.exp(part[0] - row_max) for part in parts]
    row_total = sum(part[1] * factor for part, factor in zip(parts, factors))
    row_sum = sum(part[2] * factor for part, factor in zip(parts, factors))
    sum_ref[...] = row_sum.reshape(count, heads, width)
    stat_ref[...] = stat_rows(row_max, row_total, row_sum.shape).reshape(count, heads, width)
    lane = lax.broadcasted_iota(jnp.int32, (heads, HALF), 1)
    for place in range(count):
        total = stat_ref[place, :, 1:2]
        rest = jnp.broadcast_to(stat_ref[place, :, 0:1] + jnp.log(total), (heads, HALF))
        terms = jnp.zeros((heads, HALF), jnp.float32)
        for term in range(TERMS):
            rounded = rest.astype(jnp.bfloat16).astype(jnp.float32)
            terms = jnp.where(lane == term, rounded, terms)
            rest = rest - rounded
        put(part_ref, (place,), jnp.concatenate([sum_ref[place] / total, terms], axis=1))


def attend(lengths, arrived, *operands):
    count, heads, width = arrived.shape
    return pl.pallas_call(
        attention_kernel,
        out_shape=jax.ShapeDtypeStruct((count, *slot(heads, width + HALF)), jnp.bfloat16),
        scratch_shapes=[pltpu.VMEM(arrived.shape, jnp.float32)] * 2,
        compiler_params=pltpu.CompilerParams(vmem_limit_bytes=24 * MIB),
        cost_estimate=COST,
    )(lengths, arrived, *operands)


def join_kernel(part_ref, copies_ref):
    logs, shares = [], []
    for source in range(part_ref.shape[0]):
        share, terms = joined(*(part_ref[source, part] for part in range(3)))
        shares.append(share)
        logs.append(jnp.sum(terms[:, :TERMS], axis=1, keepdims=True))
    largest = functools.reduce(jnp.maximum, logs)
    factors = [jnp.exp(log - largest) for log in logs]
    summed = sum(share * factor for share, factor in zip(shares, factors))
    attention = (summed / sum(factors)).astype(jnp.bfloat16)
    for place in range(copies_ref.shape[0]):
        copies_ref[place] = attention


def join_partials(parts, shape):
    return pl.pallas_call(
        join_kernel,
        out_shape=jax.ShapeDtypeStruct(shape, jnp.bfloat16),
        compiler_params=pltpu.CompilerParams(vmem_limit_bytes=8 * MIB),
        cost_estimate=COST,
    )(parts)


def project_kernel(order, rows_ref, w_ref, residual_ref, out_ref, copies_ref, wide_ref):
    devices, heads, width = rows_ref.shape
    completions = residual_ref.shape[0]
    all_heads = devices * heads // completions
    for place, device in enumerate(order):
        wide_ref[device * heads : (device + 1) * heads] = rows_ref[place].astype(jnp.float32)
    rows = [wide_ref[pl.ds(head, completions, stride=all_heads), :] for head in range(all_heads)]
    rows = jnp.concatenate([row.astype(jnp.bfloat16) for row in rows], axis=1)
    projected = dot_rows(rows, w_ref[...])
    hidden = (residual_ref[...].astype(jnp.float32) + projected).astype(jnp.bfloat16)
    out_ref[...] = hidden
    if copies_ref.ndim == 4:
        put_turned(copies_ref, hidden.astype(jnp.float32))
    else:
        put(copies_ref, range(copies_ref.shape[0]), hidden)


def project(order, rows, w_out, residual):
    devices, heads, width = rows.shape
    return pl.pallas_call(
        functools.partial(project_kernel, order),
        out_shape=(
            jax.ShapeDtypeStruct(residual.shape, jnp.bfloat16),
            jax.ShapeDtypeStruct((devices, *slot(*residual.shape)), jnp.bfloat16),
        ),
        scratch_shapes=[pltpu.VMEM((devices * heads, width), jnp.float32)],
        compiler_params=pltpu.CompilerParams(vmem_limit_bytes=12 * MIB),
        cost_estimate=COST,
    )(rows, w_out, residual)


def forward_kernel(
    order, pieces_ref, gain_ref, copies_ref, gate_ref, up_ref, down_ref, out_ref, attention_hbm, state_ref, sem
):
    keep = pltpu.make_async_copy(copies_ref.at[0], attention_hbm, sem)
    keep.start()
    devices = pieces_ref.shape[0]
    columns = gain_ref.shape[0] // devices
    if pieces_ref.ndim == 4:
        state = whole_state(pieces_ref, order, columns)
    else:
        for place, device in enumerate(order):
            columns_of = slice(device * columns, (device + 1) * columns)
            state_ref[:, columns_of] = pieces_ref[place].astype(jnp.float32)
        state = state_ref[...]
    mean_square = jnp.mean(state * state, axis=-1, keepdims=True)
    gain = gain_ref[...].reshape(1, devices * columns)
    scale = lax.rsqrt(mean_square + NORM_EPSILON)
    scaled = (state * gain).astype(jnp.bfloat16)
    units = gate_ref.shape[0]
    count = CHUNKS if units % (16 * CHUNKS) == 0 else 1
    size = units // count
    share = jnp.zeros((scaled.shape[0], down_ref.shape[1]), jnp.float32)
    ready = None
    for chunk in range(count + 1):
        if chunk < count:
            rows = slice(chunk * size, (chunk + 1) * size)
            gate_values = dot_rows(gate_ref[rows], scaled)
            up_values = dot_rows(scaled, up_ref[rows]) * scale
        if ready is not None:
            activated, held = ready
            share += jnp.dot(activated, down_ref[held], preferred_element_type=jnp.float32)
        if chunk < count:
            activated = jax.nn.gelu(gate_values.T * scale, approximate=True) * up_values
            ready = activated.astype(jnp.bfloat16), rows
    if pieces_ref.ndim == 4:
        put_columns(out_ref, order, share, columns)
    else:
        for place, device in enumerate(order):
            put(out_ref, (place,), share[:, device * columns : (device + 1) * columns])
    keep.wait()


def forward(order, pieces, completions, gain, copies, *weights):
    return pl.pallas_call(
        functools.partial(forward_kernel, order),
        out_shape=(
            jax.ShapeDtypeStruct(pieces.shape, jnp.bfloat16),
            jax.ShapeDtypeStruct(copies.shape[1:], jnp.bfloat16),
        ),
        out_specs=(pl.BlockSpec(memory_space=pltpu.VMEM), pl.BlockSpec(memory_space=pl.ANY)),
        scratch_shapes=[
            pltpu.VMEM((completions, gain.shape[0]), jnp.float32),
            pltpu.SemaphoreType.DMA,
        ],
        compiler_params=pltpu.CompilerParams(vmem_limit_bytes=8 * MIB),
        cost_estimate=COST,
    )(pieces, gain, copies, *weights)


def total_kernel(shares_ref, hidden_ref, out_ref):
    summed = jnp.sum(shares_ref[...].astype(jnp.float32), axis=0)
    if shares_ref.ndim == 4:
        columns = hidden_ref.shape[1]
        low, rest = (turn(part, columns, back=True) for part in joined(*summed))
        summed = jnp.concatenate([low, rest[:, : columns - LANES]], axis=1)
    out_ref[...] = (hidden_ref[...].astype(jnp.float32) + summed).astype(jnp.bfloat16)


def total(shares, hidden):
    return pl.pallas_call(
        total_kernel,
        out_shape=jax.ShapeDtypeStruct(hidden.shape, jnp.bfloat16),
        compiler_params=pltpu.CompilerParams(vmem_limit_bytes=16 * MIB),
    )(shares, hidden)


def listed(ctx_count, groups):
    order = (0, 1, 4, 5, 6, 7, 2, 3) if ctx_count == 8 else range(ctx_count)
    return [ctx * groups + group for ctx in order for group in range(groups)]


def exchange(copies, axes=BOTH):
    groups = None
    if axes == BOTH:
        groups = [listed(lax.axis_size("ctx"), lax.axis_size("head"))]
    return lax.all_to_all(
        copies, axes, split_axis=0, concat_axis=0, tiled=True, axis_index_groups=groups
    )


def body(
    queries,
    k_new,
    v_new,
    k_suffix,
    v_suffix,
    lengths,
    k_prefix,
    v_prefix,
    w_out,
    residual,
    norm_gain,
    w_gate,
    w_up,
    w_down,
):
    ctx_count = lax.axis_size("ctx")
    devices = ctx_count * lax.axis_size("head")
    copies, own_length = spread(lengths, queries, ctx_count)
    arrived = exchange(copies, "ctx")
    rows_of = lambda values: values.reshape(-1, values.shape[-1])
    parts = attend(
        own_length, arrived, k_new, v_new, *map(rows_of, (k_suffix, v_suffix, k_prefix, v_prefix))
    )
    copies = join_partials(exchange(parts, "ctx"), (devices, *queries.shape[1:]))
    order = listed(ctx_count, devices // ctx_count)
    hidden_part, hidden_copies = project(order, exchange(copies), w_out.T, residual)
    shares, attention = forward(
        order, exchange(hidden_copies), residual.shape[0], norm_gain, copies, w_gate.T, w_up.T, w_down
    )
    return (attention[None], total(exchange(shares), hidden_part))


def solution(mesh):
    placed = (
        P("ctx", "head", None),
        P("ctx", "head", None),
        P("ctx", "head", None),
        P("ctx", None, "head", None),
        P("ctx", None, "head", None),
        P("ctx"),
        P("ctx", "head", None),
        P("ctx", "head", None),
        P(None, BOTH),
        P(None, BOTH),
        P(),
        P(None, BOTH),
        P(None, BOTH),
        P(BOTH, None),
    )
    return jax.shard_map(
        body,
        mesh=mesh,
        in_specs=placed,
        out_specs=(P("ctx", "head", None), P(None, BOTH)),
        check_vma=False,
    )
```

```python
import functools

import jax
import jax.numpy as jnp
from jax import lax
from jax.experimental import pallas as pl
from jax.experimental.pallas import tpu as pltpu
from jax.sharding import PartitionSpec as P

SCORE_SCALE = 168.0 ** (-0.5)
NORM_EPSILON = 1e-06
MASKED = -1e30
MIB = 1024 * 1024
COST = pl.CostEstimate(flops=10**10, bytes_accessed=MIB, transcendentals=10**6)
TERMS = 3
CHUNKS = 3
BLOCK_ROWS = 2048
LANES = 128
HALF = LANES // 2
BOTH = ("ctx", "head")


def head_bias(rows, columns, heads, kv_heads):
    group = heads // kv_heads
    tile = (heads, 128)
    row = lax.broadcasted_iota(jnp.int32, tile, 0)
    column = lax.broadcasted_iota(jnp.int32, tile, 1)
    bias = jnp.where(row // group == lax.rem(column, kv_heads), 0.0, MASKED)
    return jnp.tile(bias, (rows // heads, columns // 128))


def in_hbm(operand):
    return pltpu.with_memory_space_constraint(operand, pltpu.HBM)


def dot_rows(left, right):
    return lax.dot_general(left, right, (((1,), (1,)), ((), ())), preferred_element_type=jnp.float32)


def stat_rows(row_max, row_total, shape):
    lane = lax.broadcasted_iota(jnp.int32, shape, 1)
    return jnp.where(lane == 0, row_max, row_total)


def slot(rows, columns):
    if rows == 8 and LANES < columns <= LANES + HALF:
        return 3, 4, LANES
    return rows, columns


def put(ref, places, value):
    if ref.ndim == 3:
        for place in places:
            ref[place] = value.astype(ref.dtype)
        return
    rows, columns = value.shape
    rest = value[:, LANES:]
    if columns < LANES + HALF:
        rest = jnp.concatenate([rest, jnp.zeros((rows, LANES + HALF - columns), value.dtype)], axis=1)
    rest = jnp.concatenate([rest[:4], rest[4:]], axis=1)
    pieces = [piece.astype(ref.dtype) for piece in (value[:4, :LANES], value[4:, :LANES], rest)]
    for place in places:
        for part, piece in enumerate(pieces):
            ref[place, part] = piece


def joined(first, second, rest):
    low = jnp.concatenate([first.astype(jnp.float32), second.astype(jnp.float32)], axis=0)
    rest = rest.astype(jnp.float32)
    return low, jnp.concatenate([rest, pltpu.roll(rest, HALF, 1)], axis=0)


def turn(value, columns, back=False):
    device = lax.axis_index("ctx") * lax.axis_size("head") + lax.axis_index("head")
    offset = lax.rem(device * columns, LANES)
    return pltpu.roll(value, lax.rem(LANES - offset, LANES) if back else offset, 1)


def put_turned(ref, value):
    rows, columns = value.shape
    rest = jnp.concatenate(
        [value[:, LANES:], jnp.zeros((rows, 2 * LANES - columns), value.dtype)], axis=1
    )
    low, rest = turn(value[:, :LANES], columns), turn(rest, columns)
    rest = rest[:4] + pltpu.roll(rest, HALF, 1)[4:]
    pieces = [piece.astype(ref.dtype) for piece in (low[:4], low[4:], rest)]
    for place in range(ref.shape[0]):
        for part, piece in enumerate(pieces):
            ref[place, part] = piece


def whole_state(pieces_ref, order, columns):
    lane = lax.broadcasted_iota(jnp.int32, (8, LANES), 1)
    tiles = {}
    for device in range(len(order)):
        place = order.index(device)
        low, rest = joined(*(pieces_ref[place, part] for part in range(3)))
        first, offset = divmod(device * columns, LANES)
        tiles[first] = jnp.where(lane >= offset, low, tiles[first]) if offset else low
        tiles[first + 1] = jnp.where(lane < offset, low, rest)
        if offset + columns - LANES > LANES:
            tiles[first + 2] = rest
    return jnp.concatenate([tiles[place] for place in range(len(order) * columns // LANES)], axis=1)


def put_columns(ref, order, share, columns):
    lane = lax.broadcasted_iota(jnp.int32, (8, LANES), 1)
    tile = lambda place: share[:, place * LANES : (place + 1) * LANES]
    for device in range(len(order)):
        first, offset = divmod(device * columns, LANES)
        end = offset + columns - LANES
        low = jnp.where(lane >= offset, tile(first), tile(first + 1)) if offset else tile(first)
        rest = tile(first + 1)
        own = (lane >= offset) & (lane < end)
        if end > LANES:
            rest = jnp.where(lane >= offset, rest, tile(first + 2))
            own = (lane >= offset) | (lane < end - LANES)
        rest = jnp.where(own[:4], rest[:4], pltpu.roll(rest, HALF, 1)[4:])
        place = order.index(device)
        for part, piece in enumerate((low[:4], low[4:], rest)):
            ref[place, part] = piece.astype(ref.dtype)


def spread_kernel(length_ref, source_hbm, copies_ref, lengths_ref, source_ref, sem):
    load = pltpu.make_async_copy(source_hbm, source_ref, sem)
    load.start()
    lengths_ref[...] = jnp.full(lengths_ref.shape, length_ref[0], jnp.int32)
    load.wait()
    for place in range(copies_ref.shape[0]):
        copies_ref[place] = source_ref[0]


def spread(lengths, value, count):
    return pl.pallas_call(
        spread_kernel,
        out_shape=(
            jax.ShapeDtypeStruct((count, *value.shape[1:]), value.dtype),
            jax.ShapeDtypeStruct(value.shape[1:], jnp.int32),
        ),
        in_specs=[pl.BlockSpec(memory_space=pltpu.SMEM), pl.BlockSpec(memory_space=pl.ANY)],
        scratch_shapes=[pltpu.VMEM(value.shape, value.dtype), pltpu.SemaphoreType.DMA],
        compiler_params=pltpu.CompilerParams(vmem_limit_bytes=4 * MIB),
        cost_estimate=COST,
    )(lengths, in_hbm(value))


def attention_kernel(
    length_ref, arrived_ref, kn_ref, vn_ref, ks_ref, vs_ref, kp_ref, vp_ref, part_ref, sum_ref, stat_ref
):
    count, heads, width = arrived_ref.shape
    kv_heads = kn_ref.shape[1]
    rows = count * heads
    queries = arrived_ref[...].reshape(rows, width)
    row = lax.broadcasted_iota(jnp.int32, (rows, LANES), 0)
    own = jnp.where(row // heads == lax.axis_index("ctx"), 0.0, MASKED)
    prompt_rows = kp_ref.shape[0]
    size = BLOCK_ROWS if prompt_rows % BLOCK_ROWS == 0 else prompt_rows
    prompt_bias = head_bias(rows, size, heads, kv_heads)
    blocks = []
    for start in range(0, prompt_rows, size):
        block = slice(start, start + size)
        scores = SCORE_SCALE * dot_rows(queries, kp_ref[block]) + prompt_bias
        blocks.append((scores, vp_ref[block], None, None))
    cached_scores = SCORE_SCALE * dot_rows(queries, ks_ref[...])
    column = lax.broadcasted_iota(jnp.int32, (heads, cached_scores.shape[1]), 1)
    unused = jnp.where(column // kv_heads < length_ref[:, 0:1], 0.0, MASKED)
    bias = head_bias(heads, cached_scores.shape[1], heads, kv_heads) + unused
    bias = jnp.tile(bias, (count, 1)) + own[:, 0:1]
    cached_scores = cached_scores + bias
    new_scores = SCORE_SCALE * dot_rows(queries, kn_ref[0])
    new_scores = new_scores + head_bias(rows, LANES, heads, kv_heads)[:, :kv_heads] + own[:, :kv_heads]
    blocks.append((cached_scores, vs_ref[...], new_scores, vn_ref[0]))
    parts = []
    for block_scores, values, more_scores, more_values in blocks:
        block_max = jnp.max(block_scores, axis=1, keepdims=True)
        if more_scores is not None:
            block_max = jnp.maximum(block_max, jnp.max(more_scores, axis=1, keepdims=True))
        weights = jnp.exp(block_scores - block_max).astype(jnp.bfloat16)
        block_total = jnp.sum(weights.astype(jnp.float32), axis=1, keepdims=True)
        block_sum = jnp.dot(weights, values, preferred_element_type=jnp.float32)
        if more_scores is not None:
            weights = jnp.exp(more_scores - block_max).astype(jnp.bfloat16)
            block_total += jnp.sum(weights.astype(jnp.float32), axis=1, keepdims=True)
            block_sum += jnp.dot(weights, more_values, preferred_element_type=jnp.float32)
        parts.append((block_max, block_total, block_sum))
    row_max = functools.reduce(jnp.maximum, [part[0] for part in parts])
    factors = [jnp.exp(part[0] - row_max) for part in parts]
    row_total = sum(part[1] * factor for part, factor in zip(parts, factors))
    row_sum = sum(part[2] * factor for part, factor in zip(parts, factors))
    sum_ref[...] = row_sum.reshape(count, heads, width)
    stat_ref[...] = stat_rows(row_max, row_total, row_sum.shape).reshape(count, heads, width)
    lane = lax.broadcasted_iota(jnp.int32, (heads, HALF), 1)
    for place in range(count):
        total = stat_ref[place, :, 1:2]
        rest = jnp.broadcast_to(stat_ref[place, :, 0:1] + jnp.log(total), (heads, HALF))
        terms = jnp.zeros((heads, HALF), jnp.float32)
        for term in range(TERMS):
            rounded = rest.astype(jnp.bfloat16).astype(jnp.float32)
            terms = jnp.where(lane == term, rounded, terms)
            rest = rest - rounded
        put(part_ref, (place,), jnp.concatenate([sum_ref[place] / total, terms], axis=1))


def attend(lengths, arrived, *operands):
    count, heads, width = arrived.shape
    return pl.pallas_call(
        attention_kernel,
        out_shape=jax.ShapeDtypeStruct((count, *slot(heads, width + HALF)), jnp.bfloat16),
        scratch_shapes=[pltpu.VMEM(arrived.shape, jnp.float32)] * 2,
        compiler_params=pltpu.CompilerParams(vmem_limit_bytes=24 * MIB),
        cost_estimate=COST,
    )(lengths, arrived, *operands)


def join_kernel(part_ref, copies_ref):
    logs, shares = [], []
    for source in range(part_ref.shape[0]):
        share, terms = joined(*(part_ref[source, part] for part in range(3)))
        shares.append(share)
        logs.append(jnp.sum(terms[:, :TERMS], axis=1, keepdims=True))
    largest = functools.reduce(jnp.maximum, logs)
    factors = [jnp.exp(log - largest) for log in logs]
    summed = sum(share * factor for share, factor in zip(shares, factors))
    attention = (summed / sum(factors)).astype(jnp.bfloat16)
    for place in range(copies_ref.shape[0]):
        copies_ref[place] = attention


def join_partials(parts, shape):
    return pl.pallas_call(
        join_kernel,
        out_shape=jax.ShapeDtypeStruct(shape, jnp.bfloat16),
        compiler_params=pltpu.CompilerParams(vmem_limit_bytes=8 * MIB),
        cost_estimate=COST,
    )(parts)


def project_kernel(order, rows_ref, w_ref, residual_ref, out_ref, copies_ref, wide_ref):
    devices, heads, width = rows_ref.shape
    completions = residual_ref.shape[0]
    all_heads = devices * heads // completions
    for place, device in enumerate(order):
        wide_ref[device * heads : (device + 1) * heads] = rows_ref[place].astype(jnp.float32)
    rows = [wide_ref[pl.ds(head, completions, stride=all_heads), :] for head in range(all_heads)]
    rows = jnp.concatenate([row.astype(jnp.bfloat16) for row in rows], axis=1)
    projected = dot_rows(rows, w_ref[...])
    hidden = (residual_ref[...].astype(jnp.float32) + projected).astype(jnp.bfloat16)
    out_ref[...] = hidden
    if copies_ref.ndim == 4:
        put_turned(copies_ref, hidden.astype(jnp.float32))
    else:
        put(copies_ref, range(copies_ref.shape[0]), hidden)


def project(order, rows, w_out, residual):
    devices, heads, width = rows.shape
    return pl.pallas_call(
        functools.partial(project_kernel, order),
        out_shape=(
            jax.ShapeDtypeStruct(residual.shape, jnp.bfloat16),
            jax.ShapeDtypeStruct((devices, *slot(*residual.shape)), jnp.bfloat16),
        ),
        scratch_shapes=[pltpu.VMEM((devices * heads, width), jnp.float32)],
        compiler_params=pltpu.CompilerParams(vmem_limit_bytes=12 * MIB),
        cost_estimate=COST,
    )(rows, w_out, residual)


def forward_kernel(
    order, pieces_ref, gain_ref, copies_ref, gate_ref, up_ref, down_ref, out_ref, attention_hbm, state_ref, sem
):
    keep = pltpu.make_async_copy(copies_ref.at[0], attention_hbm, sem)
    keep.start()
    devices = pieces_ref.shape[0]
    columns = gain_ref.shape[0] // devices
    if pieces_ref.ndim == 4:
        state = whole_state(pieces_ref, order, columns)
    else:
        for place, device in enumerate(order):
            columns_of = slice(device * columns, (device + 1) * columns)
            state_ref[:, columns_of] = pieces_ref[place].astype(jnp.float32)
        state = state_ref[...]
    mean_square = jnp.mean(state * state, axis=-1, keepdims=True)
    gain = gain_ref[...].reshape(1, devices * columns)
    normed = (state * lax.rsqrt(mean_square + NORM_EPSILON) * gain).astype(jnp.bfloat16)
    units = gate_ref.shape[0]
    count = CHUNKS if units % (16 * CHUNKS) == 0 else 1
    size = units // count
    share = jnp.zeros((normed.shape[0], down_ref.shape[1]), jnp.float32)
    ready = None
    for chunk in range(count + 1):
        if chunk < count:
            rows = slice(chunk * size, (chunk + 1) * size)
            gate_values = dot_rows(gate_ref[rows], normed)
            up_values = dot_rows(normed, up_ref[rows])
        if ready is not None:
            activated, held = ready
            share += jnp.dot(activated, down_ref[held], preferred_element_type=jnp.float32)
        if chunk < count:
            activated = jax.nn.gelu(gate_values.T, approximate=True) * up_values
            ready = activated.astype(jnp.bfloat16), rows
    if pieces_ref.ndim == 4:
        put_columns(out_ref, order, share, columns)
    else:
        for place, device in enumerate(order):
            put(out_ref, (place,), share[:, device * columns : (device + 1) * columns])
    keep.wait()


def forward(order, pieces, completions, gain, copies, *weights):
    return pl.pallas_call(
        functools.partial(forward_kernel, order),
        out_shape=(
            jax.ShapeDtypeStruct(pieces.shape, jnp.bfloat16),
            jax.ShapeDtypeStruct(copies.shape[1:], jnp.bfloat16),
        ),
        out_specs=(pl.BlockSpec(memory_space=pltpu.VMEM), pl.BlockSpec(memory_space=pl.ANY)),
        scratch_shapes=[
            pltpu.VMEM((completions, gain.shape[0]), jnp.float32),
            pltpu.SemaphoreType.DMA,
        ],
        compiler_params=pltpu.CompilerParams(vmem_limit_bytes=8 * MIB),
        cost_estimate=COST,
    )(pieces, gain, copies, *weights)


def total_kernel(shares_ref, hidden_ref, out_ref):
    half = shares_ref.shape[0] // 2
    pairs = shares_ref[:half].astype(jnp.float32) + shares_ref[half:].astype(jnp.float32)
    summed = jnp.sum(pairs, axis=0)
    if shares_ref.ndim == 4:
        columns = hidden_ref.shape[1]
        low, rest = (turn(part, columns, back=True) for part in joined(*summed))
        summed = jnp.concatenate([low, rest[:, : columns - LANES]], axis=1)
    out_ref[...] = (hidden_ref[...].astype(jnp.float32) + summed).astype(jnp.bfloat16)


def total(shares, hidden):
    return pl.pallas_call(
        total_kernel,
        out_shape=jax.ShapeDtypeStruct(hidden.shape, jnp.bfloat16),
        compiler_params=pltpu.CompilerParams(vmem_limit_bytes=16 * MIB),
    )(shares, hidden)


def listed(ctx_count, groups):
    order = (0, 1, 4, 5, 6, 7, 2, 3) if ctx_count == 8 else range(ctx_count)
    return [ctx * groups + group for ctx in order for group in range(groups)]


def exchange(copies, axes=BOTH):
    groups = None
    if axes == BOTH:
        groups = [listed(lax.axis_size("ctx"), lax.axis_size("head"))]
    return lax.all_to_all(
        copies, axes, split_axis=0, concat_axis=0, tiled=True, axis_index_groups=groups
    )


def body(
    queries,
    k_new,
    v_new,
    k_suffix,
    v_suffix,
    lengths,
    k_prefix,
    v_prefix,
    w_out,
    residual,
    norm_gain,
    w_gate,
    w_up,
    w_down,
):
    ctx_count = lax.axis_size("ctx")
    devices = ctx_count * lax.axis_size("head")
    copies, own_length = spread(lengths, queries, ctx_count)
    arrived = exchange(copies, "ctx")
    rows_of = lambda values: values.reshape(-1, values.shape[-1])
    parts = attend(
        own_length, arrived, k_new, v_new, *map(rows_of, (k_suffix, v_suffix, k_prefix, v_prefix))
    )
    copies = join_partials(exchange(parts, "ctx"), (devices, *queries.shape[1:]))
    order = listed(ctx_count, devices // ctx_count)
    hidden_part, hidden_copies = project(order, exchange(copies), w_out.T, residual)
    shares, attention = forward(
        order, exchange(hidden_copies), residual.shape[0], norm_gain, copies, w_gate.T, w_up.T, w_down
    )
    return (attention[None], total(exchange(shares), hidden_part))


def solution(mesh):
    placed = (
        P("ctx", "head", None),
        P("ctx", "head", None),
        P("ctx", "head", None),
        P("ctx", None, "head", None),
        P("ctx", None, "head", None),
        P("ctx"),
        P("ctx", "head", None),
        P("ctx", "head", None),
        P(None, BOTH),
        P(None, BOTH),
        P(),
        P(None, BOTH),
        P(None, BOTH),
        P(BOTH, None),
    )
    return jax.shard_map(
        body,
        mesh=mesh,
        in_specs=placed,
        out_specs=(P("ctx", "head", None), P(None, BOTH)),
        check_vma=False,
    )
```

```python
import functools

import jax
import jax.numpy as jnp
from jax import lax
from jax.experimental import pallas as pl
from jax.experimental.pallas import tpu as pltpu
from jax.sharding import PartitionSpec as P

SCORE_SCALE = 168.0 ** (-0.5)
NORM_EPSILON = 1e-06
MASKED = -1e30
MIB = 1024 * 1024
COST = pl.CostEstimate(flops=10**10, bytes_accessed=MIB, transcendentals=10**6)
TERMS = 3
CHUNKS = 3
BLOCK_ROWS = 1024
LANES = 128
HALF = LANES // 2
BOTH = ("ctx", "head")


def head_bias(rows, columns, heads, kv_heads):
    group = heads // kv_heads
    tile = (heads, 128)
    row = lax.broadcasted_iota(jnp.int32, tile, 0)
    column = lax.broadcasted_iota(jnp.int32, tile, 1)
    bias = jnp.where(row // group == lax.rem(column, kv_heads), 0.0, MASKED)
    return jnp.tile(bias, (rows // heads, columns // 128))


def in_hbm(operand):
    return pltpu.with_memory_space_constraint(operand, pltpu.HBM)


def dot_rows(left, right):
    return lax.dot_general(left, right, (((1,), (1,)), ((), ())), preferred_element_type=jnp.float32)


def stat_rows(row_max, row_total, shape):
    lane = lax.broadcasted_iota(jnp.int32, shape, 1)
    return jnp.where(lane == 0, row_max, row_total)


def slot(rows, columns):
    if rows == 8 and LANES < columns <= LANES + HALF:
        return 3, 4, LANES
    return rows, columns


def put(ref, places, value):
    if ref.ndim == 3:
        for place in places:
            ref[place] = value.astype(ref.dtype)
        return
    rows, columns = value.shape
    rest = value[:, LANES:]
    if columns < LANES + HALF:
        rest = jnp.concatenate([rest, jnp.zeros((rows, LANES + HALF - columns), value.dtype)], axis=1)
    rest = jnp.concatenate([rest[:4], rest[4:]], axis=1)
    pieces = [piece.astype(ref.dtype) for piece in (value[:4, :LANES], value[4:, :LANES], rest)]
    for place in places:
        for part, piece in enumerate(pieces):
            ref[place, part] = piece


def joined(first, second, rest):
    low = jnp.concatenate([first.astype(jnp.float32), second.astype(jnp.float32)], axis=0)
    rest = rest.astype(jnp.float32)
    return low, jnp.concatenate([rest, pltpu.roll(rest, HALF, 1)], axis=0)


def turn(value, columns, back=False):
    device = lax.axis_index("ctx") * lax.axis_size("head") + lax.axis_index("head")
    offset = lax.rem(device * columns, LANES)
    return pltpu.roll(value, lax.rem(LANES - offset, LANES) if back else offset, 1)


def put_turned(ref, value):
    rows, columns = value.shape
    rest = jnp.concatenate(
        [value[:, LANES:], jnp.zeros((rows, 2 * LANES - columns), value.dtype)], axis=1
    )
    low, rest = turn(value[:, :LANES], columns), turn(rest, columns)
    rest = rest[:4] + pltpu.roll(rest, HALF, 1)[4:]
    pieces = [piece.astype(ref.dtype) for piece in (low[:4], low[4:], rest)]
    for place in range(ref.shape[0]):
        for part, piece in enumerate(pieces):
            ref[place, part] = piece


def whole_state(pieces_ref, order, columns):
    lane = lax.broadcasted_iota(jnp.int32, (8, LANES), 1)
    tiles = {}
    for device in range(len(order)):
        place = order.index(device)
        low, rest = joined(*(pieces_ref[place, part] for part in range(3)))
        first, offset = divmod(device * columns, LANES)
        tiles[first] = jnp.where(lane >= offset, low, tiles[first]) if offset else low
        tiles[first + 1] = jnp.where(lane < offset, low, rest)
        if offset + columns - LANES > LANES:
            tiles[first + 2] = rest
    return jnp.concatenate([tiles[place] for place in range(len(order) * columns // LANES)], axis=1)


def put_columns(ref, order, share, columns):
    lane = lax.broadcasted_iota(jnp.int32, (8, LANES), 1)
    tile = lambda place: share[:, place * LANES : (place + 1) * LANES]
    for device in range(len(order)):
        first, offset = divmod(device * columns, LANES)
        end = offset + columns - LANES
        low = jnp.where(lane >= offset, tile(first), tile(first + 1)) if offset else tile(first)
        rest = tile(first + 1)
        own = (lane >= offset) & (lane < end)
        if end > LANES:
            rest = jnp.where(lane >= offset, rest, tile(first + 2))
            own = (lane >= offset) | (lane < end - LANES)
        rest = jnp.where(own[:4], rest[:4], pltpu.roll(rest, HALF, 1)[4:])
        place = order.index(device)
        for part, piece in enumerate((low[:4], low[4:], rest)):
            ref[place, part] = piece.astype(ref.dtype)


def spread_kernel(length_ref, source_hbm, copies_ref, lengths_ref, source_ref, sem):
    load = pltpu.make_async_copy(source_hbm, source_ref, sem)
    load.start()
    lengths_ref[...] = jnp.full(lengths_ref.shape, length_ref[0], jnp.int32)
    load.wait()
    for place in range(copies_ref.shape[0]):
        copies_ref[place] = source_ref[0]


def spread(lengths, value, count):
    return pl.pallas_call(
        spread_kernel,
        out_shape=(
            jax.ShapeDtypeStruct((count, *value.shape[1:]), value.dtype),
            jax.ShapeDtypeStruct(value.shape[1:], jnp.int32),
        ),
        in_specs=[pl.BlockSpec(memory_space=pltpu.SMEM), pl.BlockSpec(memory_space=pl.ANY)],
        scratch_shapes=[pltpu.VMEM(value.shape, value.dtype), pltpu.SemaphoreType.DMA],
        compiler_params=pltpu.CompilerParams(vmem_limit_bytes=4 * MIB),
        cost_estimate=COST,
    )(lengths, in_hbm(value))


def attention_kernel(
    length_ref, arrived_ref, kn_ref, vn_ref, ks_ref, vs_ref, kp_ref, vp_ref, part_ref, sum_ref, stat_ref
):
    count, heads, width = arrived_ref.shape
    kv_heads = kn_ref.shape[1]
    rows = count * heads
    queries = arrived_ref[...].reshape(rows, width)
    row = lax.broadcasted_iota(jnp.int32, (rows, LANES), 0)
    own = jnp.where(row // heads == lax.axis_index("ctx"), 0.0, MASKED)
    prompt_rows = kp_ref.shape[0]
    size = BLOCK_ROWS if prompt_rows % BLOCK_ROWS == 0 else prompt_rows
    prompt_bias = head_bias(rows, size, heads, kv_heads)
    blocks = []
    for start in range(0, prompt_rows, size):
        block = slice(start, start + size)
        scores = SCORE_SCALE * dot_rows(queries, kp_ref[block]) + prompt_bias
        blocks.append((scores, vp_ref[block], None, None))
    cached_scores = SCORE_SCALE * dot_rows(queries, ks_ref[...])
    column = lax.broadcasted_iota(jnp.int32, (heads, cached_scores.shape[1]), 1)
    unused = jnp.where(column // kv_heads < length_ref[:, 0:1], 0.0, MASKED)
    bias = head_bias(heads, cached_scores.shape[1], heads, kv_heads) + unused
    bias = jnp.tile(bias, (count, 1)) + own[:, 0:1]
    cached_scores = cached_scores + bias
    new_scores = SCORE_SCALE * dot_rows(queries, kn_ref[0])
    new_scores = new_scores + head_bias(rows, LANES, heads, kv_heads)[:, :kv_heads] + own[:, :kv_heads]
    blocks.append((cached_scores, vs_ref[...], new_scores, vn_ref[0]))
    parts = []
    for block_scores, values, more_scores, more_values in blocks:
        block_max = jnp.max(block_scores, axis=1, keepdims=True)
        if more_scores is not None:
            block_max = jnp.maximum(block_max, jnp.max(more_scores, axis=1, keepdims=True))
        weights = jnp.exp(block_scores - block_max).astype(jnp.bfloat16)
        block_total = jnp.sum(weights.astype(jnp.float32), axis=1, keepdims=True)
        block_sum = jnp.dot(weights, values, preferred_element_type=jnp.float32)
        if more_scores is not None:
            weights = jnp.exp(more_scores - block_max).astype(jnp.bfloat16)
            block_total += jnp.sum(weights.astype(jnp.float32), axis=1, keepdims=True)
            block_sum += jnp.dot(weights, more_values, preferred_element_type=jnp.float32)
        parts.append((block_max, block_total, block_sum))
    row_max = functools.reduce(jnp.maximum, [part[0] for part in parts])
    factors = [jnp.exp(part[0] - row_max) for part in parts]
    row_total = sum(part[1] * factor for part, factor in zip(parts, factors))
    row_sum = sum(part[2] * factor for part, factor in zip(parts, factors))
    sum_ref[...] = row_sum.reshape(count, heads, width)
    stat_ref[...] = stat_rows(row_max, row_total, row_sum.shape).reshape(count, heads, width)
    lane = lax.broadcasted_iota(jnp.int32, (heads, HALF), 1)
    for place in range(count):
        total = stat_ref[place, :, 1:2]
        rest = jnp.broadcast_to(stat_ref[place, :, 0:1] + jnp.log(total), (heads, HALF))
        terms = jnp.zeros((heads, HALF), jnp.float32)
        for term in range(TERMS):
            rounded = rest.astype(jnp.bfloat16).astype(jnp.float32)
            terms = jnp.where(lane == term, rounded, terms)
            rest = rest - rounded
        put(part_ref, (place,), jnp.concatenate([sum_ref[place] / total, terms], axis=1))


def attend(lengths, arrived, *operands):
    count, heads, width = arrived.shape
    return pl.pallas_call(
        attention_kernel,
        out_shape=jax.ShapeDtypeStruct((count, *slot(heads, width + HALF)), jnp.bfloat16),
        scratch_shapes=[pltpu.VMEM(arrived.shape, jnp.float32)] * 2,
        compiler_params=pltpu.CompilerParams(vmem_limit_bytes=24 * MIB),
        cost_estimate=COST,
    )(lengths, arrived, *operands)


def join_kernel(part_ref, copies_ref):
    logs, shares = [], []
    for source in range(part_ref.shape[0]):
        share, terms = joined(*(part_ref[source, part] for part in range(3)))
        shares.append(share)
        logs.append(jnp.sum(terms[:, :TERMS], axis=1, keepdims=True))
    largest = functools.reduce(jnp.maximum, logs)
    factors = [jnp.exp(log - largest) for log in logs]
    summed = sum(share * factor for share, factor in zip(shares, factors))
    attention = (summed / sum(factors)).astype(jnp.bfloat16)
    for place in range(copies_ref.shape[0]):
        copies_ref[place] = attention


def join_partials(parts, shape):
    return pl.pallas_call(
        join_kernel,
        out_shape=jax.ShapeDtypeStruct(shape, jnp.bfloat16),
        compiler_params=pltpu.CompilerParams(vmem_limit_bytes=8 * MIB),
        cost_estimate=COST,
    )(parts)


def project_kernel(order, rows_ref, w_ref, residual_ref, out_ref, copies_ref, wide_ref):
    devices, heads, width = rows_ref.shape
    completions = residual_ref.shape[0]
    all_heads = devices * heads // completions
    for place, device in enumerate(order):
        wide_ref[device * heads : (device + 1) * heads] = rows_ref[place].astype(jnp.float32)
    rows = [wide_ref[pl.ds(head, completions, stride=all_heads), :] for head in range(all_heads)]
    rows = jnp.concatenate([row.astype(jnp.bfloat16) for row in rows], axis=1)
    projected = dot_rows(rows, w_ref[...])
    hidden = (residual_ref[...].astype(jnp.float32) + projected).astype(jnp.bfloat16)
    out_ref[...] = hidden
    if copies_ref.ndim == 4:
        put_turned(copies_ref, hidden.astype(jnp.float32))
    else:
        put(copies_ref, range(copies_ref.shape[0]), hidden)


def project(order, rows, w_out, residual):
    devices, heads, width = rows.shape
    return pl.pallas_call(
        functools.partial(project_kernel, order),
        out_shape=(
            jax.ShapeDtypeStruct(residual.shape, jnp.bfloat16),
            jax.ShapeDtypeStruct((devices, *slot(*residual.shape)), jnp.bfloat16),
        ),
        scratch_shapes=[pltpu.VMEM((devices * heads, width), jnp.float32)],
        compiler_params=pltpu.CompilerParams(vmem_limit_bytes=12 * MIB),
        cost_estimate=COST,
    )(rows, w_out, residual)


def forward_kernel(
    order, pieces_ref, gain_ref, copies_ref, gate_ref, up_ref, down_ref, out_ref, attention_hbm, state_ref, sem
):
    keep = pltpu.make_async_copy(copies_ref.at[0], attention_hbm, sem)
    keep.start()
    devices = pieces_ref.shape[0]
    columns = gain_ref.shape[0] // devices
    if pieces_ref.ndim == 4:
        state = whole_state(pieces_ref, order, columns)
    else:
        for place, device in enumerate(order):
            columns_of = slice(device * columns, (device + 1) * columns)
            state_ref[:, columns_of] = pieces_ref[place].astype(jnp.float32)
        state = state_ref[...]
    mean_square = jnp.mean(state * state, axis=-1, keepdims=True)
    gain = gain_ref[...].reshape(1, devices * columns)
    normed = (state * lax.rsqrt(mean_square + NORM_EPSILON) * gain).astype(jnp.bfloat16)
    units = gate_ref.shape[0]
    count = CHUNKS if units % (16 * CHUNKS) == 0 else 1
    size = units // count
    share = jnp.zeros((normed.shape[0], down_ref.shape[1]), jnp.float32)
    ready = None
    for chunk in range(count + 1):
        if chunk < count:
            rows = slice(chunk * size, (chunk + 1) * size)
            gate_values = dot_rows(gate_ref[rows], normed)
            up_values = dot_rows(normed, up_ref[rows])
        if ready is not None:
            activated, held = ready
            share += jnp.dot(activated, down_ref[held], preferred_element_type=jnp.float32)
        if chunk < count:
            activated = jax.nn.gelu(gate_values.T, approximate=True) * up_values
            ready = activated.astype(jnp.bfloat16), rows
    if pieces_ref.ndim == 4:
        put_columns(out_ref, order, share, columns)
    else:
        for place, device in enumerate(order):
            put(out_ref, (place,), share[:, device * columns : (device + 1) * columns])
    keep.wait()


def forward(order, pieces, completions, gain, copies, *weights):
    return pl.pallas_call(
        functools.partial(forward_kernel, order),
        out_shape=(
            jax.ShapeDtypeStruct(pieces.shape, jnp.bfloat16),
            jax.ShapeDtypeStruct(copies.shape[1:], jnp.bfloat16),
        ),
        out_specs=(pl.BlockSpec(memory_space=pltpu.VMEM), pl.BlockSpec(memory_space=pl.ANY)),
        scratch_shapes=[
            pltpu.VMEM((completions, gain.shape[0]), jnp.float32),
            pltpu.SemaphoreType.DMA,
        ],
        compiler_params=pltpu.CompilerParams(vmem_limit_bytes=8 * MIB),
        cost_estimate=COST,
    )(pieces, gain, copies, *weights)


def total_kernel(shares_ref, hidden_ref, out_ref):
    half = shares_ref.shape[0] // 2
    pairs = shares_ref[:half].astype(jnp.float32) + shares_ref[half:].astype(jnp.float32)
    summed = jnp.sum(pairs, axis=0)
    if shares_ref.ndim == 4:
        columns = hidden_ref.shape[1]
        low, rest = (turn(part, columns, back=True) for part in joined(*summed))
        summed = jnp.concatenate([low, rest[:, : columns - LANES]], axis=1)
    out_ref[...] = (hidden_ref[...].astype(jnp.float32) + summed).astype(jnp.bfloat16)


def total(shares, hidden):
    return pl.pallas_call(
        total_kernel,
        out_shape=jax.ShapeDtypeStruct(hidden.shape, jnp.bfloat16),
        compiler_params=pltpu.CompilerParams(vmem_limit_bytes=16 * MIB),
    )(shares, hidden)


def listed(ctx_count, groups):
    order = (0, 1, 4, 5, 6, 7, 2, 3) if ctx_count == 8 else range(ctx_count)
    return [ctx * groups + group for ctx in order for group in range(groups)]


def exchange(copies, axes=BOTH):
    groups = None
    if axes == BOTH:
        groups = [listed(lax.axis_size("ctx"), lax.axis_size("head"))]
    return lax.all_to_all(
        copies, axes, split_axis=0, concat_axis=0, tiled=True, axis_index_groups=groups
    )


def body(
    queries,
    k_new,
    v_new,
    k_suffix,
    v_suffix,
    lengths,
    k_prefix,
    v_prefix,
    w_out,
    residual,
    norm_gain,
    w_gate,
    w_up,
    w_down,
):
    ctx_count = lax.axis_size("ctx")
    devices = ctx_count * lax.axis_size("head")
    copies, own_length = spread(lengths, queries, ctx_count)
    arrived = exchange(copies, "ctx")
    rows_of = lambda values: values.reshape(-1, values.shape[-1])
    parts = attend(
        own_length, arrived, k_new, v_new, *map(rows_of, (k_suffix, v_suffix, k_prefix, v_prefix))
    )
    copies = join_partials(exchange(parts, "ctx"), (devices, *queries.shape[1:]))
    order = listed(ctx_count, devices // ctx_count)
    hidden_part, hidden_copies = project(order, exchange(copies), w_out.T, residual)
    shares, attention = forward(
        order, exchange(hidden_copies), residual.shape[0], norm_gain, copies, w_gate.T, w_up.T, w_down
    )
    return (attention[None], total(exchange(shares), hidden_part))


def solution(mesh):
    placed = (
        P("ctx", "head", None),
        P("ctx", "head", None),
        P("ctx", "head", None),
        P("ctx", None, "head", None),
        P("ctx", None, "head", None),
        P("ctx"),
        P("ctx", "head", None),
        P("ctx", "head", None),
        P(None, BOTH),
        P(None, BOTH),
        P(),
        P(None, BOTH),
        P(None, BOTH),
        P(BOTH, None),
    )
    return jax.shard_map(
        body,
        mesh=mesh,
        in_specs=placed,
        out_specs=(P("ctx", "head", None), P(None, BOTH)),
        check_vma=False,
    )
```

```python
import functools

import jax
import jax.numpy as jnp
from jax import lax
from jax.experimental import pallas as pl
from jax.experimental.pallas import tpu as pltpu
from jax.sharding import PartitionSpec as P

SCORE_SCALE = 168.0 ** (-0.5)
NORM_EPSILON = 1e-06
MASKED = -1e30
MIB = 1024 * 1024
COST = pl.CostEstimate(flops=10**10, bytes_accessed=MIB, transcendentals=10**6)
TERMS = 3
CHUNKS = 3
PARTS = 7
BLOCK_ROWS = 1024
LANES = 128
HALF = LANES // 2
BOTH = ("ctx", "head")


def head_bias(rows, columns, heads, kv_heads):
    group = heads // kv_heads
    tile = (heads, 128)
    row = lax.broadcasted_iota(jnp.int32, tile, 0)
    column = lax.broadcasted_iota(jnp.int32, tile, 1)
    bias = jnp.where(row // group == lax.rem(column, kv_heads), 0.0, MASKED)
    return jnp.tile(bias, (rows // heads, columns // 128))


def in_hbm(operand):
    return pltpu.with_memory_space_constraint(operand, pltpu.HBM)


def dot_rows(left, right):
    return lax.dot_general(left, right, (((1,), (1,)), ((), ())), preferred_element_type=jnp.float32)


def stat_rows(row_max, row_total, shape):
    lane = lax.broadcasted_iota(jnp.int32, shape, 1)
    return jnp.where(lane == 0, row_max, row_total)


def slot(rows, columns):
    if rows == 8 and LANES < columns <= LANES + HALF:
        return 3, 4, LANES
    return rows, columns


def put(ref, places, value):
    if ref.ndim == 3:
        for place in places:
            ref[place] = value.astype(ref.dtype)
        return
    rows, columns = value.shape
    rest = value[:, LANES:]
    if columns < LANES + HALF:
        rest = jnp.concatenate([rest, jnp.zeros((rows, LANES + HALF - columns), value.dtype)], axis=1)
    rest = jnp.concatenate([rest[:4], rest[4:]], axis=1)
    pieces = [piece.astype(ref.dtype) for piece in (value[:4, :LANES], value[4:, :LANES], rest)]
    for place in places:
        for part, piece in enumerate(pieces):
            ref[place, part] = piece


def joined(first, second, rest):
    low = jnp.concatenate([first.astype(jnp.float32), second.astype(jnp.float32)], axis=0)
    rest = rest.astype(jnp.float32)
    return low, jnp.concatenate([rest, pltpu.roll(rest, HALF, 1)], axis=0)


def turn(value, columns, back=False):
    device = lax.axis_index("ctx") * lax.axis_size("head") + lax.axis_index("head")
    offset = lax.rem(device * columns, LANES)
    return pltpu.roll(value, lax.rem(LANES - offset, LANES) if back else offset, 1)


def put_turned(ref, value):
    rows, columns = value.shape
    rest = jnp.concatenate(
        [value[:, LANES:], jnp.zeros((rows, 2 * LANES - columns), value.dtype)], axis=1
    )
    low, rest = turn(value[:, :LANES], columns), turn(rest, columns)
    rest = rest[:4] + pltpu.roll(rest, HALF, 1)[4:]
    pieces = [piece.astype(ref.dtype) for piece in (low[:4], low[4:], rest)]
    for place in range(ref.shape[0]):
        for part, piece in enumerate(pieces):
            ref[place, part] = piece


def whole_state(pieces_ref, order, columns):
    lane = lax.broadcasted_iota(jnp.int32, (8, LANES), 1)
    tiles = {}
    for device in range(len(order)):
        place = order.index(device)
        low, rest = joined(*(pieces_ref[place, part] for part in range(3)))
        first, offset = divmod(device * columns, LANES)
        tiles[first] = jnp.where(lane >= offset, low, tiles[first]) if offset else low
        tiles[first + 1] = jnp.where(lane < offset, low, rest)
        if offset + columns - LANES > LANES:
            tiles[first + 2] = rest
    return jnp.concatenate([tiles[place] for place in range(len(order) * columns // LANES)], axis=1)


def put_columns(ref, order, share, columns):
    lane = lax.broadcasted_iota(jnp.int32, (8, LANES), 1)
    tile = lambda place: share[:, place * LANES : (place + 1) * LANES]
    for device in range(len(order)):
        first, offset = divmod(device * columns, LANES)
        end = offset + columns - LANES
        low = jnp.where(lane >= offset, tile(first), tile(first + 1)) if offset else tile(first)
        rest = tile(first + 1)
        own = (lane >= offset) & (lane < end)
        if end > LANES:
            rest = jnp.where(lane >= offset, rest, tile(first + 2))
            own = (lane >= offset) | (lane < end - LANES)
        rest = jnp.where(own[:4], rest[:4], pltpu.roll(rest, HALF, 1)[4:])
        place = order.index(device)
        for part, piece in enumerate((low[:4], low[4:], rest)):
            ref[place, part] = piece.astype(ref.dtype)


def spread_kernel(length_ref, source_hbm, copies_ref, lengths_ref, source_ref, sem):
    load = pltpu.make_async_copy(source_hbm, source_ref, sem)
    load.start()
    lengths_ref[...] = jnp.full(lengths_ref.shape, length_ref[0], jnp.int32)
    load.wait()
    for place in range(copies_ref.shape[0]):
        copies_ref[place] = source_ref[0]


def spread(lengths, value, count):
    return pl.pallas_call(
        spread_kernel,
        out_shape=(
            jax.ShapeDtypeStruct((count, *value.shape[1:]), value.dtype),
            jax.ShapeDtypeStruct(value.shape[1:], jnp.int32),
        ),
        in_specs=[pl.BlockSpec(memory_space=pltpu.SMEM), pl.BlockSpec(memory_space=pl.ANY)],
        scratch_shapes=[pltpu.VMEM(value.shape, value.dtype), pltpu.SemaphoreType.DMA],
        compiler_params=pltpu.CompilerParams(vmem_limit_bytes=4 * MIB),
        cost_estimate=COST,
    )(lengths, in_hbm(value))


def attention_kernel(
    length_ref, arrived_ref, kn_ref, vn_ref, ks_ref, vs_ref, kp_ref, vp_ref, part_ref, sum_ref, stat_ref
):
    count, heads, width = arrived_ref.shape
    kv_heads = kn_ref.shape[1]
    rows = count * heads
    queries = arrived_ref[...].reshape(rows, width)
    row = lax.broadcasted_iota(jnp.int32, (rows, LANES), 0)
    own = jnp.where(row // heads == lax.axis_index("ctx"), 0.0, MASKED)
    prompt_rows = kp_ref.shape[0]
    size = BLOCK_ROWS if prompt_rows % BLOCK_ROWS == 0 else prompt_rows
    prompt_bias = head_bias(rows, size, heads, kv_heads)
    blocks = []
    for start in range(0, prompt_rows, size):
        block = slice(start, start + size)
        scores = SCORE_SCALE * dot_rows(queries, kp_ref[block]) + prompt_bias
        blocks.append((scores, vp_ref[block], None, None))
    cached_scores = SCORE_SCALE * dot_rows(queries, ks_ref[...])
    column = lax.broadcasted_iota(jnp.int32, (heads, cached_scores.shape[1]), 1)
    unused = jnp.where(column // kv_heads < length_ref[:, 0:1], 0.0, MASKED)
    bias = head_bias(heads, cached_scores.shape[1], heads, kv_heads) + unused
    bias = jnp.tile(bias, (count, 1)) + own[:, 0:1]
    cached_scores = cached_scores + bias
    new_scores = SCORE_SCALE * dot_rows(queries, kn_ref[0])
    new_scores = new_scores + head_bias(rows, LANES, heads, kv_heads)[:, :kv_heads] + own[:, :kv_heads]
    blocks.append((cached_scores, vs_ref[...], new_scores, vn_ref[0]))
    parts = []
    for block_scores, values, more_scores, more_values in blocks:
        block_max = jnp.max(block_scores, axis=1, keepdims=True)
        if more_scores is not None:
            block_max = jnp.maximum(block_max, jnp.max(more_scores, axis=1, keepdims=True))
        weights = jnp.exp(block_scores - block_max).astype(jnp.bfloat16)
        block_total = jnp.sum(weights.astype(jnp.float32), axis=1, keepdims=True)
        block_sum = jnp.dot(weights, values, preferred_element_type=jnp.float32)
        if more_scores is not None:
            weights = jnp.exp(more_scores - block_max).astype(jnp.bfloat16)
            block_total += jnp.sum(weights.astype(jnp.float32), axis=1, keepdims=True)
            block_sum += jnp.dot(weights, more_values, preferred_element_type=jnp.float32)
        parts.append((block_max, block_total, block_sum))
    row_max = functools.reduce(jnp.maximum, [part[0] for part in parts])
    factors = [jnp.exp(part[0] - row_max) for part in parts]
    row_total = sum(part[1] * factor for part, factor in zip(parts, factors))
    row_sum = sum(part[2] * factor for part, factor in zip(parts, factors))
    sum_ref[...] = row_sum.reshape(count, heads, width)
    stat_ref[...] = stat_rows(row_max, row_total, row_sum.shape).reshape(count, heads, width)
    lane = lax.broadcasted_iota(jnp.int32, (heads, HALF), 1)
    for place in range(count):
        total = stat_ref[place, :, 1:2]
        rest = jnp.broadcast_to(stat_ref[place, :, 0:1] + jnp.log(total), (heads, HALF))
        terms = jnp.zeros((heads, HALF), jnp.float32)
        for term in range(TERMS):
            rounded = rest.astype(jnp.bfloat16).astype(jnp.float32)
            terms = jnp.where(lane == term, rounded, terms)
            rest = rest - rounded
        put(part_ref, (place,), jnp.concatenate([sum_ref[place] / total, terms], axis=1))


def attend(lengths, arrived, *operands):
    count, heads, width = arrived.shape
    return pl.pallas_call(
        attention_kernel,
        out_shape=jax.ShapeDtypeStruct((count, *slot(heads, width + HALF)), jnp.bfloat16),
        scratch_shapes=[pltpu.VMEM(arrived.shape, jnp.float32)] * 2,
        compiler_params=pltpu.CompilerParams(vmem_limit_bytes=24 * MIB),
        cost_estimate=COST,
    )(lengths, arrived, *operands)


def join_kernel(part_ref, copies_ref):
    logs, shares = [], []
    for source in range(part_ref.shape[0]):
        share, terms = joined(*(part_ref[source, part] for part in range(3)))
        shares.append(share)
        logs.append(jnp.sum(terms[:, :TERMS], axis=1, keepdims=True))
    largest = functools.reduce(jnp.maximum, logs)
    factors = [jnp.exp(log - largest) for log in logs]
    summed = sum(share * factor for share, factor in zip(shares, factors))
    attention = (summed / sum(factors)).astype(jnp.bfloat16)
    for place in range(copies_ref.shape[0]):
        copies_ref[place] = attention


def join_partials(parts, shape):
    return pl.pallas_call(
        join_kernel,
        out_shape=jax.ShapeDtypeStruct(shape, jnp.bfloat16),
        compiler_params=pltpu.CompilerParams(vmem_limit_bytes=8 * MIB),
        cost_estimate=COST,
    )(parts)


def project_kernel(order, rows_ref, w_ref, residual_ref, out_ref, copies_ref, wide_ref):
    devices, heads, width = rows_ref.shape
    completions = residual_ref.shape[0]
    all_heads = devices * heads // completions
    for place, device in enumerate(order):
        wide_ref[device * heads : (device + 1) * heads] = rows_ref[place].astype(jnp.float32)
    rows = [wide_ref[pl.ds(head, completions, stride=all_heads), :] for head in range(all_heads)]
    rows = jnp.concatenate([row.astype(jnp.bfloat16) for row in rows], axis=1)
    projected = dot_rows(rows, w_ref[...])
    hidden = (residual_ref[...].astype(jnp.float32) + projected).astype(jnp.bfloat16)
    out_ref[...] = hidden
    if copies_ref.ndim == 4:
        put_turned(copies_ref, hidden.astype(jnp.float32))
    else:
        put(copies_ref, range(copies_ref.shape[0]), hidden)


def project(order, rows, w_out, residual):
    devices, heads, width = rows.shape
    return pl.pallas_call(
        functools.partial(project_kernel, order),
        out_shape=(
            jax.ShapeDtypeStruct(residual.shape, jnp.bfloat16),
            jax.ShapeDtypeStruct((devices, *slot(*residual.shape)), jnp.bfloat16),
        ),
        scratch_shapes=[pltpu.VMEM((devices * heads, width), jnp.float32)],
        compiler_params=pltpu.CompilerParams(vmem_limit_bytes=12 * MIB),
        cost_estimate=COST,
    )(rows, w_out, residual)


def forward_kernel(
    order, pieces_ref, gain_ref, copies_ref, gate_ref, up_ref, down_ref, out_ref, attention_hbm, state_ref, sem
):
    keep = pltpu.make_async_copy(copies_ref.at[0], attention_hbm, sem)
    keep.start()
    devices = pieces_ref.shape[0]
    columns = gain_ref.shape[0] // devices
    if pieces_ref.ndim == 4:
        state = whole_state(pieces_ref, order, columns)
    else:
        for place, device in enumerate(order):
            columns_of = slice(device * columns, (device + 1) * columns)
            state_ref[:, columns_of] = pieces_ref[place].astype(jnp.float32)
        state = state_ref[...]
    mean_square = jnp.mean(state * state, axis=-1, keepdims=True)
    gain = gain_ref[...].reshape(1, devices * columns)
    normed = (state * lax.rsqrt(mean_square + NORM_EPSILON) * gain).astype(jnp.bfloat16)
    units = gate_ref.shape[0]
    count = CHUNKS if units % (16 * CHUNKS) == 0 else 1
    size = units // count
    features = down_ref.shape[1]
    parts = PARTS if features % (LANES * PARTS) == 0 else 1
    cuts = [slice(part * (features // parts), (part + 1) * (features // parts)) for part in range(parts)]
    shares = [0.0] * parts
    ready = None
    for chunk in range(count + 1):
        if chunk < count:
            rows = slice(chunk * size, (chunk + 1) * size)
            gate_values = dot_rows(gate_ref[rows], normed)
            up_values = dot_rows(normed, up_ref[rows])
        if ready is not None:
            activated, held = ready
            for part, cut in enumerate(cuts):
                shares[part] += jnp.dot(
                    activated, down_ref[held, cut], preferred_element_type=jnp.float32
                )
        if chunk < count:
            activated = jax.nn.gelu(gate_values.T, approximate=True) * up_values
            ready = activated.astype(jnp.bfloat16), rows
    share = jnp.concatenate(shares, axis=1)
    if pieces_ref.ndim == 4:
        put_columns(out_ref, order, share, columns)
    else:
        for place, device in enumerate(order):
            put(out_ref, (place,), share[:, device * columns : (device + 1) * columns])
    keep.wait()


def forward(order, pieces, completions, gain, copies, *weights):
    return pl.pallas_call(
        functools.partial(forward_kernel, order),
        out_shape=(
            jax.ShapeDtypeStruct(pieces.shape, jnp.bfloat16),
            jax.ShapeDtypeStruct(copies.shape[1:], jnp.bfloat16),
        ),
        out_specs=(pl.BlockSpec(memory_space=pltpu.VMEM), pl.BlockSpec(memory_space=pl.ANY)),
        scratch_shapes=[
            pltpu.VMEM((completions, gain.shape[0]), jnp.float32),
            pltpu.SemaphoreType.DMA,
        ],
        compiler_params=pltpu.CompilerParams(vmem_limit_bytes=8 * MIB),
        cost_estimate=COST,
    )(pieces, gain, copies, *weights)


def total_kernel(shares_ref, hidden_ref, out_ref):
    half = shares_ref.shape[0] // 2
    pairs = shares_ref[:half].astype(jnp.float32) + shares_ref[half:].astype(jnp.float32)
    summed = jnp.sum(pairs, axis=0)
    if shares_ref.ndim == 4:
        columns = hidden_ref.shape[1]
        low, rest = (turn(part, columns, back=True) for part in joined(*summed))
        summed = jnp.concatenate([low, rest[:, : columns - LANES]], axis=1)
    out_ref[...] = (hidden_ref[...].astype(jnp.float32) + summed).astype(jnp.bfloat16)


def total(shares, hidden):
    return pl.pallas_call(
        total_kernel,
        out_shape=jax.ShapeDtypeStruct(hidden.shape, jnp.bfloat16),
        compiler_params=pltpu.CompilerParams(vmem_limit_bytes=16 * MIB),
    )(shares, hidden)


def listed(ctx_count, groups):
    order = (0, 1, 4, 5, 6, 7, 2, 3) if ctx_count == 8 else range(ctx_count)
    return [ctx * groups + group for ctx in order for group in range(groups)]


def exchange(copies, axes=BOTH):
    groups = None
    if axes == BOTH:
        groups = [listed(lax.axis_size("ctx"), lax.axis_size("head"))]
    return lax.all_to_all(
        copies, axes, split_axis=0, concat_axis=0, tiled=True, axis_index_groups=groups
    )


def body(
    queries,
    k_new,
    v_new,
    k_suffix,
    v_suffix,
    lengths,
    k_prefix,
    v_prefix,
    w_out,
    residual,
    norm_gain,
    w_gate,
    w_up,
    w_down,
):
    ctx_count = lax.axis_size("ctx")
    devices = ctx_count * lax.axis_size("head")
    copies, own_length = spread(lengths, queries, ctx_count)
    arrived = exchange(copies, "ctx")
    rows_of = lambda values: values.reshape(-1, values.shape[-1])
    parts = attend(
        own_length, arrived, k_new, v_new, *map(rows_of, (k_suffix, v_suffix, k_prefix, v_prefix))
    )
    copies = join_partials(exchange(parts, "ctx"), (devices, *queries.shape[1:]))
    order = listed(ctx_count, devices // ctx_count)
    hidden_part, hidden_copies = project(order, exchange(copies), w_out.T, residual)
    shares, attention = forward(
        order, exchange(hidden_copies), residual.shape[0], norm_gain, copies, w_gate.T, w_up.T, w_down
    )
    return (attention[None], total(exchange(shares), hidden_part))


def solution(mesh):
    placed = (
        P("ctx", "head", None),
        P("ctx", "head", None),
        P("ctx", "head", None),
        P("ctx", None, "head", None),
        P("ctx", None, "head", None),
        P("ctx"),
        P("ctx", "head", None),
        P("ctx", "head", None),
        P(None, BOTH),
        P(None, BOTH),
        P(),
        P(None, BOTH),
        P(None, BOTH),
        P(BOTH, None),
    )
    return jax.shard_map(
        body,
        mesh=mesh,
        in_specs=placed,
        out_specs=(P("ctx", "head", None), P(None, BOTH)),
        check_vma=False,
    )
```

```python
import functools

import jax
import jax.numpy as jnp
from jax import lax
from jax.experimental import pallas as pl
from jax.experimental.pallas import tpu as pltpu
from jax.sharding import PartitionSpec as P

SCORE_SCALE = 168.0 ** (-0.5)
NORM_EPSILON = 1e-06
MASKED = -1e30
MIB = 1024 * 1024
COST = pl.CostEstimate(flops=10**10, bytes_accessed=MIB, transcendentals=10**6)
TERMS = 3
CHUNKS = 3
QUARTERS = 4
BLOCK_ROWS = 1024
LANES = 128
HALF = LANES // 2
BOTH = ("ctx", "head")


def head_bias(rows, columns, heads, kv_heads):
    group = heads // kv_heads
    tile = (heads, 128)
    row = lax.broadcasted_iota(jnp.int32, tile, 0)
    column = lax.broadcasted_iota(jnp.int32, tile, 1)
    bias = jnp.where(row // group == lax.rem(column, kv_heads), 0.0, MASKED)
    return jnp.tile(bias, (rows // heads, columns // 128))


def in_hbm(operand):
    return pltpu.with_memory_space_constraint(operand, pltpu.HBM)


def dot_rows(left, right):
    return lax.dot_general(left, right, (((1,), (1,)), ((), ())), preferred_element_type=jnp.float32)


def stat_rows(row_max, row_total, shape):
    lane = lax.broadcasted_iota(jnp.int32, shape, 1)
    return jnp.where(lane == 0, row_max, row_total)


def slot(rows, columns):
    if rows == 8 and LANES < columns <= LANES + HALF:
        return 3, 4, LANES
    return rows, columns


def put(ref, places, value):
    if ref.ndim == 3:
        for place in places:
            ref[place] = value.astype(ref.dtype)
        return
    rows, columns = value.shape
    rest = value[:, LANES:]
    if columns < LANES + HALF:
        rest = jnp.concatenate([rest, jnp.zeros((rows, LANES + HALF - columns), value.dtype)], axis=1)
    rest = jnp.concatenate([rest[:4], rest[4:]], axis=1)
    pieces = [piece.astype(ref.dtype) for piece in (value[:4, :LANES], value[4:, :LANES], rest)]
    for place in places:
        for part, piece in enumerate(pieces):
            ref[place, part] = piece


def joined(first, second, rest):
    low = jnp.concatenate([first.astype(jnp.float32), second.astype(jnp.float32)], axis=0)
    rest = rest.astype(jnp.float32)
    return low, jnp.concatenate([rest, pltpu.roll(rest, HALF, 1)], axis=0)


def turn(value, columns, back=False):
    device = lax.axis_index("ctx") * lax.axis_size("head") + lax.axis_index("head")
    offset = lax.rem(device * columns, LANES)
    return pltpu.roll(value, lax.rem(LANES - offset, LANES) if back else offset, 1)


def put_turned(ref, value):
    rows, columns = value.shape
    rest = jnp.concatenate(
        [value[:, LANES:], jnp.zeros((rows, 2 * LANES - columns), value.dtype)], axis=1
    )
    low, rest = turn(value[:, :LANES], columns), turn(rest, columns)
    rest = rest[:4] + pltpu.roll(rest, HALF, 1)[4:]
    pieces = [piece.astype(ref.dtype) for piece in (low[:4], low[4:], rest)]
    for place in range(ref.shape[0]):
        for part, piece in enumerate(pieces):
            ref[place, part] = piece


def whole_state(pieces_ref, order, columns):
    lane = lax.broadcasted_iota(jnp.int32, (8, LANES), 1)
    tiles = {}
    for device in range(len(order)):
        place = order.index(device)
        low, rest = joined(*(pieces_ref[place, part] for part in range(3)))
        first, offset = divmod(device * columns, LANES)
        tiles[first] = jnp.where(lane >= offset, low, tiles[first]) if offset else low
        tiles[first + 1] = jnp.where(lane < offset, low, rest)
        if offset + columns - LANES > LANES:
            tiles[first + 2] = rest
    return jnp.concatenate([tiles[place] for place in range(len(order) * columns // LANES)], axis=1)


def put_columns(ref, order, share, columns):
    lane = lax.broadcasted_iota(jnp.int32, (8, LANES), 1)
    tile = lambda place: share[:, place * LANES : (place + 1) * LANES]
    for device in range(len(order)):
        first, offset = divmod(device * columns, LANES)
        end = offset + columns - LANES
        low = jnp.where(lane >= offset, tile(first), tile(first + 1)) if offset else tile(first)
        rest = tile(first + 1)
        own = (lane >= offset) & (lane < end)
        if end > LANES:
            rest = jnp.where(lane >= offset, rest, tile(first + 2))
            own = (lane >= offset) | (lane < end - LANES)
        rest = jnp.where(own[:4], rest[:4], pltpu.roll(rest, HALF, 1)[4:])
        place = order.index(device)
        for part, piece in enumerate((low[:4], low[4:], rest)):
            ref[place, part] = piece.astype(ref.dtype)


def spread_kernel(length_ref, source_hbm, copies_ref, lengths_ref, source_ref, sem):
    load = pltpu.make_async_copy(source_hbm, source_ref, sem)
    load.start()
    lengths_ref[...] = jnp.full(lengths_ref.shape, length_ref[0], jnp.int32)
    load.wait()
    for place in range(copies_ref.shape[0]):
        copies_ref[place] = source_ref[0]


def spread(lengths, value, count):
    return pl.pallas_call(
        spread_kernel,
        out_shape=(
            jax.ShapeDtypeStruct((count, *value.shape[1:]), value.dtype),
            jax.ShapeDtypeStruct(value.shape[1:], jnp.int32),
        ),
        in_specs=[pl.BlockSpec(memory_space=pltpu.SMEM), pl.BlockSpec(memory_space=pl.ANY)],
        scratch_shapes=[pltpu.VMEM(value.shape, value.dtype), pltpu.SemaphoreType.DMA],
        compiler_params=pltpu.CompilerParams(vmem_limit_bytes=4 * MIB),
        cost_estimate=COST,
    )(lengths, in_hbm(value))


def attention_kernel(
    length_ref, arrived_ref, kn_ref, vn_ref, ks_ref, vs_ref, kp_ref, vp_ref, part_ref, sum_ref, stat_ref
):
    count, heads, width = arrived_ref.shape
    kv_heads = kn_ref.shape[1]
    rows = count * heads
    queries = arrived_ref[...].reshape(rows, width)
    row = lax.broadcasted_iota(jnp.int32, (rows, LANES), 0)
    own = jnp.where(row // heads == lax.axis_index("ctx"), 0.0, MASKED)
    prompt_rows = kp_ref.shape[0]
    size = BLOCK_ROWS if prompt_rows % BLOCK_ROWS == 0 else prompt_rows
    prompt_bias = head_bias(rows, size, heads, kv_heads)
    blocks = []
    for start in range(0, prompt_rows, size):
        block = slice(start, start + size)
        scores = SCORE_SCALE * dot_rows(queries, kp_ref[block]) + prompt_bias
        blocks.append((scores, vp_ref[block], None, None))
    cached_scores = SCORE_SCALE * dot_rows(queries, ks_ref[...])
    column = lax.broadcasted_iota(jnp.int32, (heads, cached_scores.shape[1]), 1)
    unused = jnp.where(column // kv_heads < length_ref[:, 0:1], 0.0, MASKED)
    bias = head_bias(heads, cached_scores.shape[1], heads, kv_heads) + unused
    bias = jnp.tile(bias, (count, 1)) + own[:, 0:1]
    cached_scores = cached_scores + bias
    new_scores = SCORE_SCALE * dot_rows(queries, kn_ref[0])
    new_scores = new_scores + head_bias(rows, LANES, heads, kv_heads)[:, :kv_heads] + own[:, :kv_heads]
    blocks.insert(0, (cached_scores, vs_ref[...], new_scores, vn_ref[0]))
    parts = []
    for block_scores, values, more_scores, more_values in blocks:
        block_max = jnp.max(block_scores, axis=1, keepdims=True)
        if more_scores is not None:
            block_max = jnp.maximum(block_max, jnp.max(more_scores, axis=1, keepdims=True))
        weights = jnp.exp(block_scores - block_max).astype(jnp.bfloat16)
        block_total = jnp.sum(weights.astype(jnp.float32), axis=1, keepdims=True)
        block_sum = jnp.dot(weights, values, preferred_element_type=jnp.float32)
        if more_scores is not None:
            weights = jnp.exp(more_scores - block_max).astype(jnp.bfloat16)
            block_total += jnp.sum(weights.astype(jnp.float32), axis=1, keepdims=True)
            block_sum += jnp.dot(weights, more_values, preferred_element_type=jnp.float32)
        parts.append((block_max, block_total, block_sum))
    row_max = functools.reduce(jnp.maximum, [part[0] for part in parts])
    factors = [jnp.exp(part[0] - row_max) for part in parts]
    row_total = sum(part[1] * factor for part, factor in zip(parts, factors))
    row_sum = sum(part[2] * factor for part, factor in zip(parts, factors))
    sum_ref[...] = row_sum.reshape(count, heads, width)
    stat_ref[...] = stat_rows(row_max, row_total, row_sum.shape).reshape(count, heads, width)
    lane = lax.broadcasted_iota(jnp.int32, (heads, HALF), 1)
    for place in range(count):
        total = stat_ref[place, :, 1:2]
        rest = jnp.broadcast_to(stat_ref[place, :, 0:1] + jnp.log(total), (heads, HALF))
        terms = jnp.zeros((heads, HALF), jnp.float32)
        for term in range(TERMS):
            rounded = rest.astype(jnp.bfloat16).astype(jnp.float32)
            terms = jnp.where(lane == term, rounded, terms)
            rest = rest - rounded
        put(part_ref, (place,), jnp.concatenate([sum_ref[place] / total, terms], axis=1))


def attend(lengths, arrived, *operands):
    count, heads, width = arrived.shape
    return pl.pallas_call(
        attention_kernel,
        out_shape=jax.ShapeDtypeStruct((count, *slot(heads, width + HALF)), jnp.bfloat16),
        scratch_shapes=[pltpu.VMEM(arrived.shape, jnp.float32)] * 2,
        compiler_params=pltpu.CompilerParams(vmem_limit_bytes=24 * MIB),
        cost_estimate=COST,
    )(lengths, arrived, *operands)


def join_kernel(part_ref, copies_ref):
    logs, shares = [], []
    for source in range(part_ref.shape[0]):
        share, terms = joined(*(part_ref[source, part] for part in range(3)))
        shares.append(share)
        logs.append(jnp.sum(terms[:, :TERMS], axis=1, keepdims=True))
    largest = functools.reduce(jnp.maximum, logs)
    factors = [jnp.exp(log - largest) for log in logs]
    summed = sum(share * factor for share, factor in zip(shares, factors))
    attention = (summed / sum(factors)).astype(jnp.bfloat16)
    for place in range(copies_ref.shape[0]):
        copies_ref[place] = attention


def join_partials(parts, shape):
    return pl.pallas_call(
        join_kernel,
        out_shape=jax.ShapeDtypeStruct(shape, jnp.bfloat16),
        compiler_params=pltpu.CompilerParams(vmem_limit_bytes=8 * MIB),
        cost_estimate=COST,
    )(parts)


def project_kernel(order, rows_ref, w_ref, residual_ref, out_ref, copies_ref, wide_ref):
    devices, heads, width = rows_ref.shape
    completions = residual_ref.shape[0]
    all_heads = devices * heads // completions
    for place, device in enumerate(order):
        wide_ref[device * heads : (device + 1) * heads] = rows_ref[place].astype(jnp.float32)
    quarter = all_heads // QUARTERS
    projected = 0.0
    for first in range(0, all_heads, quarter):
        rows = [
            wide_ref[pl.ds(head, completions, stride=all_heads), :].astype(jnp.bfloat16)
            for head in range(first, first + quarter)
        ]
        cut = slice(first * width, (first + quarter) * width)
        projected += dot_rows(jnp.concatenate(rows, axis=1), w_ref[:, cut])
    hidden = (residual_ref[...].astype(jnp.float32) + projected).astype(jnp.bfloat16)
    out_ref[...] = hidden
    if copies_ref.ndim == 4:
        put_turned(copies_ref, hidden.astype(jnp.float32))
    else:
        put(copies_ref, range(copies_ref.shape[0]), hidden)


def project(order, rows, w_out, residual):
    devices, heads, width = rows.shape
    return pl.pallas_call(
        functools.partial(project_kernel, order),
        out_shape=(
            jax.ShapeDtypeStruct(residual.shape, jnp.bfloat16),
            jax.ShapeDtypeStruct((devices, *slot(*residual.shape)), jnp.bfloat16),
        ),
        scratch_shapes=[pltpu.VMEM((devices * heads, width), jnp.float32)],
        compiler_params=pltpu.CompilerParams(vmem_limit_bytes=12 * MIB),
        cost_estimate=COST,
    )(rows, w_out, residual)


def forward_kernel(
    order, pieces_ref, gain_ref, copies_ref, gate_ref, up_ref, down_ref, out_ref, attention_hbm, state_ref, sem
):
    keep = pltpu.make_async_copy(copies_ref.at[0], attention_hbm, sem)
    keep.start()
    devices = pieces_ref.shape[0]
    columns = gain_ref.shape[0] // devices
    if pieces_ref.ndim == 4:
        state = whole_state(pieces_ref, order, columns)
    else:
        for place, device in enumerate(order):
            columns_of = slice(device * columns, (device + 1) * columns)
            state_ref[:, columns_of] = pieces_ref[place].astype(jnp.float32)
        state = state_ref[...]
    mean_square = jnp.mean(state * state, axis=-1, keepdims=True)
    gain = gain_ref[...].reshape(1, devices * columns)
    normed = (state * lax.rsqrt(mean_square + NORM_EPSILON) * gain).astype(jnp.bfloat16)
    units = gate_ref.shape[0]
    count = CHUNKS if units % (16 * CHUNKS) == 0 else 1
    size = units // count
    share = jnp.zeros((normed.shape[0], down_ref.shape[1]), jnp.float32)
    ready = None
    for chunk in range(count + 1):
        if chunk < count:
            rows = slice(chunk * size, (chunk + 1) * size)
            up_values = dot_rows(normed, up_ref[rows])
            gate_values = dot_rows(gate_ref[rows], normed)
        if ready is not None:
            activated, held = ready
            share += jnp.dot(activated, down_ref[held], preferred_element_type=jnp.float32)
        if chunk < count:
            activated = jax.nn.gelu(gate_values.T, approximate=True) * up_values
            ready = activated.astype(jnp.bfloat16), rows
    if pieces_ref.ndim == 4:
        put_columns(out_ref, order, share, columns)
    else:
        for place, device in enumerate(order):
            put(out_ref, (place,), share[:, device * columns : (device + 1) * columns])
    keep.wait()


def forward(order, pieces, completions, gain, copies, *weights):
    return pl.pallas_call(
        functools.partial(forward_kernel, order),
        out_shape=(
            jax.ShapeDtypeStruct(pieces.shape, jnp.bfloat16),
            jax.ShapeDtypeStruct(copies.shape[1:], jnp.bfloat16),
        ),
        out_specs=(pl.BlockSpec(memory_space=pltpu.VMEM), pl.BlockSpec(memory_space=pl.ANY)),
        scratch_shapes=[
            pltpu.VMEM((completions, gain.shape[0]), jnp.float32),
            pltpu.SemaphoreType.DMA,
        ],
        compiler_params=pltpu.CompilerParams(vmem_limit_bytes=8 * MIB),
        cost_estimate=COST,
    )(pieces, gain, copies, *weights)


def total_kernel(shares_ref, hidden_ref, out_ref):
    half = shares_ref.shape[0] // 2
    pairs = shares_ref[:half].astype(jnp.float32) + shares_ref[half:].astype(jnp.float32)
    summed = jnp.sum(pairs, axis=0)
    if shares_ref.ndim == 4:
        columns = hidden_ref.shape[1]
        low, rest = (turn(part, columns, back=True) for part in joined(*summed))
        summed = jnp.concatenate([low, rest[:, : columns - LANES]], axis=1)
    out_ref[...] = (hidden_ref[...].astype(jnp.float32) + summed).astype(jnp.bfloat16)


def total(shares, hidden):
    return pl.pallas_call(
        total_kernel,
        out_shape=jax.ShapeDtypeStruct(hidden.shape, jnp.bfloat16),
        compiler_params=pltpu.CompilerParams(vmem_limit_bytes=16 * MIB),
    )(shares, hidden)


def listed(ctx_count, groups):
    order = (0, 1, 4, 5, 6, 7, 2, 3) if ctx_count == 8 else range(ctx_count)
    return [ctx * groups + group for ctx in order for group in range(groups)]


def exchange(copies, axes=BOTH):
    groups = None
    if axes == BOTH:
        groups = [listed(lax.axis_size("ctx"), lax.axis_size("head"))]
    return lax.all_to_all(
        copies, axes, split_axis=0, concat_axis=0, tiled=True, axis_index_groups=groups
    )


def body(
    queries,
    k_new,
    v_new,
    k_suffix,
    v_suffix,
    lengths,
    k_prefix,
    v_prefix,
    w_out,
    residual,
    norm_gain,
    w_gate,
    w_up,
    w_down,
):
    ctx_count = lax.axis_size("ctx")
    devices = ctx_count * lax.axis_size("head")
    copies, own_length = spread(lengths, queries, ctx_count)
    arrived = exchange(copies, "ctx")
    rows_of = lambda values: values.reshape(-1, values.shape[-1])
    parts = attend(
        own_length, arrived, k_new, v_new, *map(rows_of, (k_suffix, v_suffix, k_prefix, v_prefix))
    )
    copies = join_partials(exchange(parts, "ctx"), (devices, *queries.shape[1:]))
    order = listed(ctx_count, devices // ctx_count)
    hidden_part, hidden_copies = project(order, exchange(copies), w_out.T, residual)
    shares, attention = forward(
        order, exchange(hidden_copies), residual.shape[0], norm_gain, copies, w_gate.T, w_up.T, w_down
    )
    return (attention[None], total(exchange(shares), hidden_part))


def solution(mesh):
    placed = (
        P("ctx", "head", None),
        P("ctx", "head", None),
        P("ctx", "head", None),
        P("ctx", None, "head", None),
        P("ctx", None, "head", None),
        P("ctx"),
        P("ctx", "head", None),
        P("ctx", "head", None),
        P(None, BOTH),
        P(None, BOTH),
        P(),
        P(None, BOTH),
        P(None, BOTH),
        P(BOTH, None),
    )
    return jax.shard_map(
        body,
        mesh=mesh,
        in_specs=placed,
        out_specs=(P("ctx", "head", None), P(None, BOTH)),
        check_vma=False,
    )
```

```python
import functools

import jax
import jax.numpy as jnp
from jax import lax
from jax.experimental import pallas as pl
from jax.experimental.pallas import tpu as pltpu
from jax.sharding import PartitionSpec as P

SCORE_SCALE = 168.0 ** (-0.5)
NORM_EPSILON = 1e-06
MASKED = -1e30
MIB = 1024 * 1024
COST = pl.CostEstimate(flops=10**10, bytes_accessed=MIB, transcendentals=10**6)
TERMS = 3
CHUNKS = 3
BLOCK_ROWS = 1024
LANES = 128
HALF = LANES // 2
BOTH = ("ctx", "head")


def head_bias(rows, columns, heads, kv_heads):
    group = heads // kv_heads
    tile = (heads, 128)
    row = lax.broadcasted_iota(jnp.int32, tile, 0)
    column = lax.broadcasted_iota(jnp.int32, tile, 1)
    bias = jnp.where(row // group == lax.rem(column, kv_heads), 0.0, MASKED)
    return jnp.tile(bias, (rows // heads, columns // 128))


def in_hbm(operand):
    return pltpu.with_memory_space_constraint(operand, pltpu.HBM)


def dot_rows(left, right):
    return lax.dot_general(left, right, (((1,), (1,)), ((), ())), preferred_element_type=jnp.float32)


def stat_rows(row_max, row_total, shape):
    lane = lax.broadcasted_iota(jnp.int32, shape, 1)
    return jnp.where(lane == 0, row_max, row_total)


def slot(rows, columns):
    if rows == 8 and LANES < columns <= LANES + HALF:
        return 3, 4, LANES
    return rows, columns


def put(ref, places, value):
    if ref.ndim == 3:
        for place in places:
            ref[place] = value.astype(ref.dtype)
        return
    rows, columns = value.shape
    rest = value[:, LANES:]
    if columns < LANES + HALF:
        rest = jnp.concatenate([rest, jnp.zeros((rows, LANES + HALF - columns), value.dtype)], axis=1)
    rest = jnp.concatenate([rest[:4], rest[4:]], axis=1)
    pieces = [piece.astype(ref.dtype) for piece in (value[:4, :LANES], value[4:, :LANES], rest)]
    for place in places:
        for part, piece in enumerate(pieces):
            ref[place, part] = piece


def joined(first, second, rest):
    low = jnp.concatenate([first.astype(jnp.float32), second.astype(jnp.float32)], axis=0)
    rest = rest.astype(jnp.float32)
    return low, jnp.concatenate([rest, pltpu.roll(rest, HALF, 1)], axis=0)


def turn(value, columns, back=False):
    device = lax.axis_index("ctx") * lax.axis_size("head") + lax.axis_index("head")
    offset = lax.rem(device * columns, LANES)
    return pltpu.roll(value, lax.rem(LANES - offset, LANES) if back else offset, 1)


def put_turned(ref, value):
    rows, columns = value.shape
    rest = jnp.concatenate(
        [value[:, LANES:], jnp.zeros((rows, 2 * LANES - columns), value.dtype)], axis=1
    )
    low, rest = turn(value[:, :LANES], columns), turn(rest, columns)
    rest = rest[:4] + pltpu.roll(rest, HALF, 1)[4:]
    pieces = [piece.astype(ref.dtype) for piece in (low[:4], low[4:], rest)]
    for place in range(ref.shape[0]):
        for part, piece in enumerate(pieces):
            ref[place, part] = piece


def whole_state(pieces_ref, order, columns):
    lane = lax.broadcasted_iota(jnp.int32, (8, LANES), 1)
    tiles = {}
    for device in range(len(order)):
        place = order.index(device)
        low, rest = joined(*(pieces_ref[place, part] for part in range(3)))
        first, offset = divmod(device * columns, LANES)
        tiles[first] = jnp.where(lane >= offset, low, tiles[first]) if offset else low
        tiles[first + 1] = jnp.where(lane < offset, low, rest)
        if offset + columns - LANES > LANES:
            tiles[first + 2] = rest
    return jnp.concatenate([tiles[place] for place in range(len(order) * columns // LANES)], axis=1)


def put_columns(ref, order, share, columns):
    lane = lax.broadcasted_iota(jnp.int32, (8, LANES), 1)
    tile = lambda place: share[:, place * LANES : (place + 1) * LANES]
    for device in range(len(order)):
        first, offset = divmod(device * columns, LANES)
        end = offset + columns - LANES
        low = jnp.where(lane >= offset, tile(first), tile(first + 1)) if offset else tile(first)
        rest = tile(first + 1)
        own = (lane >= offset) & (lane < end)
        if end > LANES:
            rest = jnp.where(lane >= offset, rest, tile(first + 2))
            own = (lane >= offset) | (lane < end - LANES)
        rest = jnp.where(own[:4], rest[:4], pltpu.roll(rest, HALF, 1)[4:])
        place = order.index(device)
        for part, piece in enumerate((low[:4], low[4:], rest)):
            ref[place, part] = piece.astype(ref.dtype)


def spread_kernel(length_ref, source_hbm, copies_ref, lengths_ref, source_ref, sem):
    load = pltpu.make_async_copy(source_hbm, source_ref, sem)
    load.start()
    lengths_ref[...] = jnp.full(lengths_ref.shape, length_ref[0], jnp.int32)
    load.wait()
    for place in range(copies_ref.shape[0]):
        copies_ref[place] = source_ref[0]


def spread(lengths, value, count):
    return pl.pallas_call(
        spread_kernel,
        out_shape=(
            jax.ShapeDtypeStruct((count, *value.shape[1:]), value.dtype),
            jax.ShapeDtypeStruct(value.shape[1:], jnp.int32),
        ),
        in_specs=[pl.BlockSpec(memory_space=pltpu.SMEM), pl.BlockSpec(memory_space=pl.ANY)],
        scratch_shapes=[pltpu.VMEM(value.shape, value.dtype), pltpu.SemaphoreType.DMA],
        compiler_params=pltpu.CompilerParams(vmem_limit_bytes=4 * MIB),
        cost_estimate=COST,
    )(lengths, in_hbm(value))


def attention_kernel(
    length_ref, arrived_ref, kn_ref, vn_ref, ks_ref, vs_ref, kp_ref, vp_ref, part_ref, sum_ref, stat_ref
):
    count, heads, width = arrived_ref.shape
    kv_heads = kn_ref.shape[1]
    rows = count * heads
    queries = arrived_ref[...].reshape(rows, width)
    row = lax.broadcasted_iota(jnp.int32, (rows, LANES), 0)
    own = jnp.where(row // heads == lax.axis_index("ctx"), 0.0, MASKED)
    prompt_rows = kp_ref.shape[0]
    size = BLOCK_ROWS if prompt_rows % BLOCK_ROWS == 0 else prompt_rows
    prompt_bias = head_bias(rows, size, heads, kv_heads)
    blocks = []
    for start in range(0, prompt_rows, size):
        block = slice(start, start + size)
        scores = SCORE_SCALE * dot_rows(queries, kp_ref[block]) + prompt_bias
        blocks.append((scores, vp_ref[block], None, None))
    cached_scores = SCORE_SCALE * dot_rows(queries, ks_ref[...])
    column = lax.broadcasted_iota(jnp.int32, (heads, cached_scores.shape[1]), 1)
    unused = jnp.where(column // kv_heads < length_ref[:, 0:1], 0.0, MASKED)
    bias = head_bias(heads, cached_scores.shape[1], heads, kv_heads) + unused
    bias = jnp.tile(bias, (count, 1)) + own[:, 0:1]
    cached_scores = cached_scores + bias
    new_scores = SCORE_SCALE * dot_rows(queries, kn_ref[0])
    new_scores = new_scores + head_bias(rows, LANES, heads, kv_heads)[:, :kv_heads] + own[:, :kv_heads]
    blocks.append((cached_scores, vs_ref[...], new_scores, vn_ref[0]))
    parts = []
    for block_scores, values, more_scores, more_values in blocks:
        block_max = jnp.max(block_scores, axis=1, keepdims=True)
        if more_scores is not None:
            block_max = jnp.maximum(block_max, jnp.max(more_scores, axis=1, keepdims=True))
        weights = jnp.exp(block_scores - block_max).astype(jnp.bfloat16)
        block_total = jnp.sum(weights.astype(jnp.float32), axis=1, keepdims=True)
        block_sum = jnp.dot(weights, values, preferred_element_type=jnp.float32)
        if more_scores is not None:
            weights = jnp.exp(more_scores - block_max).astype(jnp.bfloat16)
            block_total += jnp.sum(weights.astype(jnp.float32), axis=1, keepdims=True)
            block_sum += jnp.dot(weights, more_values, preferred_element_type=jnp.float32)
        parts.append((block_max, block_total, block_sum))
    row_max = functools.reduce(jnp.maximum, [part[0] for part in parts])
    factors = [jnp.exp(part[0] - row_max) for part in parts]
    row_total = sum(part[1] * factor for part, factor in zip(parts, factors))
    row_sum = sum(part[2] * factor for part, factor in zip(parts, factors))
    sum_ref[...] = row_sum.reshape(count, heads, width)
    stat_ref[...] = stat_rows(row_max, row_total, row_sum.shape).reshape(count, heads, width)
    lane = lax.broadcasted_iota(jnp.int32, (heads, HALF), 1)
    for place in range(count):
        total = stat_ref[place, :, 1:2]
        rest = jnp.broadcast_to(stat_ref[place, :, 0:1] + jnp.log(total), (heads, HALF))
        terms = jnp.zeros((heads, HALF), jnp.float32)
        for term in range(TERMS):
            rounded = rest.astype(jnp.bfloat16).astype(jnp.float32)
            terms = jnp.where(lane == term, rounded, terms)
            rest = rest - rounded
        put(part_ref, (place,), jnp.concatenate([sum_ref[place] / total, terms], axis=1))


def attend(lengths, arrived, *operands):
    count, heads, width = arrived.shape
    return pl.pallas_call(
        attention_kernel,
        out_shape=jax.ShapeDtypeStruct((count, *slot(heads, width + HALF)), jnp.bfloat16),
        scratch_shapes=[pltpu.VMEM(arrived.shape, jnp.float32)] * 2,
        compiler_params=pltpu.CompilerParams(vmem_limit_bytes=24 * MIB),
        cost_estimate=COST,
    )(lengths, arrived, *operands)


def join_kernel(part_ref, copies_ref):
    logs, shares = [], []
    for source in range(part_ref.shape[0]):
        share, terms = joined(*(part_ref[source, part] for part in range(3)))
        shares.append(share)
        logs.append(jnp.sum(terms[:, :TERMS], axis=1, keepdims=True))
    largest = functools.reduce(jnp.maximum, logs)
    factors = [jnp.exp(log - largest) for log in logs]
    summed = sum(share * factor for share, factor in zip(shares, factors))
    attention = (summed / sum(factors)).astype(jnp.bfloat16)
    for place in range(copies_ref.shape[0]):
        copies_ref[place] = attention


def join_partials(parts, shape):
    return pl.pallas_call(
        join_kernel,
        out_shape=jax.ShapeDtypeStruct(shape, jnp.bfloat16),
        compiler_params=pltpu.CompilerParams(vmem_limit_bytes=8 * MIB),
        cost_estimate=COST,
    )(parts)


def project_kernel(order, rows_ref, w_ref, residual_ref, out_ref, copies_ref, wide_ref):
    devices, heads, width = rows_ref.shape
    completions = residual_ref.shape[0]
    all_heads = devices * heads // completions
    for place, device in enumerate(order):
        wide_ref[device * heads : (device + 1) * heads] = rows_ref[place].astype(jnp.float32)
    rows = [wide_ref[pl.ds(head, completions, stride=all_heads), :] for head in range(all_heads)]
    rows = jnp.concatenate([row.astype(jnp.bfloat16) for row in rows], axis=1)
    projected = dot_rows(rows, w_ref[...])
    hidden = (residual_ref[...].astype(jnp.float32) + projected).astype(jnp.bfloat16)
    out_ref[...] = hidden
    if copies_ref.ndim == 4:
        put_turned(copies_ref, hidden.astype(jnp.float32))
    else:
        put(copies_ref, range(copies_ref.shape[0]), hidden)


def project(order, rows, w_out, residual):
    devices, heads, width = rows.shape
    return pl.pallas_call(
        functools.partial(project_kernel, order),
        out_shape=(
            jax.ShapeDtypeStruct(residual.shape, jnp.bfloat16),
            jax.ShapeDtypeStruct((devices, *slot(*residual.shape)), jnp.bfloat16),
        ),
        scratch_shapes=[pltpu.VMEM((devices * heads, width), jnp.float32)],
        compiler_params=pltpu.CompilerParams(vmem_limit_bytes=12 * MIB),
        cost_estimate=COST,
    )(rows, w_out, residual)


def forward_kernel(
    order, pieces_ref, gain_ref, copies_ref, gate_ref, up_ref, down_ref, out_ref, attention_hbm, state_ref, sem
):
    keep = pltpu.make_async_copy(copies_ref.at[0], attention_hbm, sem)
    keep.start()
    devices = pieces_ref.shape[0]
    columns = gain_ref.shape[0] // devices
    if pieces_ref.ndim == 4:
        state = whole_state(pieces_ref, order, columns)
    else:
        for place, device in enumerate(order):
            columns_of = slice(device * columns, (device + 1) * columns)
            state_ref[:, columns_of] = pieces_ref[place].astype(jnp.float32)
        state = state_ref[...]
    mean_square = jnp.mean(state * state, axis=-1, keepdims=True)
    gain = gain_ref[...].reshape(1, devices * columns)
    normed = (state * lax.rsqrt(mean_square + NORM_EPSILON) * gain).astype(jnp.bfloat16)
    units = gate_ref.shape[0]
    count = CHUNKS if units % (16 * CHUNKS) == 0 else 1
    size = units // count
    share = jnp.zeros((normed.shape[0], down_ref.shape[1]), jnp.float32)
    ready = None
    for chunk in range(count + 1):
        if chunk < count:
            rows = slice(chunk * size, (chunk + 1) * size)
            gate_values = dot_rows(gate_ref[rows], normed)
        if ready is not None:
            activated, held = ready
            share += jnp.dot(activated, down_ref[held], preferred_element_type=jnp.float32)
        if chunk < count:
            up_values = dot_rows(normed, up_ref[rows])
            activated = jax.nn.gelu(gate_values.T, approximate=True) * up_values
            ready = activated.astype(jnp.bfloat16), rows
    if pieces_ref.ndim == 4:
        put_columns(out_ref, order, share, columns)
    else:
        for place, device in enumerate(order):
            put(out_ref, (place,), share[:, device * columns : (device + 1) * columns])
    keep.wait()


def forward(order, pieces, completions, gain, copies, *weights):
    return pl.pallas_call(
        functools.partial(forward_kernel, order),
        out_shape=(
            jax.ShapeDtypeStruct(pieces.shape, jnp.bfloat16),
            jax.ShapeDtypeStruct(copies.shape[1:], jnp.bfloat16),
        ),
        out_specs=(pl.BlockSpec(memory_space=pltpu.VMEM), pl.BlockSpec(memory_space=pl.ANY)),
        scratch_shapes=[
            pltpu.VMEM((completions, gain.shape[0]), jnp.float32),
            pltpu.SemaphoreType.DMA,
        ],
        compiler_params=pltpu.CompilerParams(vmem_limit_bytes=8 * MIB),
        cost_estimate=COST,
    )(pieces, gain, copies, *weights)


def total_kernel(shares_ref, hidden_ref, out_ref):
    half = shares_ref.shape[0] // 2
    pairs = shares_ref[:half].astype(jnp.float32) + shares_ref[half:].astype(jnp.float32)
    summed = jnp.sum(pairs, axis=0)
    if shares_ref.ndim == 4:
        columns = hidden_ref.shape[1]
        low, rest = (turn(part, columns, back=True) for part in joined(*summed))
        summed = jnp.concatenate([low, rest[:, : columns - LANES]], axis=1)
    out_ref[...] = (hidden_ref[...].astype(jnp.float32) + summed).astype(jnp.bfloat16)


def total(shares, hidden):
    return pl.pallas_call(
        total_kernel,
        out_shape=jax.ShapeDtypeStruct(hidden.shape, jnp.bfloat16),
        compiler_params=pltpu.CompilerParams(vmem_limit_bytes=16 * MIB),
    )(shares, hidden)


def listed(ctx_count, groups):
    order = (0, 1, 4, 5, 6, 7, 2, 3) if ctx_count == 8 else range(ctx_count)
    return [ctx * groups + group for ctx in order for group in range(groups)]


def exchange(copies, axes=BOTH):
    groups = None
    if axes == BOTH:
        groups = [listed(lax.axis_size("ctx"), lax.axis_size("head"))]
    return lax.all_to_all(
        copies, axes, split_axis=0, concat_axis=0, tiled=True, axis_index_groups=groups
    )


def body(
    queries,
    k_new,
    v_new,
    k_suffix,
    v_suffix,
    lengths,
    k_prefix,
    v_prefix,
    w_out,
    residual,
    norm_gain,
    w_gate,
    w_up,
    w_down,
):
    ctx_count = lax.axis_size("ctx")
    devices = ctx_count * lax.axis_size("head")
    copies, own_length = spread(lengths, queries, ctx_count)
    arrived = exchange(copies, "ctx")
    rows_of = lambda values: values.reshape(-1, values.shape[-1])
    parts = attend(
        own_length, arrived, k_new, v_new, *map(rows_of, (k_suffix, v_suffix, k_prefix, v_prefix))
    )
    copies = join_partials(exchange(parts, "ctx"), (devices, *queries.shape[1:]))
    order = listed(ctx_count, devices // ctx_count)
    hidden_part, hidden_copies = project(order, exchange(copies), w_out.T, residual)
    shares, attention = forward(
        order, exchange(hidden_copies), residual.shape[0], norm_gain, copies, w_gate.T, w_up.T, w_down
    )
    return (attention[None], total(exchange(shares), hidden_part))


def solution(mesh):
    placed = (
        P("ctx", "head", None),
        P("ctx", "head", None),
        P("ctx", "head", None),
        P("ctx", None, "head", None),
        P("ctx", None, "head", None),
        P("ctx"),
        P("ctx", "head", None),
        P("ctx", "head", None),
        P(None, BOTH),
        P(None, BOTH),
        P(),
        P(None, BOTH),
        P(None, BOTH),
        P(BOTH, None),
    )
    return jax.shard_map(
        body,
        mesh=mesh,
        in_specs=placed,
        out_specs=(P("ctx", "head", None), P(None, BOTH)),
        check_vma=False,
    )
```

```python
import functools

import jax
import jax.numpy as jnp
from jax import lax
from jax.experimental import pallas as pl
from jax.experimental.pallas import tpu as pltpu
from jax.sharding import PartitionSpec as P

SCORE_SCALE = 168.0 ** (-0.5)
NORM_EPSILON = 1e-06
MASKED = -1e30
MIB = 1024 * 1024
COST = pl.CostEstimate(flops=10**10, bytes_accessed=MIB, transcendentals=10**6)
TERMS = 3
CHUNKS = 3
BLOCK_ROWS = 512
LANES = 128
HALF = LANES // 2
BOTH = ("ctx", "head")


def head_bias(rows, columns, heads, kv_heads):
    group = heads // kv_heads
    tile = (heads, 128)
    row = lax.broadcasted_iota(jnp.int32, tile, 0)
    column = lax.broadcasted_iota(jnp.int32, tile, 1)
    bias = jnp.where(row // group == lax.rem(column, kv_heads), 0.0, MASKED)
    return jnp.tile(bias, (rows // heads, columns // 128))


def in_hbm(operand):
    return pltpu.with_memory_space_constraint(operand, pltpu.HBM)


def dot_rows(left, right):
    return lax.dot_general(left, right, (((1,), (1,)), ((), ())), preferred_element_type=jnp.float32)


def stat_rows(row_max, row_total, shape):
    lane = lax.broadcasted_iota(jnp.int32, shape, 1)
    return jnp.where(lane == 0, row_max, row_total)


def slot(rows, columns):
    if rows == 8 and LANES < columns <= LANES + HALF:
        return 3, 4, LANES
    return rows, columns


def put(ref, places, value):
    if ref.ndim == 3:
        for place in places:
            ref[place] = value.astype(ref.dtype)
        return
    rows, columns = value.shape
    rest = value[:, LANES:]
    if columns < LANES + HALF:
        rest = jnp.concatenate([rest, jnp.zeros((rows, LANES + HALF - columns), value.dtype)], axis=1)
    rest = jnp.concatenate([rest[:4], rest[4:]], axis=1)
    pieces = [piece.astype(ref.dtype) for piece in (value[:4, :LANES], value[4:, :LANES], rest)]
    for place in places:
        for part, piece in enumerate(pieces):
            ref[place, part] = piece


def joined(first, second, rest):
    low = jnp.concatenate([first.astype(jnp.float32), second.astype(jnp.float32)], axis=0)
    rest = rest.astype(jnp.float32)
    return low, jnp.concatenate([rest, pltpu.roll(rest, HALF, 1)], axis=0)


def turn(value, columns, back=False):
    device = lax.axis_index("ctx") * lax.axis_size("head") + lax.axis_index("head")
    offset = lax.rem(device * columns, LANES)
    return pltpu.roll(value, lax.rem(LANES - offset, LANES) if back else offset, 1)


def put_turned(ref, value):
    rows, columns = value.shape
    rest = jnp.concatenate(
        [value[:, LANES:], jnp.zeros((rows, 2 * LANES - columns), value.dtype)], axis=1
    )
    low, rest = turn(value[:, :LANES], columns), turn(rest, columns)
    rest = rest[:4] + pltpu.roll(rest, HALF, 1)[4:]
    pieces = [piece.astype(ref.dtype) for piece in (low[:4], low[4:], rest)]
    for place in range(ref.shape[0]):
        for part, piece in enumerate(pieces):
            ref[place, part] = piece


def whole_state(pieces_ref, order, columns):
    lane = lax.broadcasted_iota(jnp.int32, (8, LANES), 1)
    tiles = {}
    for device in range(len(order)):
        place = order.index(device)
        low, rest = joined(*(pieces_ref[place, part] for part in range(3)))
        first, offset = divmod(device * columns, LANES)
        tiles[first] = jnp.where(lane >= offset, low, tiles[first]) if offset else low
        tiles[first + 1] = jnp.where(lane < offset, low, rest)
        if offset + columns - LANES > LANES:
            tiles[first + 2] = rest
    return jnp.concatenate([tiles[place] for place in range(len(order) * columns // LANES)], axis=1)


def put_columns(ref, order, share, columns):
    lane = lax.broadcasted_iota(jnp.int32, (8, LANES), 1)
    tile = lambda place: share[:, place * LANES : (place + 1) * LANES]
    for device in range(len(order)):
        first, offset = divmod(device * columns, LANES)
        end = offset + columns - LANES
        low = jnp.where(lane >= offset, tile(first), tile(first + 1)) if offset else tile(first)
        rest = tile(first + 1)
        own = (lane >= offset) & (lane < end)
        if end > LANES:
            rest = jnp.where(lane >= offset, rest, tile(first + 2))
            own = (lane >= offset) | (lane < end - LANES)
        rest = jnp.where(own[:4], rest[:4], pltpu.roll(rest, HALF, 1)[4:])
        place = order.index(device)
        for part, piece in enumerate((low[:4], low[4:], rest)):
            ref[place, part] = piece.astype(ref.dtype)


def spread_kernel(length_ref, source_hbm, copies_ref, lengths_ref, source_ref, sem):
    load = pltpu.make_async_copy(source_hbm, source_ref, sem)
    load.start()
    lengths_ref[...] = jnp.full(lengths_ref.shape, length_ref[0], jnp.int32)
    load.wait()
    for place in range(copies_ref.shape[0]):
        copies_ref[place] = source_ref[0]


def spread(lengths, value, count):
    return pl.pallas_call(
        spread_kernel,
        out_shape=(
            jax.ShapeDtypeStruct((count, *value.shape[1:]), value.dtype),
            jax.ShapeDtypeStruct(value.shape[1:], jnp.int32),
        ),
        in_specs=[pl.BlockSpec(memory_space=pltpu.SMEM), pl.BlockSpec(memory_space=pl.ANY)],
        scratch_shapes=[pltpu.VMEM(value.shape, value.dtype), pltpu.SemaphoreType.DMA],
        compiler_params=pltpu.CompilerParams(vmem_limit_bytes=4 * MIB),
        cost_estimate=COST,
    )(lengths, in_hbm(value))


def attention_kernel(
    length_ref, arrived_ref, kn_ref, vn_ref, ks_ref, vs_ref, kp_ref, vp_ref, part_ref, sum_ref, stat_ref
):
    count, heads, width = arrived_ref.shape
    kv_heads = kn_ref.shape[1]
    rows = count * heads
    queries = arrived_ref[...].reshape(rows, width)
    row = lax.broadcasted_iota(jnp.int32, (rows, LANES), 0)
    own = jnp.where(row // heads == lax.axis_index("ctx"), 0.0, MASKED)
    prompt_rows = kp_ref.shape[0]
    size = BLOCK_ROWS if prompt_rows % BLOCK_ROWS == 0 else prompt_rows
    prompt_bias = head_bias(rows, size, heads, kv_heads)
    blocks = []
    for start in range(0, prompt_rows, size):
        block = slice(start, start + size)
        scores = SCORE_SCALE * dot_rows(queries, kp_ref[block]) + prompt_bias
        blocks.append((scores, vp_ref[block], None, None))
    cached_scores = SCORE_SCALE * dot_rows(queries, ks_ref[...])
    column = lax.broadcasted_iota(jnp.int32, (heads, cached_scores.shape[1]), 1)
    unused = jnp.where(column // kv_heads < length_ref[:, 0:1], 0.0, MASKED)
    bias = head_bias(heads, cached_scores.shape[1], heads, kv_heads) + unused
    bias = jnp.tile(bias, (count, 1)) + own[:, 0:1]
    cached_scores = cached_scores + bias
    new_scores = SCORE_SCALE * dot_rows(queries, kn_ref[0])
    new_scores = new_scores + head_bias(rows, LANES, heads, kv_heads)[:, :kv_heads] + own[:, :kv_heads]
    blocks.append((cached_scores, vs_ref[...], new_scores, vn_ref[0]))
    parts = []
    for block_scores, values, more_scores, more_values in blocks:
        block_max = jnp.max(block_scores, axis=1, keepdims=True)
        if more_scores is not None:
            block_max = jnp.maximum(block_max, jnp.max(more_scores, axis=1, keepdims=True))
        weights = jnp.exp(block_scores - block_max).astype(jnp.bfloat16)
        block_total = jnp.sum(weights.astype(jnp.float32), axis=1, keepdims=True)
        block_sum = jnp.dot(weights, values, preferred_element_type=jnp.float32)
        if more_scores is not None:
            weights = jnp.exp(more_scores - block_max).astype(jnp.bfloat16)
            block_total += jnp.sum(weights.astype(jnp.float32), axis=1, keepdims=True)
            block_sum += jnp.dot(weights, more_values, preferred_element_type=jnp.float32)
        parts.append((block_max, block_total, block_sum))
    row_max = functools.reduce(jnp.maximum, [part[0] for part in parts])
    factors = [jnp.exp(part[0] - row_max) for part in parts]
    row_total = sum(part[1] * factor for part, factor in zip(parts, factors))
    row_sum = sum(part[2] * factor for part, factor in zip(parts, factors))
    sum_ref[...] = row_sum.reshape(count, heads, width)
    stat_ref[...] = stat_rows(row_max, row_total, row_sum.shape).reshape(count, heads, width)
    lane = lax.broadcasted_iota(jnp.int32, (heads, HALF), 1)
    for place in range(count):
        total = stat_ref[place, :, 1:2]
        rest = jnp.broadcast_to(stat_ref[place, :, 0:1] + jnp.log(total), (heads, HALF))
        terms = jnp.zeros((heads, HALF), jnp.float32)
        for term in range(TERMS):
            rounded = rest.astype(jnp.bfloat16).astype(jnp.float32)
            terms = jnp.where(lane == term, rounded, terms)
            rest = rest - rounded
        put(part_ref, (place,), jnp.concatenate([sum_ref[place] / total, terms], axis=1))


def attend(lengths, arrived, *operands):
    count, heads, width = arrived.shape
    return pl.pallas_call(
        attention_kernel,
        out_shape=jax.ShapeDtypeStruct((count, *slot(heads, width + HALF)), jnp.bfloat16),
        scratch_shapes=[pltpu.VMEM(arrived.shape, jnp.float32)] * 2,
        compiler_params=pltpu.CompilerParams(vmem_limit_bytes=24 * MIB),
        cost_estimate=COST,
    )(lengths, arrived, *operands)


def join_kernel(part_ref, copies_ref):
    logs, shares = [], []
    for source in range(part_ref.shape[0]):
        share, terms = joined(*(part_ref[source, part] for part in range(3)))
        shares.append(share)
        logs.append(jnp.sum(terms[:, :TERMS], axis=1, keepdims=True))
    largest = functools.reduce(jnp.maximum, logs)
    factors = [jnp.exp(log - largest) for log in logs]
    summed = sum(share * factor for share, factor in zip(shares, factors))
    attention = (summed / sum(factors)).astype(jnp.bfloat16)
    for place in range(copies_ref.shape[0]):
        copies_ref[place] = attention


def join_partials(parts, shape):
    return pl.pallas_call(
        join_kernel,
        out_shape=jax.ShapeDtypeStruct(shape, jnp.bfloat16),
        compiler_params=pltpu.CompilerParams(vmem_limit_bytes=8 * MIB),
        cost_estimate=COST,
    )(parts)


def project_kernel(order, rows_ref, w_ref, residual_ref, out_ref, copies_ref, wide_ref):
    devices, heads, width = rows_ref.shape
    completions = residual_ref.shape[0]
    all_heads = devices * heads // completions
    for place, device in enumerate(order):
        wide_ref[device * heads : (device + 1) * heads] = rows_ref[place].astype(jnp.float32)
    rows = [wide_ref[pl.ds(head, completions, stride=all_heads), :] for head in range(all_heads)]
    rows = jnp.concatenate([row.astype(jnp.bfloat16) for row in rows], axis=1)
    projected = dot_rows(rows, w_ref[...])
    hidden = (residual_ref[...].astype(jnp.float32) + projected).astype(jnp.bfloat16)
    out_ref[...] = hidden
    if copies_ref.ndim == 4:
        put_turned(copies_ref, hidden.astype(jnp.float32))
    else:
        put(copies_ref, range(copies_ref.shape[0]), hidden)


def project(order, rows, w_out, residual):
    devices, heads, width = rows.shape
    return pl.pallas_call(
        functools.partial(project_kernel, order),
        out_shape=(
            jax.ShapeDtypeStruct(residual.shape, jnp.bfloat16),
            jax.ShapeDtypeStruct((devices, *slot(*residual.shape)), jnp.bfloat16),
        ),
        scratch_shapes=[pltpu.VMEM((devices * heads, width), jnp.float32)],
        compiler_params=pltpu.CompilerParams(vmem_limit_bytes=12 * MIB),
        cost_estimate=COST,
    )(rows, w_out, residual)


def forward_kernel(
    order, pieces_ref, gain_ref, copies_ref, gate_ref, up_ref, down_ref, out_ref, attention_hbm, state_ref, sem
):
    keep = pltpu.make_async_copy(copies_ref.at[0], attention_hbm, sem)
    keep.start()
    devices = pieces_ref.shape[0]
    columns = gain_ref.shape[0] // devices
    if pieces_ref.ndim == 4:
        state = whole_state(pieces_ref, order, columns)
    else:
        for place, device in enumerate(order):
            columns_of = slice(device * columns, (device + 1) * columns)
            state_ref[:, columns_of] = pieces_ref[place].astype(jnp.float32)
        state = state_ref[...]
    mean_square = jnp.mean(state * state, axis=-1, keepdims=True)
    gain = gain_ref[...].reshape(1, devices * columns)
    normed = (state * lax.rsqrt(mean_square + NORM_EPSILON) * gain).astype(jnp.bfloat16)
    units = gate_ref.shape[0]
    count = CHUNKS if units % (16 * CHUNKS) == 0 else 1
    size = units // count
    share = jnp.zeros((normed.shape[0], down_ref.shape[1]), jnp.float32)
    ready = None
    for chunk in range(count + 1):
        if chunk < count:
            rows = slice(chunk * size, (chunk + 1) * size)
            gate_values = dot_rows(gate_ref[rows], normed)
            up_values = dot_rows(normed, up_ref[rows])
        if ready is not None:
            activated, held = ready
            share += jnp.dot(activated, down_ref[held], preferred_element_type=jnp.float32)
        if chunk < count:
            activated = jax.nn.gelu(gate_values.T, approximate=True) * up_values
            ready = activated.astype(jnp.bfloat16), rows
    if pieces_ref.ndim == 4:
        put_columns(out_ref, order, share, columns)
    else:
        for place, device in enumerate(order):
            put(out_ref, (place,), share[:, device * columns : (device + 1) * columns])
    keep.wait()


def forward(order, pieces, completions, gain, copies, *weights):
    return pl.pallas_call(
        functools.partial(forward_kernel, order),
        out_shape=(
            jax.ShapeDtypeStruct(pieces.shape, jnp.bfloat16),
            jax.ShapeDtypeStruct(copies.shape[1:], jnp.bfloat16),
        ),
        out_specs=(pl.BlockSpec(memory_space=pltpu.VMEM), pl.BlockSpec(memory_space=pl.ANY)),
        scratch_shapes=[
            pltpu.VMEM((completions, gain.shape[0]), jnp.float32),
            pltpu.SemaphoreType.DMA,
        ],
        compiler_params=pltpu.CompilerParams(vmem_limit_bytes=8 * MIB),
        cost_estimate=COST,
    )(pieces, gain, copies, *weights)


def total_kernel(shares_ref, hidden_ref, out_ref):
    half = shares_ref.shape[0] // 2
    pairs = shares_ref[:half].astype(jnp.float32) + shares_ref[half:].astype(jnp.float32)
    summed = jnp.sum(pairs, axis=0)
    if shares_ref.ndim == 4:
        columns = hidden_ref.shape[1]
        low, rest = (turn(part, columns, back=True) for part in joined(*summed))
        summed = jnp.concatenate([low, rest[:, : columns - LANES]], axis=1)
    out_ref[...] = (hidden_ref[...].astype(jnp.float32) + summed).astype(jnp.bfloat16)


def total(shares, hidden):
    return pl.pallas_call(
        total_kernel,
        out_shape=jax.ShapeDtypeStruct(hidden.shape, jnp.bfloat16),
        compiler_params=pltpu.CompilerParams(vmem_limit_bytes=16 * MIB),
    )(shares, hidden)


def listed(ctx_count, groups):
    order = (0, 1, 4, 5, 6, 7, 2, 3) if ctx_count == 8 else range(ctx_count)
    return [ctx * groups + group for ctx in order for group in range(groups)]


def exchange(copies, axes=BOTH):
    groups = None
    if axes == BOTH:
        groups = [listed(lax.axis_size("ctx"), lax.axis_size("head"))]
    return lax.all_to_all(
        copies, axes, split_axis=0, concat_axis=0, tiled=True, axis_index_groups=groups
    )


def body(
    queries,
    k_new,
    v_new,
    k_suffix,
    v_suffix,
    lengths,
    k_prefix,
    v_prefix,
    w_out,
    residual,
    norm_gain,
    w_gate,
    w_up,
    w_down,
):
    ctx_count = lax.axis_size("ctx")
    devices = ctx_count * lax.axis_size("head")
    copies, own_length = spread(lengths, queries, ctx_count)
    arrived = exchange(copies, "ctx")
    rows_of = lambda values: values.reshape(-1, values.shape[-1])
    parts = attend(
        own_length, arrived, k_new, v_new, *map(rows_of, (k_suffix, v_suffix, k_prefix, v_prefix))
    )
    copies = join_partials(exchange(parts, "ctx"), (devices, *queries.shape[1:]))
    order = listed(ctx_count, devices // ctx_count)
    hidden_part, hidden_copies = project(order, exchange(copies), w_out.T, residual)
    shares, attention = forward(
        order, exchange(hidden_copies), residual.shape[0], norm_gain, copies, w_gate.T, w_up.T, w_down
    )
    return (attention[None], total(exchange(shares), hidden_part))


def solution(mesh):
    placed = (
        P("ctx", "head", None),
        P("ctx", "head", None),
        P("ctx", "head", None),
        P("ctx", None, "head", None),
        P("ctx", None, "head", None),
        P("ctx"),
        P("ctx", "head", None),
        P("ctx", "head", None),
        P(None, BOTH),
        P(None, BOTH),
        P(),
        P(None, BOTH),
        P(None, BOTH),
        P(BOTH, None),
    )
    return jax.shard_map(
        body,
        mesh=mesh,
        in_specs=placed,
        out_specs=(P("ctx", "head", None), P(None, BOTH)),
        check_vma=False,
    )
```
